32 devices in a mesh: table: 8 (over z, core), user: 4 (over y, x).
Axes of the slice: x: 2, y: 2, z: 4, core: 2. Of those that a mesh axis runs over, the one named last changes fastest.
Arguments:
- item_table: bfloat16 [32768, 512], P(None, 'table')
- event_ids: int32 [16384], P('user'), may hold values from 0 to 32767
- seq_lengths: int32 [4, 16], P('user'), may hold values from 128 to 640, as said below
- seq_owner: int32 [4, 16], P('user'), may hold values from 0 to 7, as said below
- negative_ids: int32 [1024], P('user'), may hold values from 0 to 32767
- w_in: bfloat16 [512, 2048], replicated, may hold values from -0.25 to 0.25
- w_mid: bfloat16 [2048, 512], replicated, may hold values from -0.125 to 0.125
- w_uvqk: bfloat16 [512, 2048], replicated, may hold values from -0.25 to 0.25
- w_proj: bfloat16 [512, 512], replicated, may hold values from -0.25 to 0.25
Outputs:
- state_grad: float32 [24576, 512], P(('table', 'user'))
The draws below stay inside these ranges and needn't reach their ends.
Inputs may be any that keep to these rules, and one draw needn't show every extreme that they name: `seq_lengths`: lengths are multiples of 128; each row sums to 4096; the sequences one owner receives from a batch row total at most 768 events, and in every row some owner receives exactly that many and some sequence has the largest length. `seq_owner`: in each row every owner index appears exactly twice.
All inputs are finite; a program needn't handle non-finite values.
Results may differ from the reference program's by a relative error of at most 0.004.
Values may be sent and summed in bfloat16 or wider, within the bound.
No kernel may reach another device: no remote copies, remote signals or barrier semaphores. Data moves between devices by JAX's collectives and lax.ppermute only.
A program may use at most 64 MiB of HBM per device.

```python
import math
import jax
import jax.numpy as jnp
import numpy as np
from jax import lax

D = 512
FF = 2048
HEADS = 4
VOCAB = 32768
NEG = 1024
PAGE = 128
PAGES_OWN = 4
CAP_PAGES = 6
EV_ROW = 4096
EVENTS = 16384
OUT_ROWS = 24576
N_TABLE = 8
N_USER = 4


def batch_plan(key):

    def one_batch_row(row_key):
        key_order, key_shift, key_part, key_shuffle = jax.random.split(row_key, 4)
        owner_order = jax.random.permutation(key_order, N_TABLE).astype(jnp.int32)
        most_shift = PAGES_OWN - 2
        load_shift = jax.random.randint(key_shift, (N_TABLE // 2,), 0, most_shift + 1).astype(jnp.int32)
        load_shift = load_shift.at[0].set(most_shift)
        owner_load = jnp.zeros((N_TABLE,), jnp.int32)
        owner_load = owner_load.at[owner_order[0::2]].set(PAGES_OWN + load_shift)
        owner_load = owner_load.at[owner_order[1::2]].set(PAGES_OWN - load_shift)
        least_first = jnp.maximum(1, owner_load - (CAP_PAGES - 1))
        most_first = owner_load - 1
        first_part = jax.random.randint(key_part, (N_TABLE,), least_first, most_first + 1).astype(jnp.int32)
        first_part = first_part.at[owner_order[0]].set(CAP_PAGES - 1)
        second_part = owner_load - first_part
        page_parts = jnp.stack([first_part, second_part], axis=1).reshape(-1)
        owners = jnp.repeat(jnp.arange(N_TABLE, dtype=jnp.int32), 2)
        shuffle = jax.random.permutation(key_shuffle, 2 * N_TABLE)
        return ((page_parts[shuffle] * PAGE).astype(jnp.int32), owners[shuffle])
    row_keys = jax.random.split(key, N_USER)
    return jax.vmap(one_batch_row)(row_keys)


def draw_seq_lengths(key, part):
    return batch_plan(key)[0]


def draw_seq_owner(key, part):
    return batch_plan(key)[1]


def draw_item_table(key, part):
    key = jax.random.fold_in(key, 7)
    key_base = jax.random.fold_in(key, 0)
    return jax.random.normal(key_base, (VOCAB, D), jnp.float32).astype(jnp.bfloat16)


def place_ends(array, key, smallest, high):
    place = [jax.random.randint(jax.random.fold_in(key, axis), (), 0, length) for axis, length in enumerate(array.shape)]
    main_axis = array.shape.index(max(array.shape))
    next_to = place[:main_axis] + [(place[main_axis] + 1) % array.shape[main_axis]] + place[main_axis + 1:]
    return array.at[tuple(place)].set(smallest).at[tuple(next_to)].set(high)


def cumulative_ranks(amount, skew):
    portions = [(1 << 20) // math.isqrt(grade ** skew) + 1 for grade in range(1, amount + 1)]
    scale = 1 + sum(portions) // (1 << 30)
    return np.cumsum(np.array([max(1, weight // scale) for weight in portions]))


def skewed_ids(key, extent, amount, slope):
    grid = cumulative_ranks(amount, slope)
    ticket = jax.random.randint(jax.random.fold_in(key, 1), extent, 0, int(grid[amount - 1]))
    grade = jnp.searchsorted(jnp.asarray(grid, jnp.int32), ticket, side="right")
    return jax.random.permutation(jax.random.fold_in(key, 2), amount)[grade].astype(jnp.int32)


def gaussian(rng, extent, scale, bound, kind=jnp.bfloat16):
    values = scale * jax.random.normal(rng, extent, jnp.float32)
    return jnp.clip(values, min=-bound, max=bound).astype(kind)


def setup_inputs(seed: int = 0) -> dict:
    keys = jax.random.split(jax.random.key(seed), 10)
    return {
        "item_table": draw_item_table(jax.random.fold_in(keys[9], 71), 0),
        "event_ids": place_ends(skewed_ids(keys[1], (EVENTS,), VOCAB, 2), jax.random.fold_in(keys[1], 3), 0, VOCAB - 1).astype(jnp.int32),
        "seq_lengths": draw_seq_lengths(jax.random.fold_in(keys[9], 71), 0),
        "seq_owner": draw_seq_owner(jax.random.fold_in(keys[9], 71), 0),
        "negative_ids": place_ends(jax.random.randint(keys[4], (NEG,), 0, VOCAB), jax.random.fold_in(keys[4], 1), 0, VOCAB - 1).astype(jnp.int32),
        "w_in": gaussian(keys[5], (D, FF), D ** -0.5, 0.25),
        "w_mid": gaussian(keys[6], (FF, D), FF ** -0.5, 0.125),
        "w_uvqk": gaussian(keys[7], (D, 4 * D), D ** -0.5, 0.25),
        "w_proj": gaussian(keys[8], (D, D), D ** -0.5, 0.25),
    }


SCORE_SHARPNESS = 0.02
NORM_EPSILON = 1e-06
LAYER_EPSILON = 1e-05

def page_plan(lengths, owners, cap_pages, page_size, tables):
    page_count = (lengths // page_size).astype(jnp.int32)
    seq_count = lengths.shape[0]
    src_start = (jnp.cumsum(page_count) - page_count).astype(jnp.int32)
    seq_order = jnp.arange(seq_count, dtype=jnp.int32)
    before = (owners[:, None] == owners[None, :]) & (seq_order[None, :] < seq_order[:, None])
    dst_start = lax.optimization_barrier(jnp.sum(jnp.where(before, page_count[None, :], 0), axis=1)).astype(jnp.int32)
    owner_grid = jnp.arange(tables, dtype=jnp.int32)[:, None, None]
    slot_grid = jnp.arange(cap_pages, dtype=jnp.int32)[None, :, None]
    matched = (owners[None, None, :] == owner_grid) & (dst_start <= slot_grid) & (slot_grid < dst_start + page_count)
    matched = matched.astype(jnp.int32)
    src_page = lax.optimization_barrier(jnp.sum(matched * (src_start + slot_grid - dst_start), axis=2)).astype(jnp.int32)
    filled = lax.optimization_barrier(jnp.sum(matched, axis=2)).astype(jnp.int32)
    segment = (lax.optimization_barrier(jnp.sum(matched * (seq_order + 1), axis=2)) - 1).astype(jnp.int32)
    seq_length = lax.optimization_barrier(jnp.sum(matched * lengths, axis=2)).astype(jnp.int32)
    within = jnp.arange(page_size, dtype=jnp.int32)
    slot_event = (src_page[:, :, None] * page_size + within).reshape(tables, cap_pages * page_size).astype(jnp.int32)

    def spread(per_page):
        return jnp.repeat(per_page, page_size, axis=1)
    return (slot_event, spread(filled), spread(segment), spread(seq_length))

def feed_forward(inputs, w_in, w_mid):
    hidden = jax.nn.silu(jnp.dot(inputs, w_in, preferred_element_type=jnp.float32)).astype(jnp.bfloat16)
    return jnp.dot(hidden, w_mid, preferred_element_type=jnp.float32).astype(jnp.bfloat16)

def layer_state(mixed_rows, segment, seq_length, w_uvqk, w_proj, head_count):
    row_count, model_width = mixed_rows.shape
    head_width = model_width // head_count
    projected = jax.nn.silu(jnp.dot(mixed_rows, w_uvqk, preferred_element_type=jnp.float32)).astype(jnp.bfloat16)
    position = jnp.arange(row_count, dtype=jnp.int32)
    allowed = (segment[:, None] == segment[None, :]) & (position[None, :] <= position[:, None]) & (segment[:, None] >= 0)
    divisor = jnp.maximum(seq_length, 1).astype(jnp.float32)[:, None]
    outputs = []
    for head_number in range(head_count):
        offset = head_number * head_width
        values = projected[:, model_width + offset:model_width + offset + head_width]
        queries = projected[:, 2 * model_width + offset:2 * model_width + offset + head_width]
        key_part = projected[:, 3 * model_width + offset:3 * model_width + offset + head_width]
        scores = lax.dot_general(queries, key_part, (((1,), (1,)), ((), ())), preferred_element_type=jnp.float32) / math.sqrt(head_width)
        weights = (jnp.where(allowed, jax.nn.silu(scores), 0.0) / divisor).astype(jnp.bfloat16)
        outputs.append(jnp.dot(weights, values, preferred_element_type=jnp.float32))
    attended = jnp.concatenate(outputs, axis=1)
    average = lax.optimization_barrier(jnp.mean(attended, axis=1, keepdims=True))
    centered = attended - average
    variance = lax.optimization_barrier(jnp.mean(centered * centered, axis=1, keepdims=True))
    gate_part = projected[:, :model_width].astype(jnp.float32)
    gated = (centered * lax.rsqrt(variance + LAYER_EPSILON) * gate_part).astype(jnp.bfloat16)
    return mixed_rows.astype(jnp.float32) + jnp.dot(gated, w_proj, preferred_element_type=jnp.float32)

def unit_rows(matrix):
    return matrix * lax.rsqrt(lax.optimization_barrier(jnp.sum(matrix * matrix, axis=1, keepdims=True)) + NORM_EPSILON)

def state_gradient(state_rows, inputs, segment, negatives):
    user_vector_rescaled = unit_rows(state_rows).astype(jnp.bfloat16)
    unit_items = unit_rows(inputs.astype(jnp.float32)).astype(jnp.bfloat16)
    correct_next_products = jnp.concatenate([unit_items[1:], jnp.zeros_like(unit_items[:1])], axis=0)
    next_segment = jnp.concatenate([segment[1:], jnp.full((1,), -1, jnp.int32)], axis=0)
    has_next = (segment >= 0) & (next_segment == segment)
    correct_next_products = jnp.where(has_next[:, None], correct_next_products, jnp.zeros_like(correct_next_products))
    distractor_vectors_rescaled = unit_rows(negatives.astype(jnp.float32)).astype(jnp.bfloat16)
    sampled_distractor_scores = lax.dot_general(user_vector_rescaled, distractor_vectors_rescaled, (((1,), (1,)), ((), ())), preferred_element_type=jnp.float32) / SCORE_SHARPNESS
    correct_pair_score = lax.optimization_barrier(jnp.sum(user_vector_rescaled.astype(jnp.float32) * correct_next_products.astype(jnp.float32), axis=1)) / SCORE_SHARPNESS
    neg_exp = jnp.exp(sampled_distractor_scores)
    correct_score_power = jnp.exp(correct_pair_score)
    partition_function_total = lax.optimization_barrier(jnp.sum(neg_exp, axis=1)) + correct_score_power
    probabilities = (neg_exp / partition_function_total[:, None]).astype(jnp.bfloat16)
    result_derivative = jnp.dot(probabilities, distractor_vectors_rescaled, preferred_element_type=jnp.float32)
    result_derivative = (result_derivative + (correct_score_power / partition_function_total - 1.0)[:, None] * correct_next_products.astype(jnp.float32)) / SCORE_SHARPNESS
    return jnp.where(has_next[:, None], result_derivative, 0.0)

def reference(item_table, event_ids, seq_lengths, seq_owner, negative_ids, w_in, w_mid, w_uvqk, w_proj):
    negatives = item_table[negative_ids]
    batch_ids = event_ids.reshape(N_USER, EV_ROW)

    def one_batch(operands):
        row_ids, lengths, owners = operands
        slot_event, filled, segment, seq_length = page_plan(lengths, owners, CAP_PAGES, PAGE, N_TABLE)

        def one_owner(owner_slot):
            inputs = item_table[row_ids[slot_event[owner_slot]]]
            inputs = jnp.where(filled[owner_slot][:, None] > 0, inputs, jnp.zeros_like(inputs))
            mixed_rows = feed_forward(inputs, w_in, w_mid)
            state_rows = layer_state(mixed_rows, segment[owner_slot], seq_length[owner_slot], w_uvqk, w_proj, HEADS)
            return state_gradient(state_rows, inputs, segment[owner_slot], negatives)
        return lax.map(one_owner, jnp.arange(N_TABLE, dtype=jnp.int32))
    result = lax.map(one_batch, (batch_ids, seq_lengths, seq_owner))
    return jnp.transpose(result, (1, 0, 2, 3)).reshape(OUT_ROWS, D)
```

```python
import functools
import math

import jax
import jax.numpy as jnp
from jax import lax
from jax.experimental import pallas as pl
from jax.experimental.pallas import tpu as pltpu
from jax.sharding import PartitionSpec as P

HEADS = 4
PAGE = 128
HALF = PAGE // 2
CAP_PAGES = 6
CHUNKS = (6,)
LANES = 128

SCORE_SHARPNESS = 0.02
NORM_EPSILON = 1e-06
LAYER_EPSILON = 1e-05

BF = jnp.bfloat16
F32 = jnp.float32
VMEM_BYTES = 60 * 1024 * 1024
COPY_PARTS = 8


def params():
    return pltpu.CompilerParams(vmem_limit_bytes=VMEM_BYTES)


def smem():
    return pl.BlockSpec(memory_space=pltpu.SMEM)


def vmem():
    return pl.BlockSpec(memory_space=pltpu.VMEM)


def hbm():
    return pl.BlockSpec(memory_space=pl.ANY)


def silu(v):
    return v * (0.5 + 0.5 * jnp.tanh(0.5 * v))


def swap_halves(v):
    width = v.shape[1] // 2
    if v.shape[1] == LANES:
        return pltpu.roll(v, width, 1)
    return jnp.concatenate([v[:, width:], v[:, :width]], axis=1)


def place_columns(ref, spare_ref, blocks, chips):
    width = blocks[0].shape[1]
    for s, block in enumerate(blocks):
        chip = source_chip(s, chips)
        if width == LANES:
            ref[:, pl.ds(pl.multiple_of(chip * width, width), width)] = block
        else:
            spare_ref[chip] = block
    if width != LANES:
        ref[...] = jnp.concatenate([spare_ref[chip] for chip in range(chips)], axis=1)


def spare_blocks(chips, rows, width):
    return pltpu.VMEM((chips, rows, width) if width != LANES else (1, 16, LANES), BF)


def lane_ids(shape):
    return lax.broadcasted_iota(jnp.int32, shape, len(shape) - 1)


def gather_kernel(tables, chunks, *refs):
    table_ref, ids_ref, neg_ref, len_ref, own_ref = refs[:5]
    count = len(chunks)
    keep_refs = refs[5 : 5 + count]
    give_refs = refs[5 + count : 5 + 2 * count]
    part_ref, rows_ref, stage_ref, next_ref, sem = refs[5 + 2 * count :]
    me = lax.axis_index("table")
    core = me % 2
    chip = me // 2
    chips = tables // 2
    width, vocab = table_ref.shape
    middle = vocab // 2
    piece = middle // COPY_PARTS

    def copy(side, i):
        at = pl.ds(side * middle + i * piece, piece)
        return pltpu.make_async_copy(table_ref.at[:, at], part_ref.at[:, at], sem.at[side, i])

    for i in range(COPY_PARTS):
        copy(0, i).start()
        copy(1, i).start()
    for i in range(COPY_PARTS):
        copy(0, i).wait()
        copy(1, i).wait()

        def turn(j, carry):
            at = pl.multiple_of(i * piece + j * LANES, LANES)
            low = part_ref[:, pl.ds(at, LANES)].astype(F32)
            high = part_ref[:, pl.ds(middle + at, LANES)].astype(F32)
            turned = jnp.concatenate([low, high], axis=0).T
            rows_ref[pl.ds(at, LANES), :] = turned
            rows_ref[pl.ds(middle + at, LANES), :] = swap_halves(turned)
            return carry

        lax.fori_loop(0, piece // LANES, turn, 0, unroll=4)

    first_xor = core * middle
    second_xor = middle - first_xor
    own_lanes = (lane_ids((1, 2 * width)) < width) == (core == 0)

    def fetch(source, base, half):
        def step(j, carry):
            at = pl.multiple_of(j * 8, 8)
            for k in range(8):
                first = source[base + at + k] ^ first_xor
                second = source[base + half + at + k] ^ second_xor
                picked = jnp.where(
                    own_lanes, rows_ref[pl.ds(first, 1), :], rows_ref[pl.ds(second, 1), :]
                )
                stage_ref[pl.ds(at + k, 1), :] = picked
            return carry

        lax.fori_loop(0, half // 8, step, 0)
        return stage_ref[0:half, :].astype(BF)

    neg_rows = neg_ref.shape[0] // 2
    neg_half = neg_rows // 2
    neg_at = chips * chunks[0] * HALF
    keep_refs[0][neg_at : neg_at + neg_half, :] = fetch(neg_ref, core * neg_rows, neg_half)
    give_refs[0][neg_at : neg_at + neg_half, :] = fetch(neg_ref, (1 - core) * neg_rows, neg_half)

    for t in range(tables):
        next_ref[t] = 0

    def sequence(i, page):
        owner = own_ref[0, i]
        pages = len_ref[0, i] // PAGE
        slot0 = next_ref[owner]
        next_ref[owner] = slot0 + pages
        shift = lax.rem(owner // 2 - chip + chips, chips)
        mine = owner % 2 == core

        def one_page(j, carry):
            block = fetch(ids_ref, (page + j) * PAGE, HALF)
            slot = slot0 + j
            start = 0
            for c, size in enumerate(chunks):
                inside = (slot >= start) & (slot < start + size)
                at = pl.multiple_of((shift * size + slot - start) * HALF, HALF)

                @pl.when(inside & mine)
                def _():
                    keep_refs[c][pl.ds(at, HALF), :] = block

                @pl.when(inside & jnp.logical_not(mine))
                def _():
                    give_refs[c][pl.ds(at, HALF), :] = block

                start += size
            return carry

        lax.fori_loop(0, pages, one_page, 0)
        return page + pages

    lax.fori_loop(0, len_ref.shape[1], sequence, 0)


def gather_rows(item_table, event_ids, negative_ids, seq_lengths, seq_owner, tables, chunks):
    vocab, width = item_table.shape
    chips = tables // 2
    neg_half = negative_ids.shape[0] // 4
    shapes = [
        jax.ShapeDtypeStruct((chips * size * HALF + (neg_half if c == 0 else 0), 2 * width), BF)
        for c, size in enumerate(chunks)
    ]
    outs = pl.pallas_call(
        functools.partial(gather_kernel, tables, chunks),
        out_shape=shapes + shapes,
        in_specs=[hbm(), smem(), smem(), smem(), smem()],
        out_specs=[vmem()] * (2 * len(chunks)),
        scratch_shapes=[
            pltpu.VMEM((width, vocab), BF),
            pltpu.VMEM((vocab, 2 * width), F32),
            pltpu.VMEM((max(HALF, neg_half), 2 * width), F32),
            pltpu.SMEM((tables,), jnp.int32),
            pltpu.SemaphoreType.DMA((2, COPY_PARTS)),
        ],
        compiler_params=params(),
        name="gather_rows",
    )(item_table.T, event_ids, negative_ids, seq_lengths, seq_owner)
    return outs[: len(chunks)], outs[len(chunks) :]


def merge_kernel(chips, pages, neg_half, keep_ref, got_ref, *out_refs):
    core = lax.axis_index("table") % 2
    width = keep_ref.shape[1] // 2
    own_lanes = (lane_ids((1, 2 * width)) < width) == (core == 0)

    def merged(at, half):
        own = keep_ref[at : at + half, :].astype(F32)
        other = got_ref[at : at + half, :].astype(F32)
        top = jnp.where(own_lanes, own, other)
        low = swap_halves(jnp.where(own_lanes, other, own))
        return top.astype(BF), low.astype(BF)

    if neg_half:
        top, low = merged(chips * pages * HALF, neg_half)
        at = pages * PAGE
        for s in range(chips):
            out_refs[s][at : at + neg_half, :] = top
            out_refs[s][at + neg_half : at + 2 * neg_half, :] = low
    for s in range(chips):
        for k in range(pages):
            top, low = merged((s * pages + k) * HALF, HALF)
            out_refs[s][k * PAGE : k * PAGE + HALF, :] = top
            out_refs[s][k * PAGE + HALF : (k + 1) * PAGE, :] = low


def merge_columns(keep, got, chips, pages, neg_half):
    shape = jax.ShapeDtypeStruct((pages * PAGE + 2 * neg_half, keep.shape[1]), BF)
    return pl.pallas_call(
        functools.partial(merge_kernel, chips, pages, neg_half),
        out_shape=[shape] * chips,
        in_specs=[vmem(), vmem()],
        out_specs=[vmem()] * chips,
        compiler_params=params(),
        name="merge_columns",
    )(keep, got)


def source_chip(s, chips):
    chip = lax.axis_index("table") // 2
    return lax.rem(chip - s + chips, chips)


def unit_negatives_kernel(chips, *refs):
    block_refs, out_ref, spare_ref = refs[:chips], refs[chips], refs[chips + 1]
    blocks = [ref[...].astype(F32) for ref in block_refs]
    squares = sum(jnp.sum(b * b, axis=1, keepdims=True) for b in blocks)
    scale = lax.rsqrt(squares + NORM_EPSILON)
    place_columns(out_ref, spare_ref, [(b * scale).astype(BF) for b in blocks], chips)


def unit_negatives(blocks, neg_rows):
    chips = len(blocks)
    tail = (blocks[0].shape[0] - neg_rows) // neg_rows
    lanes = blocks[0].shape[1]
    spec = pl.BlockSpec((neg_rows, lanes), lambda i: (tail, 0))
    return pl.pallas_call(
        functools.partial(unit_negatives_kernel, chips),
        grid=(1,),
        out_shape=jax.ShapeDtypeStruct((neg_rows, chips * lanes), BF),
        in_specs=[spec] * chips,
        out_specs=pl.BlockSpec((neg_rows, chips * lanes), lambda i: (0, 0)),
        scratch_shapes=[spare_blocks(chips, neg_rows, lanes)],
        compiler_params=params(),
        name="unit_negatives",
    )(*blocks)


def own_plan(len_ref, own_ref):
    me = lax.axis_index("table")
    segment = [jnp.int32(-1)] * CAP_PAGES
    length = [jnp.int32(1)] * CAP_PAGES
    start = jnp.int32(0)
    for i in range(len_ref.shape[1]):
        size = len_ref[0, i]
        mine = own_ref[0, i] == me
        end = jnp.where(mine, start + size // PAGE, start)
        for p in range(CAP_PAGES):
            inside = (start <= p) & (p < end)
            segment[p] = jnp.where(inside, i, segment[p])
            length[p] = jnp.where(inside, size, length[p])
        start = end
    return segment, length


def layer_kernel(chips, first, pages, last, *refs):
    len_ref, own_ref = refs[:2]
    block_refs = refs[2 : 2 + chips]
    refs = refs[2 + chips :]
    w_in, w_mid, w_uvqk, w_proj = refs[:4]
    refs = refs[4:]
    if first:
        prior_ref, refs = refs[0], refs[1:]
    unit_ref, item_ref = refs[:2]
    refs = refs[2:]
    if not last:
        kv_out, refs = refs[0], refs[1:]
    w_in_v, w_mid_v, w_uvqk_v, w_proj_v, x_ref, proj_ref, att_ref, spare_ref, sem = refs
    copies = [
        pltpu.make_async_copy(a, b, sem.at[i])
        for i, (a, b) in enumerate(
            ((w_in, w_in_v), (w_mid, w_mid_v), (w_uvqk, w_uvqk_v), (w_proj, w_proj_v))
        )
    ]
    for c in copies:
        c.start()
    width = w_in.shape[0]
    segment, length = own_plan(len_ref, own_ref)
    place_columns(x_ref, spare_ref, [ref[0 : pages * PAGE, :] for ref in block_refs], chips)
    for p in range(pages):
        part = slice(p * PAGE, (p + 1) * PAGE)
        page_x = x_ref[part, :]
        page_x = jnp.where(segment[first + p] >= 0, page_x, jnp.zeros_like(page_x))
        x_ref[part, :] = page_x
        x32 = page_x.astype(F32)
        item_ref[part, :] = (
            x32 * lax.rsqrt(jnp.sum(x32 * x32, axis=1, keepdims=True) + NORM_EPSILON)
        ).astype(BF)

    x = x_ref[...]
    hidden_width = w_in.shape[1]
    step = 512
    copies[0].wait()
    mixed = None
    for f in range(0, hidden_width, step):
        hidden = silu(
            jnp.dot(x, w_in_v[:, f : f + step], preferred_element_type=F32)
        ).astype(BF)
        if f == 0:
            copies[1].wait()
        part = jnp.dot(hidden, w_mid_v[f : f + step, :], preferred_element_type=F32)
        mixed = part if mixed is None else mixed + part
    mixed = mixed.astype(BF)
    copies[2].wait()
    for f in range(0, 4 * width, step):
        proj_ref[:, f : f + step] = silu(
            jnp.dot(mixed, w_uvqk_v[:, f : f + step], preferred_element_type=F32)
        ).astype(BF)
    if not last:
        kv_out[:, :width] = proj_ref[:, width : 2 * width]
        kv_out[:, width:] = proj_ref[:, 3 * width :]

    head_width = width // HEADS
    scale = 1.0 / math.sqrt(head_width)
    row_at = lax.broadcasted_iota(jnp.int32, (PAGE, PAGE), 0)
    causal = lane_ids((PAGE, PAGE)) <= row_at
    for p in range(pages):
        whole = first + p
        part = slice(p * PAGE, (p + 1) * PAGE)
        inverse = jnp.where(
            segment[whole] >= 0, 1.0 / jnp.full((1, PAGE), length[whole], jnp.int32).astype(F32), 0.0
        )
        factors = [
            jnp.where(segment[c] == segment[whole], inverse, 0.0) for c in range(whole)
        ]
        for h in range(HEADS):
            low = h * head_width
            query = proj_ref[part, 2 * width + low : 2 * width + low + head_width]
            keys = proj_ref[0 : (p + 1) * PAGE, 3 * width + low : 3 * width + low + head_width]
            values = proj_ref[0 : (p + 1) * PAGE, width + low : width + low + head_width]
            if first:
                keys = jnp.concatenate(
                    [prior_ref[:, width + low : width + low + head_width], keys], axis=0
                )
                values = jnp.concatenate([prior_ref[:, low : low + head_width], values], axis=0)
            scores = lax.dot_general(
                query, keys, (((1,), (1,)), ((), ())), preferred_element_type=F32
            )
            weights = []
            for c in range(whole + 1):
                score = silu(scores[:, c * PAGE : (c + 1) * PAGE] * scale)
                if c < whole:
                    weights.append((score * factors[c]).astype(BF))
                else:
                    weights.append(jnp.where(causal, score * inverse, 0.0).astype(BF))
            weights = weights[0] if whole == 0 else jnp.concatenate(weights, axis=1)
            att_ref[part, low : low + head_width] = jnp.dot(
                weights, values, preferred_element_type=F32
            )
    attended = att_ref[...]
    centered = attended - jnp.mean(attended, axis=1, keepdims=True)
    variance = jnp.mean(centered * centered, axis=1, keepdims=True)
    gated = (
        centered * lax.rsqrt(variance + LAYER_EPSILON) * proj_ref[:, :width].astype(F32)
    ).astype(BF)
    copies[3].wait()
    state = mixed.astype(F32) + jnp.dot(gated, w_proj_v[...], preferred_element_type=F32)
    unit_ref[...] = (
        state * lax.rsqrt(jnp.sum(state * state, axis=1, keepdims=True) + NORM_EPSILON)
    ).astype(BF)


def layer(seq_lengths, seq_owner, blocks, weights, prior, first, pages, last):
    chips = len(blocks)
    lanes = blocks[0].shape[1]
    width = chips * lanes
    rows = pages * PAGE
    wide = 4 * width
    operands = [seq_lengths, seq_owner, *blocks, *weights]
    in_specs = [smem(), smem()] + [vmem()] * chips + [hbm()] * 4
    if first:
        operands.append(prior)
        in_specs.append(vmem())
    out_shape = [jax.ShapeDtypeStruct((rows, width), BF)] * 2
    if not last:
        out_shape.append(jax.ShapeDtypeStruct((first * PAGE + rows, 2 * width), BF))
    return pl.pallas_call(
        functools.partial(layer_kernel, chips, first, pages, last),
        out_shape=out_shape,
        in_specs=in_specs,
        out_specs=[vmem()] * len(out_shape),
        scratch_shapes=[pltpu.VMEM(w.shape, BF) for w in weights]
        + [
            pltpu.VMEM((rows, width), BF),
            pltpu.VMEM((rows, wide), BF),
            pltpu.VMEM((rows, width), F32),
            spare_blocks(chips, rows, lanes),
            pltpu.SemaphoreType.DMA((4,)),
        ],
        compiler_params=params(),
        name="layer",
    )(*operands)


def gradient_kernel(count, *refs):
    len_ref, own_ref, near_ref, far_ref = refs[:4]
    unit_refs = refs[4 : 4 + count]
    item_refs = refs[4 + count : 4 + 2 * count]
    out_ref, neg_ref, next_ref = refs[4 + 2 * count :]
    half = near_ref.shape[0]
    neg_ref[:half, :] = near_ref[...]
    neg_ref[half:, :] = far_ref[...]
    rows = out_ref.shape[0]
    at = 0
    for ref in item_refs:
        next_ref[at : at + ref.shape[0], :] = ref[...].astype(F32)
        at += ref.shape[0]
    next_ref[rows:, :] = jnp.zeros_like(next_ref[rows:, :])
    segment, _ = own_plan(len_ref, own_ref)
    segment = segment + [jnp.int32(-1)]
    negatives = neg_ref[...]
    sharp = 1.0 / SCORE_SHARPNESS
    row_at = lax.broadcasted_iota(jnp.int32, (PAGE, 1), 0)
    at = 0
    for ref in unit_refs:
        for low in range(0, ref.shape[0], PAGE):
            page = at // PAGE
            unit = ref[low : low + PAGE, :]
            scores = lax.dot_general(
                unit, negatives, (((1,), (1,)), ((), ())), preferred_element_type=F32
            )
            targets = next_ref[at + 1 : at + 1 + PAGE, :]
            last_row = jnp.where(segment[page + 1] == segment[page], PAGE, PAGE - 1)
            limit = jnp.where(segment[page] >= 0, last_row, 0)
            has_next = row_at < limit
            targets = jnp.where(has_next, targets, 0.0)
            positive = jnp.exp(
                jnp.sum(unit.astype(F32) * targets, axis=1, keepdims=True) * sharp
            )
            powers = jnp.exp(scores * sharp)
            total = jnp.sum(powers, axis=1, keepdims=True) + positive
            inverse = 1.0 / total
            probs = (powers * inverse).astype(BF)
            grad = jnp.dot(probs, negatives, preferred_element_type=F32)
            grad = (grad + (positive * inverse - 1.0) * targets) * sharp
            out_ref[at : at + PAGE, :] = jnp.where(has_next, grad, 0.0)
            at += PAGE


def gradient(seq_lengths, seq_owner, near, far, units, items):
    rows = sum(u.shape[0] for u in units)
    half, width = near.shape
    return pl.pallas_call(
        functools.partial(gradient_kernel, len(units)),
        out_shape=jax.ShapeDtypeStruct((rows, width), F32),
        in_specs=[smem(), smem()] + [vmem()] * (2 + 2 * len(units)),
        out_specs=vmem(),
        scratch_shapes=[pltpu.VMEM((2 * half, width), BF), pltpu.VMEM((rows + 8, width), F32)],
        compiler_params=params(),
        name="gradient",
    )(seq_lengths, seq_owner, near, far, *units, *items)


def on_device(
    item_table, event_ids, seq_lengths, seq_owner, negative_ids, w_in, w_mid, w_uvqk, w_proj
):
    tables = lax.axis_size("table")
    users = lax.axis_size("user")
    chips = tables // 2
    neg_half = negative_ids.shape[0] // 4
    cores = [(t, t ^ 1) for t in range(tables)]
    keeps, gives = gather_rows(
        item_table, event_ids, negative_ids, seq_lengths, seq_owner, tables, CHUNKS
    )
    arrived = []
    for c, size in enumerate(CHUNKS):
        got = lax.ppermute(gives[c], "table", cores)
        blocks = list(merge_columns(keeps[c], got, chips, size, neg_half if c == 0 else 0))
        for s in range(1, chips):
            moves = [(t, (t // 2 + s) % chips * 2 + t % 2) for t in range(tables)]
            blocks[s] = lax.ppermute(blocks[s], "table", moves)
        arrived.append(blocks)

    own = unit_negatives(arrived[0], 2 * neg_half)
    parts = [own]
    for s in range(1, users):
        parts.append(lax.ppermute(own, "user", [(u, u ^ s) for u in range(users)]))
    near = jnp.concatenate(parts, axis=0)
    far = lax.ppermute(near, "table", cores)

    weights = (w_in, w_mid, w_uvqk, w_proj)
    units, items = [], []
    prior, first = None, 0
    for c, size in enumerate(CHUNKS):
        last = c == len(CHUNKS) - 1
        outs = layer(seq_lengths, seq_owner, arrived[c], weights, prior, first, size, last)
        units.append(outs[0])
        items.append(outs[1])
        if not last:
            prior = outs[2]
        first += size
    return gradient(seq_lengths, seq_owner, near, far, units, items)


def solution(mesh):
    return jax.shard_map(
        on_device,
        mesh=mesh,
        in_specs=(
            P(None, "table"),
            P("user"),
            P("user", None),
            P("user", None),
            P("user"),
            P(),
            P(),
            P(),
            P(),
        ),
        out_specs=P(("table", "user"), None),
        check_vma=False,
    )
```

```python
import functools
import math

import jax
import jax.numpy as jnp
from jax import lax
from jax.experimental import pallas as pl
from jax.experimental.pallas import tpu as pltpu
from jax.sharding import PartitionSpec as P

HEADS = 4
PAGE = 128
HALF = PAGE // 2
CAP_PAGES = 6
CHUNKS = (6,)
LANES = 128

SCORE_SHARPNESS = 0.02
NORM_EPSILON = 1e-06
LAYER_EPSILON = 1e-05

BF = jnp.bfloat16
F32 = jnp.float32
COPY_PARTS = 8
GRADIENT_PAGES = 3
QUERY_PAGES = 2


def params(mebibytes):
    return pltpu.CompilerParams(vmem_limit_bytes=mebibytes * 1024 * 1024)


def smem():
    return pl.BlockSpec(memory_space=pltpu.SMEM)


def vmem():
    return pl.BlockSpec(memory_space=pltpu.VMEM)


def hbm():
    return pl.BlockSpec(memory_space=pl.ANY)


def silu(v):
    return v * (0.5 + 0.5 * jnp.tanh(0.5 * v))


def swap_halves(v):
    width = v.shape[1] // 2
    if v.shape[1] == LANES:
        return pltpu.roll(v, width, 1)
    return jnp.concatenate([v[:, width:], v[:, :width]], axis=1)


def place_columns(ref, spare_ref, blocks, chips):
    width = blocks[0].shape[1]
    for s, block in enumerate(blocks):
        chip = source_chip(s, chips)
        if width == LANES:
            ref[:, pl.ds(pl.multiple_of(chip * width, width), width)] = block
        else:
            spare_ref[chip] = block
    if width != LANES:
        ref[...] = jnp.concatenate([spare_ref[chip] for chip in range(chips)], axis=1)


def spare_blocks(chips, rows, width):
    return pltpu.VMEM((chips, rows, width) if width != LANES else (1, 16, LANES), BF)


def lane_ids(shape):
    return lax.broadcasted_iota(jnp.int32, shape, len(shape) - 1)


def gather_kernel(tables, chunks, *refs):
    table_ref, ids_ref, neg_ref, len_ref, own_ref = refs[:5]
    count = len(chunks)
    keep_refs = refs[5 : 5 + count]
    give_refs = refs[5 + count : 5 + 2 * count]
    part_ref, rows_ref, stage_ref, next_ref, sem = refs[5 + 2 * count :]
    me = lax.axis_index("table")
    core = me % 2
    chip = me // 2
    chips = tables // 2
    width, vocab = table_ref.shape
    middle = vocab // 2
    piece = middle // COPY_PARTS

    def copy(side, i):
        at = pl.ds(side * middle + i * piece, piece)
        return pltpu.make_async_copy(table_ref.at[:, at], part_ref.at[:, at], sem.at[side, i])

    for i in range(COPY_PARTS):
        copy(0, i).start()
        copy(1, i).start()
    for i in range(COPY_PARTS):
        copy(0, i).wait()
        copy(1, i).wait()

        def turn(j, carry):
            at = pl.multiple_of(i * piece + j * LANES, LANES)
            low = part_ref[:, pl.ds(at, LANES)]
            high = part_ref[:, pl.ds(middle + at, LANES)]
            rows_ref[pl.ds(at, LANES), :] = jnp.concatenate([low, high], axis=0).T.astype(F32)
            rows_ref[pl.ds(middle + at, LANES), :] = jnp.concatenate([high, low], axis=0).T.astype(
                F32
            )
            return carry

        lax.fori_loop(0, piece // LANES, turn, 0, unroll=4)

    first_xor = core * middle
    second_xor = middle - first_xor
    own_lanes = (lane_ids((1, 2 * width)) < width) == (core == 0)

    def fetch(source, base, half):
        def step(j, carry):
            at = pl.multiple_of(j * 8, 8)
            for k in range(8):
                first = source[base + at + k] ^ first_xor
                second = source[base + half + at + k] ^ second_xor
                picked = jnp.where(
                    own_lanes, rows_ref[pl.ds(first, 1), :], rows_ref[pl.ds(second, 1), :]
                )
                stage_ref[pl.ds(at + k, 1), :] = picked
            return carry

        lax.fori_loop(0, half // 8, step, 0)
        return stage_ref[0:half, :].astype(BF)

    neg_rows = neg_ref.shape[0] // 2
    neg_half = neg_rows // 2
    neg_at = chips * chunks[0] * HALF
    keep_refs[0][neg_at : neg_at + neg_half, :] = fetch(neg_ref, core * neg_rows, neg_half)
    give_refs[0][neg_at : neg_at + neg_half, :] = fetch(neg_ref, (1 - core) * neg_rows, neg_half)

    for t in range(tables):
        next_ref[t] = 0

    def sequence(i, page):
        owner = own_ref[0, i]
        pages = len_ref[0, i] // PAGE
        slot0 = next_ref[owner]
        next_ref[owner] = slot0 + pages
        shift = lax.rem(owner // 2 - chip + chips, chips)
        mine = owner % 2 == core

        def one_page(j, carry):
            block = fetch(ids_ref, (page + j) * PAGE, HALF)
            slot = slot0 + j
            start = 0
            for c, size in enumerate(chunks):
                inside = (slot >= start) & (slot < start + size)
                at = pl.multiple_of((shift * size + slot - start) * HALF, HALF)

                @pl.when(inside & mine)
                def _():
                    keep_refs[c][pl.ds(at, HALF), :] = block

                @pl.when(inside & jnp.logical_not(mine))
                def _():
                    give_refs[c][pl.ds(at, HALF), :] = block

                start += size
            return carry

        lax.fori_loop(0, pages, one_page, 0)
        return page + pages

    lax.fori_loop(0, len_ref.shape[1], sequence, 0)


def gather_rows(item_table, event_ids, negative_ids, seq_lengths, seq_owner, tables, chunks):
    vocab, width = item_table.shape
    chips = tables // 2
    neg_half = negative_ids.shape[0] // 4
    shapes = [
        jax.ShapeDtypeStruct((chips * size * HALF + (neg_half if c == 0 else 0), 2 * width), BF)
        for c, size in enumerate(chunks)
    ]
    outs = pl.pallas_call(
        functools.partial(gather_kernel, tables, chunks),
        out_shape=shapes + shapes,
        in_specs=[hbm(), smem(), smem(), smem(), smem()],
        out_specs=[vmem()] * (2 * len(chunks)),
        scratch_shapes=[
            pltpu.VMEM((width, vocab), BF),
            pltpu.VMEM((vocab, 2 * width), F32),
            pltpu.VMEM((max(HALF, neg_half), 2 * width), F32),
            pltpu.SMEM((tables,), jnp.int32),
            pltpu.SemaphoreType.DMA((2, COPY_PARTS)),
        ],
        compiler_params=params(32),
        name="gather_rows",
    )(item_table.T, event_ids, negative_ids, seq_lengths, seq_owner)
    return outs[: len(chunks)], outs[len(chunks) :]


def merge_kernel(chips, pages, neg_half, keep_ref, got_ref, *out_refs):
    core = lax.axis_index("table") % 2
    width = keep_ref.shape[1] // 2
    own_lanes = (lane_ids((1, 2 * width)) < width) == (core == 0)

    def merged(at, half):
        own = keep_ref[at : at + half, :].astype(F32)
        other = got_ref[at : at + half, :].astype(F32)
        top = jnp.where(own_lanes, own, other)
        low = swap_halves(jnp.where(own_lanes, other, own))
        return top.astype(BF), low.astype(BF)

    if neg_half:
        top, low = merged(chips * pages * HALF, neg_half)
        at = pages * PAGE
        for s in range(chips):
            out_refs[s][at : at + neg_half, :] = top
            out_refs[s][at + neg_half : at + 2 * neg_half, :] = low
    for s in range(chips):
        for k in range(pages):
            top, low = merged((s * pages + k) * HALF, HALF)
            out_refs[s][k * PAGE : k * PAGE + HALF, :] = top
            out_refs[s][k * PAGE + HALF : (k + 1) * PAGE, :] = low


def merge_columns(keep, got, chips, pages, neg_half):
    shape = jax.ShapeDtypeStruct((pages * PAGE + 2 * neg_half, keep.shape[1]), BF)
    return pl.pallas_call(
        functools.partial(merge_kernel, chips, pages, neg_half),
        out_shape=[shape] * chips,
        in_specs=[vmem(), vmem()],
        out_specs=[vmem()] * chips,
        compiler_params=params(12),
        name="merge_columns",
    )(keep, got)


def source_chip(s, chips):
    chip = lax.axis_index("table") // 2
    return lax.rem(chip - s + chips, chips)


def unit_negatives_kernel(chips, *refs):
    block_refs, out_ref, spare_ref = refs[:chips], refs[chips], refs[chips + 1]
    blocks = [ref[...].astype(F32) for ref in block_refs]
    squares = sum(jnp.sum(b * b, axis=1, keepdims=True) for b in blocks)
    scale = lax.rsqrt(squares + NORM_EPSILON)
    place_columns(out_ref, spare_ref, [(b * scale).astype(BF) for b in blocks], chips)


def unit_negatives(blocks, neg_rows):
    chips = len(blocks)
    tail = (blocks[0].shape[0] - neg_rows) // neg_rows
    lanes = blocks[0].shape[1]
    spec = pl.BlockSpec((neg_rows, lanes), lambda i: (tail, 0))
    return pl.pallas_call(
        functools.partial(unit_negatives_kernel, chips),
        grid=(1,),
        out_shape=jax.ShapeDtypeStruct((neg_rows, chips * lanes), BF),
        in_specs=[spec] * chips,
        out_specs=pl.BlockSpec((neg_rows, chips * lanes), lambda i: (0, 0)),
        scratch_shapes=[spare_blocks(chips, neg_rows, lanes)],
        compiler_params=params(8),
        name="unit_negatives",
    )(*blocks)


def own_plan(len_ref, own_ref):
    me = lax.axis_index("table")
    segment = [jnp.int32(-1)] * CAP_PAGES
    length = [jnp.int32(1)] * CAP_PAGES
    start = jnp.int32(0)
    for i in range(len_ref.shape[1]):
        size = len_ref[0, i]
        mine = own_ref[0, i] == me
        end = jnp.where(mine, start + size // PAGE, start)
        for p in range(CAP_PAGES):
            inside = (start <= p) & (p < end)
            segment[p] = jnp.where(inside, i, segment[p])
            length[p] = jnp.where(inside, size, length[p])
        start = end
    return segment, length


def layer_kernel(chips, first, pages, last, *refs):
    len_ref, own_ref = refs[:2]
    block_refs = refs[2 : 2 + chips]
    refs = refs[2 + chips :]
    w_in, w_mid, w_uvqk, w_proj = refs[:4]
    refs = refs[4:]
    if first:
        prior_ref, refs = refs[0], refs[1:]
    unit_ref, item_ref = refs[:2]
    refs = refs[2:]
    if not last:
        kv_out, refs = refs[0], refs[1:]
    w_in_v, w_mid_v, w_uvqk_v, w_proj_v, x_ref, proj_ref, att_ref, spare_ref, sem = refs
    copies = [
        pltpu.make_async_copy(a, b, sem.at[i])
        for i, (a, b) in enumerate(
            ((w_in, w_in_v), (w_mid, w_mid_v), (w_uvqk, w_uvqk_v), (w_proj, w_proj_v))
        )
    ]
    for c in copies:
        c.start()
    width = w_in.shape[0]
    segment, length = own_plan(len_ref, own_ref)
    place_columns(x_ref, spare_ref, [ref[0 : pages * PAGE, :] for ref in block_refs], chips)
    for p in range(pages):
        part = slice(p * PAGE, (p + 1) * PAGE)
        page_x = x_ref[part, :]
        page_x = jnp.where(segment[first + p] >= 0, page_x, jnp.zeros_like(page_x))
        x_ref[part, :] = page_x
        x32 = page_x.astype(F32)
        item_ref[part, :] = (
            x32 * lax.rsqrt(jnp.sum(x32 * x32, axis=1, keepdims=True) + NORM_EPSILON)
        ).astype(BF)

    x = x_ref[...]
    hidden_width = w_in.shape[1]
    step = 512
    copies[0].wait()
    mixed = None
    for f in range(0, hidden_width, step):
        hidden = silu(
            jnp.dot(x, w_in_v[:, f : f + step], preferred_element_type=F32)
        ).astype(BF)
        if f == 0:
            copies[1].wait()
        part = jnp.dot(hidden, w_mid_v[f : f + step, :], preferred_element_type=F32)
        mixed = part if mixed is None else mixed + part
    mixed = mixed.astype(BF)
    copies[2].wait()
    for f in range(0, 4 * width, step):
        proj_ref[:, f : f + step] = silu(
            jnp.dot(mixed, w_uvqk_v[:, f : f + step], preferred_element_type=F32)
        ).astype(BF)
    if not last:
        kv_out[:, :width] = proj_ref[:, width : 2 * width]
        kv_out[:, width:] = proj_ref[:, 3 * width :]

    head_width = width // HEADS
    scale = 1.0 / math.sqrt(head_width)
    row_at = lax.broadcasted_iota(jnp.int32, (PAGE, PAGE), 0)
    causal = lane_ids((PAGE, PAGE)) <= row_at
    inverses = [
        jnp.where(
            segment[p] >= 0, 1.0 / jnp.full((1, PAGE), length[p], jnp.int32).astype(F32), 0.0
        )
        for p in range(first + pages)
    ]
    for group in range(0, pages, QUERY_PAGES):
        inside = range(group, min(group + QUERY_PAGES, pages))
        part = slice(group * PAGE, (inside[-1] + 1) * PAGE)
        upto = (inside[-1] + 1) * PAGE
        for h in range(HEADS):
            low = h * head_width
            query = proj_ref[part, 2 * width + low : 2 * width + low + head_width]
            keys = proj_ref[0:upto, 3 * width + low : 3 * width + low + head_width]
            values = proj_ref[0:upto, width + low : width + low + head_width]
            if first:
                keys = jnp.concatenate(
                    [prior_ref[:, width + low : width + low + head_width], keys], axis=0
                )
                values = jnp.concatenate([prior_ref[:, low : low + head_width], values], axis=0)
            scores = lax.dot_general(
                query, keys, (((1,), (1,)), ((), ())), preferred_element_type=F32
            )
            rows = []
            for i, p in enumerate(inside):
                whole = first + p
                row = []
                for c in range(first + inside[-1] + 1):
                    if c > whole:
                        row.append(jnp.zeros((PAGE, PAGE), BF))
                        continue
                    score = silu(
                        scores[i * PAGE : (i + 1) * PAGE, c * PAGE : (c + 1) * PAGE] * scale
                    )
                    if c < whole:
                        factor = jnp.where(segment[c] == segment[whole], inverses[whole], 0.0)
                        row.append((score * factor).astype(BF))
                    else:
                        row.append(jnp.where(causal, score * inverses[whole], 0.0).astype(BF))
                rows.append(row[0] if len(row) == 1 else jnp.concatenate(row, axis=1))
            weights = rows[0] if len(rows) == 1 else jnp.concatenate(rows, axis=0)
            att_ref[part, low : low + head_width] = jnp.dot(
                weights, values, preferred_element_type=F32
            )
    attended = att_ref[...]
    centered = attended - jnp.mean(attended, axis=1, keepdims=True)
    variance = jnp.mean(centered * centered, axis=1, keepdims=True)
    gated = (
        centered * lax.rsqrt(variance + LAYER_EPSILON) * proj_ref[:, :width].astype(F32)
    ).astype(BF)
    copies[3].wait()
    state = mixed.astype(F32) + jnp.dot(gated, w_proj_v[...], preferred_element_type=F32)
    unit_ref[...] = (
        state * lax.rsqrt(jnp.sum(state * state, axis=1, keepdims=True) + NORM_EPSILON)
    ).astype(BF)


def layer(seq_lengths, seq_owner, blocks, weights, prior, first, pages, last):
    chips = len(blocks)
    lanes = blocks[0].shape[1]
    width = chips * lanes
    rows = pages * PAGE
    wide = 4 * width
    operands = [seq_lengths, seq_owner, *blocks, *weights]
    in_specs = [smem(), smem()] + [vmem()] * chips + [hbm()] * 4
    if first:
        operands.append(prior)
        in_specs.append(vmem())
    out_shape = [jax.ShapeDtypeStruct((rows, width), BF)] * 2
    if not last:
        out_shape.append(jax.ShapeDtypeStruct((first * PAGE + rows, 2 * width), BF))
    return pl.pallas_call(
        functools.partial(layer_kernel, chips, first, pages, last),
        out_shape=out_shape,
        in_specs=in_specs,
        out_specs=[vmem()] * len(out_shape),
        scratch_shapes=[pltpu.VMEM(w.shape, BF) for w in weights]
        + [
            pltpu.VMEM((rows, width), BF),
            pltpu.VMEM((rows, wide), BF),
            pltpu.VMEM((rows, width), F32),
            spare_blocks(chips, rows, lanes),
            pltpu.SemaphoreType.DMA((4,)),
        ],
        compiler_params=params(32),
        name="layer",
    )(*operands)


def gradient_kernel(count, *refs):
    len_ref, own_ref, near_ref, far_ref = refs[:4]
    unit_refs = refs[4 : 4 + count]
    item_refs = refs[4 + count : 4 + 2 * count]
    out_ref, neg_ref, next_ref = refs[4 + 2 * count :]
    half = near_ref.shape[0]
    neg_ref[:half, :] = near_ref[...]
    neg_ref[half:, :] = far_ref[...]
    rows = out_ref.shape[0]
    at = 0
    for ref in item_refs:
        next_ref[at : at + ref.shape[0], :] = ref[...].astype(F32)
        at += ref.shape[0]
    next_ref[rows:, :] = jnp.zeros_like(next_ref[rows:, :])
    segment, _ = own_plan(len_ref, own_ref)
    segment = segment + [jnp.int32(-1)]
    negatives = neg_ref[...]
    sharp = 1.0 / SCORE_SHARPNESS
    row_at = lax.broadcasted_iota(jnp.int32, (PAGE, 1), 0)
    at = 0
    for ref in unit_refs:
        size = GRADIENT_PAGES * PAGE
        for low in range(0, ref.shape[0], size):
            count_pages = min(size, ref.shape[0] - low) // PAGE
            block = count_pages * PAGE
            unit = ref[low : low + block, :]
            scores = lax.dot_general(
                unit, negatives, (((1,), (1,)), ((), ())), preferred_element_type=F32
            )
            limits = []
            for page in range(at // PAGE, at // PAGE + count_pages):
                last_row = jnp.where(segment[page + 1] == segment[page], PAGE, PAGE - 1)
                limit = jnp.where(segment[page] >= 0, last_row, 0)
                limits.append((row_at < limit).astype(F32))
            has_next = (limits[0] if count_pages == 1 else jnp.concatenate(limits, axis=0)) > 0.5
            targets = jnp.where(has_next, next_ref[at + 1 : at + 1 + block, :], 0.0)
            positive = jnp.exp(
                jnp.sum(unit.astype(F32) * targets, axis=1, keepdims=True) * sharp
            )
            powers = jnp.exp(scores * sharp)
            total = jnp.sum(powers, axis=1, keepdims=True) + positive
            inverse = 1.0 / total
            probs = (powers * inverse).astype(BF)
            grad = jnp.dot(probs, negatives, preferred_element_type=F32)
            grad = (grad + (positive * inverse - 1.0) * targets) * sharp
            out_ref[at : at + block, :] = jnp.where(has_next, grad, 0.0)
            at += block


def gradient(seq_lengths, seq_owner, near, far, units, items):
    rows = sum(u.shape[0] for u in units)
    half, width = near.shape
    return pl.pallas_call(
        functools.partial(gradient_kernel, len(units)),
        out_shape=jax.ShapeDtypeStruct((rows, width), F32),
        in_specs=[smem(), smem()] + [vmem()] * (2 + 2 * len(units)),
        out_specs=vmem(),
        scratch_shapes=[pltpu.VMEM((2 * half, width), BF), pltpu.VMEM((rows + 8, width), F32)],
        compiler_params=params(28),
        name="gradient",
    )(seq_lengths, seq_owner, near, far, *units, *items)


def on_device(
    item_table, event_ids, seq_lengths, seq_owner, negative_ids, w_in, w_mid, w_uvqk, w_proj
):
    tables = lax.axis_size("table")
    users = lax.axis_size("user")
    chips = tables // 2
    neg_half = negative_ids.shape[0] // 4
    cores = [(t, t ^ 1) for t in range(tables)]
    keeps, gives = gather_rows(
        item_table, event_ids, negative_ids, seq_lengths, seq_owner, tables, CHUNKS
    )
    arrived = []
    for c, size in enumerate(CHUNKS):
        got = lax.ppermute(gives[c], "table", cores)
        blocks = list(merge_columns(keeps[c], got, chips, size, neg_half if c == 0 else 0))
        for s in range(1, chips):
            moves = [(t, (t // 2 + s) % chips * 2 + t % 2) for t in range(tables)]
            blocks[s] = lax.ppermute(blocks[s], "table", moves)
        arrived.append(blocks)

    own = unit_negatives(arrived[0], 2 * neg_half)
    parts = [own]
    for s in range(1, users):
        parts.append(lax.ppermute(own, "user", [(u, u ^ s) for u in range(users)]))
    near = jnp.concatenate(parts, axis=0)
    far = lax.ppermute(near, "table", cores)

    weights = (w_in, w_mid, w_uvqk, w_proj)
    units, items = [], []
    prior, first = None, 0
    for c, size in enumerate(CHUNKS):
        last = c == len(CHUNKS) - 1
        outs = layer(seq_lengths, seq_owner, arrived[c], weights, prior, first, size, last)
        units.append(outs[0])
        items.append(outs[1])
        if not last:
            prior = outs[2]
        first += size
    return gradient(seq_lengths, seq_owner, near, far, units, items)


def solution(mesh):
    return jax.shard_map(
        on_device,
        mesh=mesh,
        in_specs=(
            P(None, "table"),
            P("user"),
            P("user", None),
            P("user", None),
            P("user"),
            P(),
            P(),
            P(),
            P(),
        ),
        out_specs=P(("table", "user"), None),
        check_vma=False,
    )
```

```python
import functools
import math

import jax
import jax.numpy as jnp
from jax import lax
from jax.experimental import pallas as pl
from jax.experimental.pallas import tpu as pltpu
from jax.sharding import PartitionSpec as P

HEADS = 4
PAGE = 128
HALF = PAGE // 2
CAP_PAGES = 6
CHUNKS = (3, 3)
LANES = 128

SCORE_SHARPNESS = 0.02
NORM_EPSILON = 1e-06
LAYER_EPSILON = 1e-05

BF = jnp.bfloat16
F32 = jnp.float32
COPY_PARTS = 8
GRADIENT_PAGES = 3
LAYER_COST = 24
QUERY_PAGES = 2


def params(mebibytes):
    return pltpu.CompilerParams(vmem_limit_bytes=mebibytes * 1024 * 1024)


def run(kernel, operands, in_specs, out_shape, scratch, mebibytes, name, after=(), flops=0):
    count = len(operands)

    def body(*refs):
        kernel(*refs[:count], *refs[count + len(after) :])

    return pl.pallas_call(
        body,
        out_shape=out_shape,
        in_specs=in_specs + [anywhere()] * len(after),
        out_specs=[vmem()] * len(out_shape),
        scratch_shapes=scratch,
        compiler_params=params(mebibytes),
        name=name,
        cost_estimate=pl.CostEstimate(flops=flops, transcendentals=0, bytes_accessed=flops // 300),
    )(*operands, *after)


def stay(array):
    return pltpu.with_memory_space_constraint(array, pltpu.HBM)


def smem():
    return pl.BlockSpec(memory_space=pltpu.SMEM)


def vmem():
    return pl.BlockSpec(memory_space=pltpu.VMEM)


def hbm():
    return pl.BlockSpec(memory_space=pltpu.HBM)


def anywhere():
    return pl.BlockSpec(memory_space=pl.ANY)


def silu(v):
    return v * (0.5 + 0.5 * jnp.tanh(0.5 * v))


def swap_halves(v):
    width = v.shape[1] // 2
    if v.shape[1] == LANES:
        return pltpu.roll(v, width, 1)
    return jnp.concatenate([v[:, width:], v[:, :width]], axis=1)


def place_columns(ref, spare_ref, blocks, chips):
    width = blocks[0].shape[1]
    for s, block in enumerate(blocks):
        chip = source_chip(s, chips)
        if width == LANES:
            ref[:, pl.ds(pl.multiple_of(chip * width, width), width)] = block
        else:
            spare_ref[chip] = block
    if width != LANES:
        ref[...] = jnp.concatenate([spare_ref[chip] for chip in range(chips)], axis=1)


def spare_blocks(chips, rows, width):
    return pltpu.VMEM((chips, rows, width) if width != LANES else (1, 16, LANES), BF)


def lane_ids(shape):
    return lax.broadcasted_iota(jnp.int32, shape, len(shape) - 1)


def turn_table(table_ref, part_ref, rows_ref, sem):
    middle = table_ref.shape[1] // 2
    piece = middle // COPY_PARTS

    def copy(side, i):
        at = pl.ds(side * middle + i * piece, piece)
        return pltpu.make_async_copy(table_ref.at[:, at], part_ref.at[:, at], sem.at[side, i])

    for i in range(COPY_PARTS):
        copy(0, i).start()
        copy(1, i).start()
    for i in range(COPY_PARTS):
        copy(0, i).wait()
        copy(1, i).wait()

        def turn(j, carry):
            at = pl.multiple_of(i * piece + j * LANES, LANES)
            low = part_ref[:, pl.ds(at, LANES)]
            high = part_ref[:, pl.ds(middle + at, LANES)]
            rows_ref[pl.ds(at, LANES), :] = jnp.concatenate([low, high], axis=0).T.astype(F32)
            rows_ref[pl.ds(middle + at, LANES), :] = jnp.concatenate([high, low], axis=0).T.astype(
                F32
            )
            return carry

        lax.fori_loop(0, piece // LANES, turn, 0, unroll=4)


def gather_kernel(tables, start, size, negatives, *refs):
    ids_in, len_in, own_in = refs[:3]
    if negatives:
        neg_in, table_ref, rows_ref, keep_ref, give_ref = refs[3:8]
    else:
        rows_ref, keep_ref, give_ref = refs[3:6]
    ids_ref, len_ref, own_ref, neg_ref, stage_ref, next_ref, small_sem = refs[-7:]
    smalls = [(ids_in, ids_ref), (len_in, len_ref), (own_in, own_ref)]
    if negatives:
        smalls.append((neg_in, neg_ref))
    copies = [pltpu.make_async_copy(a, b, small_sem.at[i]) for i, (a, b) in enumerate(smalls)]
    for c in copies:
        c.start()
    if negatives:
        turn_table(table_ref, refs[-9], rows_ref, refs[-8])
    for c in copies:
        c.wait()
    me = lax.axis_index("table")
    core = me % 2
    chip = me // 2
    chips = tables // 2
    vocab, lanes = rows_ref.shape
    middle = vocab // 2
    first_xor = core * middle
    second_xor = middle - first_xor
    own_lanes = (lane_ids((1, lanes)) < lanes // 2) == (core == 0)

    def fetch(source, base, half):
        def step(j, carry):
            at = pl.multiple_of(j * 8, 8)
            for k in range(8):
                first = source[base + at + k] ^ first_xor
                second = source[base + half + at + k] ^ second_xor
                picked = jnp.where(
                    own_lanes, rows_ref[pl.ds(first, 1), :], rows_ref[pl.ds(second, 1), :]
                )
                stage_ref[pl.ds(at + k, 1), :] = picked
            return carry

        lax.fori_loop(0, half // 8, step, 0, unroll=2)
        return stage_ref[0:half, :].astype(BF)

    if negatives:
        neg_rows = neg_ref.shape[0] // 2
        neg_half = neg_rows // 2
        neg_at = chips * size * HALF
        keep_ref[neg_at : neg_at + neg_half, :] = fetch(neg_ref, core * neg_rows, neg_half)
        give_ref[neg_at : neg_at + neg_half, :] = fetch(neg_ref, (1 - core) * neg_rows, neg_half)

    for t in range(tables):
        next_ref[t] = 0

    def sequence(i, page):
        owner = own_ref[0, i]
        pages = len_ref[0, i] // PAGE
        slot0 = next_ref[owner]
        next_ref[owner] = slot0 + pages
        shift = lax.rem(owner // 2 - chip + chips, chips)
        mine = owner % 2 == core

        def one_page(slot, carry):
            block = fetch(ids_ref, (page + slot - slot0) * PAGE, HALF)
            at = pl.multiple_of((shift * size + slot - start) * HALF, HALF)

            @pl.when(mine)
            def _():
                keep_ref[pl.ds(at, HALF), :] = block

            @pl.when(jnp.logical_not(mine))
            def _():
                give_ref[pl.ds(at, HALF), :] = block

            return carry

        low = jnp.maximum(slot0, start)
        high = jnp.minimum(slot0 + pages, start + size)
        lax.fori_loop(low, high, one_page, 0)
        return page + pages

    lax.fori_loop(0, len_ref.shape[1], sequence, 0)


def gather_rows(event_ids, seq_lengths, seq_owner, negative_ids, table, rows, tables, start, size):
    chips = tables // 2
    negatives = rows is None
    neg_half = negative_ids.shape[0] // 4
    columns, vocab = table.shape
    lanes = 2 * columns
    block = jax.ShapeDtypeStruct((chips * size * HALF + (neg_half if negatives else 0), lanes), BF)
    operands = [event_ids, seq_lengths, seq_owner]
    in_specs = [hbm()] * 3
    out_shape = [block, block]
    scratch = [
        pltpu.SMEM(event_ids.shape, jnp.int32),
        pltpu.SMEM(seq_lengths.shape, jnp.int32),
        pltpu.SMEM(seq_owner.shape, jnp.int32),
        pltpu.SMEM(negative_ids.shape, jnp.int32),
        pltpu.VMEM((max(HALF, neg_half), lanes), F32),
        pltpu.SMEM((tables,), jnp.int32),
        pltpu.SemaphoreType.DMA((4,)),
    ]
    if negatives:
        operands += [negative_ids, table]
        in_specs += [hbm(), hbm()]
        out_shape = [jax.ShapeDtypeStruct((vocab, lanes), F32)] + out_shape
        scratch = [
            pltpu.VMEM((columns, vocab), BF),
            pltpu.SemaphoreType.DMA((2, COPY_PARTS)),
        ] + scratch
    else:
        operands.append(rows)
        in_specs.append(vmem())
    kernel = functools.partial(gather_kernel, tables, start, size, negatives)
    return run(kernel, operands, in_specs, out_shape, scratch, 28, "gather_rows")


def merge_kernel(chips, pages, neg_half, keep_ref, got_ref, *out_refs):
    core = lax.axis_index("table") % 2
    width = keep_ref.shape[1] // 2
    own_lanes = (lane_ids((1, 2 * width)) < width) == (core == 0)

    def merged(at, half):
        own = keep_ref[at : at + half, :].astype(F32)
        other = got_ref[at : at + half, :].astype(F32)
        top = jnp.where(own_lanes, own, other)
        low = swap_halves(jnp.where(own_lanes, other, own))
        return top.astype(BF), low.astype(BF)

    if neg_half:
        top, low = merged(chips * pages * HALF, neg_half)
        at = pages * PAGE
        for s in range(chips):
            out_refs[s][at : at + neg_half, :] = top
            out_refs[s][at + neg_half : at + 2 * neg_half, :] = low
    for s in range(chips):
        for k in range(pages):
            top, low = merged((s * pages + k) * HALF, HALF)
            out_refs[s][k * PAGE : k * PAGE + HALF, :] = top
            out_refs[s][k * PAGE + HALF : (k + 1) * PAGE, :] = low


def merge_columns(keep, got, chips, pages, neg_half, after):
    shape = jax.ShapeDtypeStruct((pages * PAGE + 2 * neg_half, keep.shape[1]), BF)
    kernel = functools.partial(merge_kernel, chips, pages, neg_half)
    specs = [vmem(), vmem()]
    return run(kernel, [keep, got], specs, [shape] * chips, [], 12, "merge_columns", after)


def source_chip(s, chips):
    chip = lax.axis_index("table") // 2
    return lax.rem(chip - s + chips, chips)


def unit_negatives_kernel(chips, neg_rows, *refs):
    block_refs, out_ref, spare_ref = refs[:chips], refs[chips], refs[chips + 1]
    blocks = [ref[ref.shape[0] - neg_rows :, :].astype(F32) for ref in block_refs]
    squares = sum(jnp.sum(b * b, axis=1, keepdims=True) for b in blocks)
    scale = lax.rsqrt(squares + NORM_EPSILON)
    place_columns(out_ref, spare_ref, [(b * scale).astype(BF) for b in blocks], chips)


def unit_negatives(blocks, neg_rows, after):
    chips = len(blocks)
    lanes = blocks[0].shape[1]
    return run(
        functools.partial(unit_negatives_kernel, chips, neg_rows),
        blocks,
        [vmem()] * chips,
        [jax.ShapeDtypeStruct((neg_rows, chips * lanes), BF)],
        [spare_blocks(chips, neg_rows, lanes)],
        8,
        "unit_negatives",
        after,
    )[0]


def own_plan(len_ref, own_ref):
    me = lax.axis_index("table")
    segment = [jnp.int32(-1)] * CAP_PAGES
    length = [jnp.int32(1)] * CAP_PAGES
    start = jnp.int32(0)
    for i in range(len_ref.shape[1]):
        size = len_ref[0, i]
        mine = own_ref[0, i] == me
        end = jnp.where(mine, start + size // PAGE, start)
        for p in range(CAP_PAGES):
            inside = (start <= p) & (p < end)
            segment[p] = jnp.where(inside, i, segment[p])
            length[p] = jnp.where(inside, size, length[p])
        start = end
    return segment, length


def layer_kernel(chips, first, pages, last, *refs):
    len_ref, own_ref = refs[:2]
    block_refs = refs[2 : 2 + chips]
    refs = refs[2 + chips :]
    w_in, w_mid, w_uvqk, w_proj = refs[:4]
    refs = refs[4:]
    if first:
        prior_ref, refs = refs[0], refs[1:]
    unit_ref, item_ref = refs[:2]
    refs = refs[2:]
    if not last:
        kv_out, refs = refs[0], refs[1:]
    w_in_v, w_mid_v, w_uvqk_v, w_proj_v, x_ref, proj_ref, att_ref, spare_ref, sem = refs
    copies = [
        pltpu.make_async_copy(a, b, sem.at[i])
        for i, (a, b) in enumerate(
            ((w_in, w_in_v), (w_mid, w_mid_v), (w_uvqk, w_uvqk_v), (w_proj, w_proj_v))
        )
    ]
    for c in copies:
        c.start()
    width = w_in.shape[0]
    segment, length = own_plan(len_ref, own_ref)
    place_columns(x_ref, spare_ref, [ref[0 : pages * PAGE, :] for ref in block_refs], chips)
    for p in range(pages):
        part = slice(p * PAGE, (p + 1) * PAGE)
        page_x = x_ref[part, :]
        page_x = jnp.where(segment[first + p] >= 0, page_x, jnp.zeros_like(page_x))
        x_ref[part, :] = page_x
        x32 = page_x.astype(F32)
        item_ref[part, :] = (
            x32 * lax.rsqrt(jnp.sum(x32 * x32, axis=1, keepdims=True) + NORM_EPSILON)
        ).astype(BF)

    x = x_ref[...]
    hidden_width = w_in.shape[1]
    step = 512
    copies[0].wait()
    mixed = None
    for f in range(0, hidden_width, step):
        hidden = silu(
            jnp.dot(x, w_in_v[:, f : f + step], preferred_element_type=F32)
        ).astype(BF)
        if f == 0:
            copies[1].wait()
        part = jnp.dot(hidden, w_mid_v[f : f + step, :], preferred_element_type=F32)
        mixed = part if mixed is None else mixed + part
    mixed = mixed.astype(BF)
    copies[2].wait()
    for f in range(0, 4 * width, step):
        proj_ref[:, f : f + step] = silu(
            jnp.dot(mixed, w_uvqk_v[:, f : f + step], preferred_element_type=F32)
        ).astype(BF)
    if not last:
        kv_out[:, :width] = proj_ref[:, width : 2 * width]
        kv_out[:, width:] = proj_ref[:, 3 * width :]

    head_width = width // HEADS
    scale = 1.0 / math.sqrt(head_width)
    row_at = lax.broadcasted_iota(jnp.int32, (PAGE, PAGE), 0)
    causal = lane_ids((PAGE, PAGE)) <= row_at
    inverses = [
        jnp.where(
            segment[p] >= 0, 1.0 / jnp.full((1, PAGE), length[p], jnp.int32).astype(F32), 0.0
        )
        for p in range(first + pages)
    ]
    for group in range(0, pages, QUERY_PAGES):
        inside = range(group, min(group + QUERY_PAGES, pages))
        part = slice(group * PAGE, (inside[-1] + 1) * PAGE)
        upto = (inside[-1] + 1) * PAGE
        for h in range(HEADS):
            low = h * head_width
            query = proj_ref[part, 2 * width + low : 2 * width + low + head_width]
            keys = proj_ref[0:upto, 3 * width + low : 3 * width + low + head_width]
            values = proj_ref[0:upto, width + low : width + low + head_width]
            if first:
                keys = jnp.concatenate(
                    [prior_ref[:, width + low : width + low + head_width], keys], axis=0
                )
                values = jnp.concatenate([prior_ref[:, low : low + head_width], values], axis=0)
            scores = lax.dot_general(
                query, keys, (((1,), (1,)), ((), ())), preferred_element_type=F32
            )
            rows = []
            for i, p in enumerate(inside):
                whole = first + p
                row = []
                for c in range(first + inside[-1] + 1):
                    if c > whole:
                        row.append(jnp.zeros((PAGE, PAGE), BF))
                        continue
                    score = silu(
                        scores[i * PAGE : (i + 1) * PAGE, c * PAGE : (c + 1) * PAGE] * scale
                    )
                    if c < whole:
                        factor = jnp.where(segment[c] == segment[whole], inverses[whole], 0.0)
                        row.append((score * factor).astype(BF))
                    else:
                        row.append(jnp.where(causal, score * inverses[whole], 0.0).astype(BF))
                rows.append(row[0] if len(row) == 1 else jnp.concatenate(row, axis=1))
            weights = rows[0] if len(rows) == 1 else jnp.concatenate(rows, axis=0)
            att_ref[part, low : low + head_width] = jnp.dot(
                weights, values, preferred_element_type=F32
            )
    attended = att_ref[...]
    centered = attended - jnp.mean(attended, axis=1, keepdims=True)
    variance = jnp.mean(centered * centered, axis=1, keepdims=True)
    gated = (
        centered * lax.rsqrt(variance + LAYER_EPSILON) * proj_ref[:, :width].astype(F32)
    ).astype(BF)
    copies[3].wait()
    state = mixed.astype(F32) + jnp.dot(gated, w_proj_v[...], preferred_element_type=F32)
    unit_ref[...] = (
        state * lax.rsqrt(jnp.sum(state * state, axis=1, keepdims=True) + NORM_EPSILON)
    ).astype(BF)


def layer(seq_lengths, seq_owner, blocks, weights, prior, first, pages, last, after):
    chips = len(blocks)
    lanes = blocks[0].shape[1]
    width = chips * lanes
    rows = pages * PAGE
    wide = 4 * width
    operands = [seq_lengths, seq_owner, *blocks, *weights]
    in_specs = [smem(), smem()] + [vmem()] * chips + [anywhere()] * 4
    if first:
        operands.append(prior)
        in_specs.append(vmem())
    out_shape = [jax.ShapeDtypeStruct((rows, width), BF)] * 2
    if not last:
        out_shape.append(jax.ShapeDtypeStruct((first * PAGE + rows, 2 * width), BF))
    scratch = [pltpu.VMEM(w.shape, BF) for w in weights] + [
        pltpu.VMEM((rows, width), BF),
        pltpu.VMEM((rows, wide), BF),
        pltpu.VMEM((rows, width), F32),
        spare_blocks(chips, rows, lanes),
        pltpu.SemaphoreType.DMA((4,)),
    ]
    kernel = functools.partial(layer_kernel, chips, first, pages, last)
    return run(kernel, operands, in_specs, out_shape, scratch, 28, "layer", after, LAYER_COST * rows * width * width)


def join_kernel(*refs):
    rows = refs[0].shape[0]
    for i, ref in enumerate(refs[:-1]):
        refs[-1][i * rows : (i + 1) * rows, :] = ref[...]


def join(parts, after):
    rows, width = parts[0].shape
    shape = [jax.ShapeDtypeStruct((len(parts) * rows, width), BF)]
    return run(join_kernel, parts, [vmem()] * len(parts), shape, [], 8, "join", after)[0]


def score_part(unit, negatives):
    scores = lax.dot_general(
        unit, negatives, (((1,), (1,)), ((), ())), preferred_element_type=F32
    )
    powers = jnp.exp(scores * (1.0 / SCORE_SHARPNESS))
    total = jnp.sum(powers, axis=1, keepdims=True)
    return total, jnp.dot(powers.astype(BF), negatives, preferred_element_type=F32)


def row_blocks(refs):
    at = 0
    for ref in refs:
        size = GRADIENT_PAGES * PAGE
        for low in range(0, ref.shape[0], size):
            block = min(size, ref.shape[0] - low)
            yield ref, low, at, block
            at += block


def near_kernel(count, *refs):
    negatives = refs[0][...]
    unit_refs, (sum_ref, total_ref) = refs[1 : 1 + count], refs[1 + count :]
    for ref, low, at, block in row_blocks(unit_refs):
        total, part = score_part(ref[low : low + block, :], negatives)
        sum_ref[at : at + block, :] = part
        total_ref[at : at + block, :] = total


def near_gradient(near, units):
    rows = sum(u.shape[0] for u in units)
    half, width = near.shape
    shapes = [
        jax.ShapeDtypeStruct((rows, width), F32),
        jax.ShapeDtypeStruct((rows, 1), F32),
    ]
    kernel = functools.partial(near_kernel, len(units))
    specs = [vmem()] * (1 + len(units))
    flops = LAYER_COST * rows * width * width // 4
    return run(kernel, [near, *units], specs, shapes, [], 20, "near_gradient", (), flops)


def far_kernel(count, *refs):
    len_ref, own_ref, far_ref, sum_ref, total_ref = refs[:5]
    unit_refs = refs[5 : 5 + count]
    item_refs = refs[5 + count : 5 + 2 * count]
    out_ref, next_ref = refs[5 + 2 * count :]
    rows = out_ref.shape[0]
    at = 0
    for ref in item_refs:
        next_ref[at : at + ref.shape[0], :] = ref[...].astype(F32)
        at += ref.shape[0]
    next_ref[rows:, :] = jnp.zeros_like(next_ref[rows:, :])
    segment, _ = own_plan(len_ref, own_ref)
    segment = segment + [jnp.int32(-1)]
    negatives = far_ref[...]
    sharp = 1.0 / SCORE_SHARPNESS
    row_at = lax.broadcasted_iota(jnp.int32, (PAGE, 1), 0)
    for ref, low, at, block in row_blocks(unit_refs):
        unit = ref[low : low + block, :]
        limits = []
        for page in range(at // PAGE, (at + block) // PAGE):
            last_row = jnp.where(segment[page + 1] == segment[page], PAGE, PAGE - 1)
            limit = jnp.where(segment[page] >= 0, last_row, 0)
            limits.append((row_at < limit).astype(F32))
        has_next = (limits[0] if len(limits) == 1 else jnp.concatenate(limits, axis=0)) > 0.5
        targets = jnp.where(has_next, next_ref[at + 1 : at + 1 + block, :], 0.0)
        positive = jnp.exp(jnp.sum(unit.astype(F32) * targets, axis=1, keepdims=True) * sharp)
        total, part = score_part(unit, negatives)
        total = total + total_ref[at : at + block, :] + positive
        inverse = 1.0 / total
        grad = (part + sum_ref[at : at + block, :]) * inverse
        grad = (grad + (positive * inverse - 1.0) * targets) * sharp
        out_ref[at : at + block, :] = jnp.where(has_next, grad, 0.0)


def far_gradient(seq_lengths, seq_owner, far, sums, totals, units, items):
    rows, width = sums.shape
    return run(
        functools.partial(far_kernel, len(units)),
        [seq_lengths, seq_owner, far, sums, totals, *units, *items],
        [smem(), smem()] + [vmem()] * (3 + 2 * len(units)),
        [jax.ShapeDtypeStruct((rows, width), F32)],
        [pltpu.VMEM((rows + 8, width), F32)],
        20,
        "far_gradient",
    )[0]


def on_device(
    item_table, event_ids, seq_lengths, seq_owner, negative_ids, w_in, w_mid, w_uvqk, w_proj
):
    tables = lax.axis_size("table")
    users = lax.axis_size("user")
    chips = tables // 2
    neg_half = negative_ids.shape[0] // 4
    cores = [(t, t ^ 1) for t in range(tables)]
    table = stay(item_table.T)
    event_ids, negative_ids = stay(event_ids), stay(negative_ids)
    lengths, owners = stay(seq_lengths), stay(seq_owner)
    rows, first = None, 0
    packed = []
    for size in CHUNKS:
        outs = gather_rows(
            event_ids, lengths, owners, negative_ids, table, rows, tables, first, size
        )
        if rows is None:
            rows = outs[0]
        packed.append(outs[-2:])
        first += size
    packed.append(())
    arrived = []
    for c, size in enumerate(CHUNKS):
        keep, give = packed[c]
        got = lax.ppermute(give, "table", cores)
        own_neg = neg_half if c == 0 else 0
        blocks = list(merge_columns(keep, got, chips, size, own_neg, packed[c + 1][-1:]))
        for s in range(1, chips):
            moves = [(t, (t // 2 + s) % chips * 2 + t % 2) for t in range(tables)]
            blocks[s] = lax.ppermute(blocks[s], "table", moves)
        arrived.append(blocks)
    arrived.append(())

    weights = (w_in, w_mid, w_uvqk, w_proj)
    units, items = [], []
    prior, first = None, 0
    for c, size in enumerate(CHUNKS):
        last = c == len(CHUNKS) - 1
        after = list(arrived[c + 1][:1])
        outs = layer(seq_lengths, seq_owner, arrived[c], weights, prior, first, size, last, after)
        units.append(outs[0])
        items.append(outs[1])
        if not last:
            prior = outs[2]
        if c == 0:
            own = unit_negatives(arrived[0], 2 * neg_half, units + list(arrived[1]))
            parts = [own]
            for s in range(1, users):
                parts.append(lax.ppermute(own, "user", [(u, u ^ s) for u in range(users)]))
        first += size
    near = join(parts, units[1:])
    far = lax.ppermute(near, "table", cores)
    sums, totals = near_gradient(near, units)
    return far_gradient(seq_lengths, seq_owner, far, sums, totals, units, items)


def solution(mesh):
    return jax.shard_map(
        on_device,
        mesh=mesh,
        in_specs=(
            P(None, "table"),
            P("user"),
            P("user", None),
            P("user", None),
            P("user"),
            P(),
            P(),
            P(),
            P(),
        ),
        out_specs=P(("table", "user"), None),
        check_vma=False,
    )
```

```python
import functools
import math

import jax
import jax.numpy as jnp
from jax import lax
from jax.experimental import pallas as pl
from jax.experimental.pallas import tpu as pltpu
from jax.sharding import PartitionSpec as P

HEADS = 4
PAGE = 128
HALF = PAGE // 2
CAP_PAGES = 6
CHUNKS = (3, 3)
LANES = 128

SCORE_SHARPNESS = 0.02
NORM_EPSILON = 1e-06
LAYER_EPSILON = 1e-05

BF = jnp.bfloat16
F32 = jnp.float32
COPY_PARTS = 8
GRADIENT_PAGES = 3
LAYER_COST = 24
FAR_PAGES = 3
QUERY_PAGES = 2


def params(mebibytes):
    return pltpu.CompilerParams(vmem_limit_bytes=mebibytes * 1024 * 1024)


def run(kernel, operands, in_specs, out_shape, scratch, mebibytes, name, after=(), flops=0):
    count = len(operands)

    def body(*refs):
        kernel(*refs[:count], *refs[count + len(after) :])

    return pl.pallas_call(
        body,
        out_shape=out_shape,
        in_specs=in_specs + [anywhere()] * len(after),
        out_specs=[vmem()] * len(out_shape),
        scratch_shapes=scratch,
        compiler_params=params(mebibytes),
        name=name,
        cost_estimate=pl.CostEstimate(flops=flops, transcendentals=0, bytes_accessed=flops // 300),
    )(*operands, *after)


def stay(array):
    return pltpu.with_memory_space_constraint(array, pltpu.HBM)


def smem():
    return pl.BlockSpec(memory_space=pltpu.SMEM)


def vmem():
    return pl.BlockSpec(memory_space=pltpu.VMEM)


def hbm():
    return pl.BlockSpec(memory_space=pltpu.HBM)


def anywhere():
    return pl.BlockSpec(memory_space=pl.ANY)


def silu(v):
    return v * (0.5 + 0.5 * jnp.tanh(0.5 * v))


def swap_halves(v):
    width = v.shape[1] // 2
    if v.shape[1] == LANES:
        return pltpu.roll(v, width, 1)
    return jnp.concatenate([v[:, width:], v[:, :width]], axis=1)


def place_columns(ref, spare_ref, blocks, chips):
    width = blocks[0].shape[1]
    for s, block in enumerate(blocks):
        chip = source_chip(s, chips)
        if width == LANES:
            ref[:, pl.ds(pl.multiple_of(chip * width, width), width)] = block
        else:
            spare_ref[chip] = block
    if width != LANES:
        ref[...] = jnp.concatenate([spare_ref[chip] for chip in range(chips)], axis=1)


def spare_blocks(chips, rows, width):
    return pltpu.VMEM((chips, rows, width) if width != LANES else (1, 16, LANES), BF)


def lane_ids(shape):
    return lax.broadcasted_iota(jnp.int32, shape, len(shape) - 1)


def turn_table(table_ref, part_ref, rows_ref, sem):
    middle = table_ref.shape[1] // 2
    piece = middle // COPY_PARTS

    def copy(side, i):
        at = pl.ds(side * middle + i * piece, piece)
        return pltpu.make_async_copy(table_ref.at[:, at], part_ref.at[:, at], sem.at[side, i])

    for i in range(COPY_PARTS):
        copy(0, i).start()
        copy(1, i).start()
    for i in range(COPY_PARTS):
        copy(0, i).wait()
        copy(1, i).wait()

        def turn(j, carry):
            at = pl.multiple_of(i * piece + j * LANES, LANES)
            low = part_ref[:, pl.ds(at, LANES)]
            high = part_ref[:, pl.ds(middle + at, LANES)]
            rows_ref[pl.ds(at, LANES), :] = jnp.concatenate([low, high], axis=0).T.astype(F32)
            rows_ref[pl.ds(middle + at, LANES), :] = jnp.concatenate([high, low], axis=0).T.astype(
                F32
            )
            return carry

        lax.fori_loop(0, piece // LANES, turn, 0, unroll=16)


def gather_kernel(tables, start, size, negatives, *refs):
    ids_in, len_in, own_in = refs[:3]
    if negatives:
        neg_in, table_ref, rows_ref, keep_ref, give_ref = refs[3:8]
    else:
        rows_ref, keep_ref, give_ref = refs[3:6]
    ids_ref, len_ref, own_ref, neg_ref, stage_ref, next_ref, small_sem = refs[-7:]
    smalls = [(ids_in, ids_ref), (len_in, len_ref), (own_in, own_ref)]
    if negatives:
        smalls.append((neg_in, neg_ref))
    copies = [pltpu.make_async_copy(a, b, small_sem.at[i]) for i, (a, b) in enumerate(smalls)]
    for c in copies:
        c.start()
    if negatives:
        turn_table(table_ref, refs[-9], rows_ref, refs[-8])
    for c in copies:
        c.wait()
    me = lax.axis_index("table")
    core = me % 2
    chip = me // 2
    chips = tables // 2
    vocab, lanes = rows_ref.shape
    middle = vocab // 2
    first_xor = core * middle
    second_xor = middle - first_xor
    own_lanes = (lane_ids((1, lanes)) < lanes // 2) == (core == 0)

    def fetch(source, base, half):
        def step(j, carry):
            at = pl.multiple_of(j * 8, 8)
            for k in range(8):
                first = source[base + at + k] ^ first_xor
                second = source[base + half + at + k] ^ second_xor
                picked = jnp.where(
                    own_lanes, rows_ref[pl.ds(first, 1), :], rows_ref[pl.ds(second, 1), :]
                )
                stage_ref[pl.ds(at + k, 1), :] = picked
            return carry

        lax.fori_loop(0, half // 8, step, 0, unroll=8)
        return stage_ref[0:half, :].astype(BF)

    if negatives:
        neg_rows = neg_ref.shape[0] // 2
        neg_half = neg_rows // 2
        neg_at = chips * size * HALF
        keep_ref[neg_at : neg_at + neg_half, :] = fetch(neg_ref, core * neg_rows, neg_half)
        give_ref[neg_at : neg_at + neg_half, :] = fetch(neg_ref, (1 - core) * neg_rows, neg_half)

    for t in range(tables):
        next_ref[t] = 0

    def sequence(i, page):
        owner = own_ref[0, i]
        pages = len_ref[0, i] // PAGE
        slot0 = next_ref[owner]
        next_ref[owner] = slot0 + pages
        shift = lax.rem(owner // 2 - chip + chips, chips)
        mine = owner % 2 == core

        def one_page(slot, carry):
            block = fetch(ids_ref, (page + slot - slot0) * PAGE, HALF)
            at = pl.multiple_of((shift * size + slot - start) * HALF, HALF)

            @pl.when(mine)
            def _():
                keep_ref[pl.ds(at, HALF), :] = block

            @pl.when(jnp.logical_not(mine))
            def _():
                give_ref[pl.ds(at, HALF), :] = block

            return carry

        low = jnp.maximum(slot0, start)
        high = jnp.minimum(slot0 + pages, start + size)
        lax.fori_loop(low, high, one_page, 0)
        return page + pages

    lax.fori_loop(0, len_ref.shape[1], sequence, 0)


def gather_rows(event_ids, seq_lengths, seq_owner, negative_ids, table, rows, tables, start, size):
    chips = tables // 2
    negatives = rows is None
    neg_half = negative_ids.shape[0] // 4
    columns, vocab = table.shape
    lanes = 2 * columns
    block = jax.ShapeDtypeStruct((chips * size * HALF + (neg_half if negatives else 0), lanes), BF)
    operands = [event_ids, seq_lengths, seq_owner]
    in_specs = [hbm()] * 3
    out_shape = [block, block]
    scratch = [
        pltpu.SMEM(event_ids.shape, jnp.int32),
        pltpu.SMEM(seq_lengths.shape, jnp.int32),
        pltpu.SMEM(seq_owner.shape, jnp.int32),
        pltpu.SMEM(negative_ids.shape, jnp.int32),
        pltpu.VMEM((max(HALF, neg_half), lanes), F32),
        pltpu.SMEM((tables,), jnp.int32),
        pltpu.SemaphoreType.DMA((4,)),
    ]
    if negatives:
        operands += [negative_ids, table]
        in_specs += [hbm(), hbm()]
        out_shape = [jax.ShapeDtypeStruct((vocab, lanes), F32)] + out_shape
        scratch = [
            pltpu.VMEM((columns, vocab), BF),
            pltpu.SemaphoreType.DMA((2, COPY_PARTS)),
        ] + scratch
    else:
        operands.append(rows)
        in_specs.append(vmem())
    kernel = functools.partial(gather_kernel, tables, start, size, negatives)
    return run(kernel, operands, in_specs, out_shape, scratch, 28, "gather_rows")


def merge_kernel(chips, pages, neg_half, keep_ref, got_ref, *out_refs):
    core = lax.axis_index("table") % 2
    width = keep_ref.shape[1] // 2
    own_lanes = (lane_ids((1, 2 * width)) < width) == (core == 0)

    def merged(at, half):
        own = keep_ref[at : at + half, :].astype(F32)
        other = got_ref[at : at + half, :].astype(F32)
        top = jnp.where(own_lanes, own, other)
        low = swap_halves(jnp.where(own_lanes, other, own))
        return top.astype(BF), low.astype(BF)

    if neg_half:
        top, low = merged(chips * pages * HALF, neg_half)
        at = pages * PAGE
        for s in range(chips):
            out_refs[s][at : at + neg_half, :] = top
            out_refs[s][at + neg_half : at + 2 * neg_half, :] = low
    for s in range(chips):
        for k in range(pages):
            top, low = merged((s * pages + k) * HALF, HALF)
            out_refs[s][k * PAGE : k * PAGE + HALF, :] = top
            out_refs[s][k * PAGE + HALF : (k + 1) * PAGE, :] = low


def merge_columns(keep, got, chips, pages, neg_half, after):
    shape = jax.ShapeDtypeStruct((pages * PAGE + 2 * neg_half, keep.shape[1]), BF)
    kernel = functools.partial(merge_kernel, chips, pages, neg_half)
    specs = [vmem(), vmem()]
    return run(kernel, [keep, got], specs, [shape] * chips, [], 12, "merge_columns", after)


def source_chip(s, chips):
    chip = lax.axis_index("table") // 2
    return lax.rem(chip - s + chips, chips)


def unit_negatives_kernel(chips, neg_rows, *refs):
    block_refs, out_ref, spare_ref = refs[:chips], refs[chips], refs[chips + 1]
    blocks = [ref[ref.shape[0] - neg_rows :, :].astype(F32) for ref in block_refs]
    squares = sum(jnp.sum(b * b, axis=1, keepdims=True) for b in blocks)
    scale = lax.rsqrt(squares + NORM_EPSILON)
    place_columns(out_ref, spare_ref, [(b * scale).astype(BF) for b in blocks], chips)


def unit_negatives(blocks, neg_rows, after):
    chips = len(blocks)
    lanes = blocks[0].shape[1]
    return run(
        functools.partial(unit_negatives_kernel, chips, neg_rows),
        blocks,
        [vmem()] * chips,
        [jax.ShapeDtypeStruct((neg_rows, chips * lanes), BF)],
        [spare_blocks(chips, neg_rows, lanes)],
        8,
        "unit_negatives",
        after,
    )[0]


def own_plan(len_ref, own_ref):
    me = lax.axis_index("table")
    segment = [jnp.int32(-1)] * CAP_PAGES
    length = [jnp.int32(1)] * CAP_PAGES
    start = jnp.int32(0)
    for i in range(len_ref.shape[1]):
        size = len_ref[0, i]
        mine = own_ref[0, i] == me
        end = jnp.where(mine, start + size // PAGE, start)
        for p in range(CAP_PAGES):
            inside = (start <= p) & (p < end)
            segment[p] = jnp.where(inside, i, segment[p])
            length[p] = jnp.where(inside, size, length[p])
        start = end
    return segment, length


def layer_kernel(chips, first, pages, last, *refs):
    len_ref, own_ref = refs[:2]
    block_refs = refs[2 : 2 + chips]
    refs = refs[2 + chips :]
    w_in, w_mid, w_uvqk, w_proj = refs[:4]
    refs = refs[4:]
    if first:
        prior_ref, refs = refs[0], refs[1:]
    unit_ref, item_ref = refs[:2]
    refs = refs[2:]
    if not last:
        kv_out, refs = refs[0], refs[1:]
    x_ref, proj_ref, att_ref, spare_ref = refs
    width = w_in.shape[0]
    segment, length = own_plan(len_ref, own_ref)
    place_columns(x_ref, spare_ref, [ref[0 : pages * PAGE, :] for ref in block_refs], chips)
    for p in range(pages):
        part = slice(p * PAGE, (p + 1) * PAGE)
        page_x = x_ref[part, :]
        page_x = jnp.where(segment[first + p] >= 0, page_x, jnp.zeros_like(page_x))
        x_ref[part, :] = page_x
        x32 = page_x.astype(F32)
        item_ref[part, :] = (
            x32 * lax.rsqrt(jnp.sum(x32 * x32, axis=1, keepdims=True) + NORM_EPSILON)
        ).astype(BF)

    x = x_ref[...]
    hidden_width = w_in.shape[1]
    step = 512
    mixed = None
    for f in range(0, hidden_width, step):
        hidden = silu(
            jnp.dot(x, w_in[:, f : f + step], preferred_element_type=F32)
        ).astype(BF)
        part = jnp.dot(hidden, w_mid[f : f + step, :], preferred_element_type=F32)
        mixed = part if mixed is None else mixed + part
    mixed = mixed.astype(BF)
    for f in range(0, 4 * width, step):
        proj_ref[:, f : f + step] = silu(
            jnp.dot(mixed, w_uvqk[:, f : f + step], preferred_element_type=F32)
        ).astype(BF)
    if not last:
        kv_out[:, :width] = proj_ref[:, width : 2 * width]
        kv_out[:, width:] = proj_ref[:, 3 * width :]

    head_width = width // HEADS
    scale = 1.0 / math.sqrt(head_width)
    row_at = lax.broadcasted_iota(jnp.int32, (PAGE, PAGE), 0)
    causal = lane_ids((PAGE, PAGE)) <= row_at
    inverses = [
        jnp.where(
            segment[p] >= 0, 1.0 / jnp.full((1, PAGE), length[p], jnp.int32).astype(F32), 0.0
        )
        for p in range(first + pages)
    ]
    for group in range(0, pages, QUERY_PAGES):
        inside = range(group, min(group + QUERY_PAGES, pages))
        part = slice(group * PAGE, (inside[-1] + 1) * PAGE)
        upto = (inside[-1] + 1) * PAGE
        for h in range(HEADS):
            low = h * head_width
            query = proj_ref[part, 2 * width + low : 2 * width + low + head_width]
            keys = proj_ref[0:upto, 3 * width + low : 3 * width + low + head_width]
            values = proj_ref[0:upto, width + low : width + low + head_width]
            if first:
                keys = jnp.concatenate(
                    [prior_ref[:, width + low : width + low + head_width], keys], axis=0
                )
                values = jnp.concatenate([prior_ref[:, low : low + head_width], values], axis=0)
            scores = lax.dot_general(
                query, keys, (((1,), (1,)), ((), ())), preferred_element_type=F32
            )
            rows = []
            for i, p in enumerate(inside):
                whole = first + p
                row = []
                for c in range(first + inside[-1] + 1):
                    if c > whole:
                        row.append(jnp.zeros((PAGE, PAGE), BF))
                        continue
                    score = silu(
                        scores[i * PAGE : (i + 1) * PAGE, c * PAGE : (c + 1) * PAGE] * scale
                    )
                    if c < whole:
                        factor = jnp.where(segment[c] == segment[whole], inverses[whole], 0.0)
                        row.append((score * factor).astype(BF))
                    else:
                        row.append(jnp.where(causal, score * inverses[whole], 0.0).astype(BF))
                rows.append(row[0] if len(row) == 1 else jnp.concatenate(row, axis=1))
            weights = rows[0] if len(rows) == 1 else jnp.concatenate(rows, axis=0)
            att_ref[part, low : low + head_width] = jnp.dot(
                weights, values, preferred_element_type=F32
            )
    attended = att_ref[...]
    centered = attended - jnp.mean(attended, axis=1, keepdims=True)
    variance = jnp.mean(centered * centered, axis=1, keepdims=True)
    gated = (
        centered * lax.rsqrt(variance + LAYER_EPSILON) * proj_ref[:, :width].astype(F32)
    ).astype(BF)
    state = mixed.astype(F32) + jnp.dot(gated, w_proj[...], preferred_element_type=F32)
    unit_ref[...] = (
        state * lax.rsqrt(jnp.sum(state * state, axis=1, keepdims=True) + NORM_EPSILON)
    ).astype(BF)


def layer(seq_lengths, seq_owner, blocks, weights, prior, first, pages, last, after):
    chips = len(blocks)
    lanes = blocks[0].shape[1]
    width = chips * lanes
    rows = pages * PAGE
    wide = 4 * width
    operands = [seq_lengths, seq_owner, *blocks, *weights]
    in_specs = [smem(), smem()] + [vmem()] * (chips + 4)
    if first:
        operands.append(prior)
        in_specs.append(vmem())
    out_shape = [jax.ShapeDtypeStruct((rows, width), BF)] * 2
    if not last:
        out_shape.append(jax.ShapeDtypeStruct((first * PAGE + rows, 2 * width), BF))
    scratch = [
        pltpu.VMEM((rows, width), BF),
        pltpu.VMEM((rows, wide), BF),
        pltpu.VMEM((rows, width), F32),
        spare_blocks(chips, rows, lanes),
    ]
    kernel = functools.partial(layer_kernel, chips, first, pages, last)
    return run(kernel, operands, in_specs, out_shape, scratch, 28, "layer", after, LAYER_COST * rows * width * width)


def join_kernel(*refs):
    rows = refs[0].shape[0]
    for i, ref in enumerate(refs[:-1]):
        refs[-1][i * rows : (i + 1) * rows, :] = ref[...]


def join(parts, after):
    rows, width = parts[0].shape
    shape = [jax.ShapeDtypeStruct((len(parts) * rows, width), BF)]
    return run(join_kernel, parts, [vmem()] * len(parts), shape, [], 8, "join", after)[0]


def score_part(unit, negatives):
    scores = lax.dot_general(
        unit, negatives, (((1,), (1,)), ((), ())), preferred_element_type=F32
    )
    powers = jnp.exp(scores * (1.0 / SCORE_SHARPNESS))
    total = jnp.sum(powers, axis=1, keepdims=True)
    return total, jnp.dot(powers.astype(BF), negatives, preferred_element_type=F32)


def row_blocks(refs):
    at = 0
    for ref in refs:
        size = GRADIENT_PAGES * PAGE
        for low in range(0, ref.shape[0], size):
            block = min(size, ref.shape[0] - low)
            yield ref, low, at, block
            at += block


def next_limits(segment, first, pages):
    row_at = lax.broadcasted_iota(jnp.int32, (PAGE, 1), 0)
    limits = []
    for page in range(first, first + pages):
        last_row = jnp.where(segment[page + 1] == segment[page], PAGE, PAGE - 1)
        limit = jnp.where(segment[page] >= 0, last_row, 0)
        limits.append((row_at < limit).astype(F32))
    return (limits[0] if pages == 1 else jnp.concatenate(limits, axis=0)) > 0.5


def near_kernel(count, *refs):
    len_ref, own_ref, near_ref = refs[:3]
    unit_refs = refs[3 : 3 + count]
    item_refs = refs[3 + count : 3 + 2 * count]
    sum_ref, total_ref, positive_ref, all_unit_ref, target_ref, next_ref = refs[3 + 2 * count :]
    negatives = near_ref[...]
    at = 0
    for unit, item in zip(unit_refs, item_refs):
        size = item.shape[0]
        next_ref[at : at + size, :] = item[...].astype(F32)
        all_unit_ref[at : at + size, :] = unit[...]
        at += size
    next_ref[at:, :] = jnp.zeros_like(next_ref[at:, :])
    segment, _ = own_plan(len_ref, own_ref)
    segment = segment + [jnp.int32(-1)]
    sharp = 1.0 / SCORE_SHARPNESS
    for ref, low, at, block in row_blocks(unit_refs):
        unit = ref[low : low + block, :]
        has_next = next_limits(segment, at // PAGE, block // PAGE)
        targets = jnp.where(has_next, next_ref[at + 1 : at + 1 + block, :], 0.0)
        target_ref[at : at + block, :] = targets.astype(BF)
        positive = jnp.exp(jnp.sum(unit.astype(F32) * targets, axis=1, keepdims=True) * sharp)
        total, part = score_part(unit, negatives)
        sum_ref[at : at + block, :] = part
        total_ref[at : at + block, :] = total + positive
        positive_ref[at : at + block, :] = jnp.where(has_next, positive, -1.0)


def near_gradient(seq_lengths, seq_owner, near, units, items):
    rows = sum(u.shape[0] for u in units)
    width = near.shape[1]
    shapes = [
        jax.ShapeDtypeStruct((rows, width), F32),
        jax.ShapeDtypeStruct((rows, 1), F32),
        jax.ShapeDtypeStruct((rows, 1), F32),
        jax.ShapeDtypeStruct((rows, width), BF),
        jax.ShapeDtypeStruct((rows, width), BF),
    ]
    return run(
        functools.partial(near_kernel, len(units)),
        [seq_lengths, seq_owner, near, *units, *items],
        [smem(), smem()] + [vmem()] * (1 + 2 * len(units)),
        shapes,
        [pltpu.VMEM((rows + 8, width), F32)],
        20,
        "near_gradient",
        (),
        LAYER_COST * rows * width * width // 4,
    )


def far_kernel(far_ref, sum_ref, total_ref, positive_ref, unit_ref, target_ref, out_ref):
    sharp = 1.0 / SCORE_SHARPNESS
    total, part = score_part(unit_ref[...], far_ref[...])
    positive = positive_ref[...]
    inverse = 1.0 / (total + total_ref[...])
    grad = (part + sum_ref[...]) * inverse
    grad = (grad + (positive * inverse - 1.0) * target_ref[...].astype(F32)) * sharp
    out_ref[...] = jnp.where(positive >= 0.0, grad, 0.0)


def far_gradient(far, sums, totals, positives, unit, targets):
    rows, width = sums.shape
    block = FAR_PAGES * PAGE

    def spec(shape):
        return pl.BlockSpec((block, shape[1]), lambda i: (i, 0))

    operands = [sums, totals, positives, unit, targets]
    return pl.pallas_call(
        far_kernel,
        grid=(rows // block,),
        out_shape=jax.ShapeDtypeStruct((rows, width), F32),
        in_specs=[pl.BlockSpec(far.shape, lambda i: (0, 0))] + [spec(x.shape) for x in operands],
        out_specs=pl.BlockSpec((block, width), lambda i: (i, 0)),
        compiler_params=params(20),
        name="far_gradient",
    )(far, *operands)


def on_device(
    item_table, event_ids, seq_lengths, seq_owner, negative_ids, w_in, w_mid, w_uvqk, w_proj
):
    tables = lax.axis_size("table")
    users = lax.axis_size("user")
    chips = tables // 2
    neg_half = negative_ids.shape[0] // 4
    cores = [(t, t ^ 1) for t in range(tables)]
    table = stay(item_table.T)
    event_ids, negative_ids = stay(event_ids), stay(negative_ids)
    lengths, owners = stay(seq_lengths), stay(seq_owner)
    rows, first = None, 0
    packed = []
    for size in CHUNKS:
        outs = gather_rows(
            event_ids, lengths, owners, negative_ids, table, rows, tables, first, size
        )
        if rows is None:
            rows = outs[0]
        packed.append(outs[-2:])
        first += size
    packed.append(())
    arrived = []
    for c, size in enumerate(CHUNKS):
        keep, give = packed[c]
        got = lax.ppermute(give, "table", cores)
        own_neg = neg_half if c == 0 else 0
        blocks = list(merge_columns(keep, got, chips, size, own_neg, packed[c + 1][-1:]))
        for s in range(1, chips):
            moves = [(t, (t // 2 + s) % chips * 2 + t % 2) for t in range(tables)]
            blocks[s] = lax.ppermute(blocks[s], "table", moves)
        arrived.append(blocks)
    arrived.append(())

    weights = (w_in, w_mid, w_uvqk, w_proj)
    units, items = [], []
    prior, first = None, 0
    for c, size in enumerate(CHUNKS):
        last = c == len(CHUNKS) - 1
        after = list(arrived[c + 1][:1])
        outs = layer(seq_lengths, seq_owner, arrived[c], weights, prior, first, size, last, after)
        units.append(outs[0])
        items.append(outs[1])
        if not last:
            prior = outs[2]
        if c == 0:
            own = unit_negatives(arrived[0], 2 * neg_half, units + list(arrived[1]))
            parts = [own]
            for s in range(1, users):
                parts.append(lax.ppermute(own, "user", [(u, u ^ s) for u in range(users)]))
        first += size
    near = join(parts, units[1:])
    far = lax.ppermute(near, "table", cores)
    return far_gradient(far, *near_gradient(seq_lengths, seq_owner, near, units, items))


def solution(mesh):
    return jax.shard_map(
        on_device,
        mesh=mesh,
        in_specs=(
            P(None, "table"),
            P("user"),
            P("user", None),
            P("user", None),
            P("user"),
            P(),
            P(),
            P(),
            P(),
        ),
        out_specs=P(("table", "user"), None),
        check_vma=False,
    )
```

```python
import functools
import math

import jax
import jax.numpy as jnp
from jax import lax
from jax.experimental import pallas as pl
from jax.experimental.pallas import tpu as pltpu
from jax.sharding import PartitionSpec as P

HEADS = 4
PAGE = 128
HALF = PAGE // 2
CAP_PAGES = 6
CHUNKS = (3, 3)
LANES = 128

SCORE_SHARPNESS = 0.02
NORM_EPSILON = 1e-06
LAYER_EPSILON = 1e-05

BF = jnp.bfloat16
F32 = jnp.float32
COPY_PARTS = 8
GRADIENT_PAGES = 3
LAYER_COST = 24
FAR_PAGES = 3
EARLIER = slice(2, 3)
QUERY_PAGES = 3


def params(mebibytes):
    return pltpu.CompilerParams(vmem_limit_bytes=mebibytes * 1024 * 1024)


def run(kernel, operands, in_specs, out_shape, scratch, mebibytes, name, after=(), flops=0):
    count = len(operands)

    def body(*refs):
        kernel(*refs[:count], *refs[count + len(after) :])

    return pl.pallas_call(
        body,
        out_shape=out_shape,
        in_specs=in_specs + [anywhere()] * len(after),
        out_specs=[vmem()] * len(out_shape),
        scratch_shapes=scratch,
        compiler_params=params(mebibytes),
        name=name,
        cost_estimate=pl.CostEstimate(flops=flops, transcendentals=0, bytes_accessed=flops // 300),
    )(*operands, *after)


def stay(array):
    return pltpu.with_memory_space_constraint(array, pltpu.HBM)


def smem():
    return pl.BlockSpec(memory_space=pltpu.SMEM)


def vmem():
    return pl.BlockSpec(memory_space=pltpu.VMEM)


def hbm():
    return pl.BlockSpec(memory_space=pltpu.HBM)


def anywhere():
    return pl.BlockSpec(memory_space=pl.ANY)


def silu(v):
    return v * (0.5 + 0.5 * jnp.tanh(0.5 * v))


def swap_halves(v):
    width = v.shape[1] // 2
    if v.shape[1] == LANES:
        return pltpu.roll(v, width, 1)
    return jnp.concatenate([v[:, width:], v[:, :width]], axis=1)


def place_columns(ref, spare_ref, blocks, chips):
    width = blocks[0].shape[1]
    for s, block in enumerate(blocks):
        chip = source_chip(s, chips)
        if width == LANES:
            ref[:, pl.ds(pl.multiple_of(chip * width, width), width)] = block
        else:
            spare_ref[chip] = block
    if width != LANES:
        ref[...] = jnp.concatenate([spare_ref[chip] for chip in range(chips)], axis=1)


def spare_blocks(chips, rows, width):
    return pltpu.VMEM((chips, rows, width) if width != LANES else (1, 16, LANES), BF)


def lane_ids(shape):
    return lax.broadcasted_iota(jnp.int32, shape, len(shape) - 1)


def turn_table(table_ref, part_ref, rows_ref, sem):
    middle = table_ref.shape[1] // 2
    piece = middle // COPY_PARTS

    def copy(side, i):
        at = pl.ds(side * middle + i * piece, piece)
        return pltpu.make_async_copy(table_ref.at[:, at], part_ref.at[:, at], sem.at[side, i])

    for i in range(COPY_PARTS):
        copy(0, i).start()
        copy(1, i).start()
    for i in range(COPY_PARTS):
        copy(0, i).wait()
        copy(1, i).wait()

        def turn(j, carry):
            at = pl.multiple_of(i * piece + j * LANES, LANES)
            low = part_ref[:, pl.ds(at, LANES)]
            high = part_ref[:, pl.ds(middle + at, LANES)]
            rows_ref[pl.ds(at, LANES), :] = jnp.concatenate([low, high], axis=0).T.astype(F32)
            rows_ref[pl.ds(middle + at, LANES), :] = jnp.concatenate([high, low], axis=0).T.astype(
                F32
            )
            return carry

        lax.fori_loop(0, piece // LANES, turn, 0, unroll=16)


def gather_kernel(tables, start, size, negatives, *refs):
    ids_in, len_in, own_in = refs[:3]
    if negatives:
        neg_in, table_ref, rows_ref, keep_ref, give_ref = refs[3:8]
    else:
        rows_ref, keep_ref, give_ref = refs[3:6]
    ids_ref, len_ref, own_ref, neg_ref, stage_ref, next_ref, small_sem = refs[-7:]
    smalls = [(ids_in, ids_ref), (len_in, len_ref), (own_in, own_ref)]
    if negatives:
        smalls.append((neg_in, neg_ref))
    copies = [pltpu.make_async_copy(a, b, small_sem.at[i]) for i, (a, b) in enumerate(smalls)]
    for c in copies:
        c.start()
    if negatives:
        turn_table(table_ref, refs[-9], rows_ref, refs[-8])
    for c in copies:
        c.wait()
    me = lax.axis_index("table")
    core = me % 2
    chip = me // 2
    chips = tables // 2
    vocab, lanes = rows_ref.shape
    middle = vocab // 2
    first_xor = core * middle
    second_xor = middle - first_xor
    own_lanes = (lane_ids((1, lanes)) < lanes // 2) == (core == 0)

    def fetch(source, base, half):
        def step(j, carry):
            at = pl.multiple_of(j * 8, 8)
            for k in range(8):
                first = source[base + at + k] ^ first_xor
                second = source[base + half + at + k] ^ second_xor
                picked = jnp.where(
                    own_lanes, rows_ref[pl.ds(first, 1), :], rows_ref[pl.ds(second, 1), :]
                )
                stage_ref[pl.ds(at + k, 1), :] = picked
            return carry

        lax.fori_loop(0, half // 8, step, 0, unroll=8)
        return stage_ref[0:half, :].astype(BF)

    if negatives:
        neg_rows = neg_ref.shape[0] // 2
        neg_half = neg_rows // 2
        neg_at = chips * size * HALF
        keep_ref[neg_at : neg_at + neg_half, :] = fetch(neg_ref, core * neg_rows, neg_half)
        give_ref[neg_at : neg_at + neg_half, :] = fetch(neg_ref, (1 - core) * neg_rows, neg_half)

    for t in range(tables):
        next_ref[t] = 0

    def sequence(i, page):
        owner = own_ref[0, i]
        pages = len_ref[0, i] // PAGE
        slot0 = next_ref[owner]
        next_ref[owner] = slot0 + pages
        shift = lax.rem(owner // 2 - chip + chips, chips)
        mine = owner % 2 == core

        def one_page(slot, carry):
            block = fetch(ids_ref, (page + slot - slot0) * PAGE, HALF)
            at = pl.multiple_of((shift * size + slot - start) * HALF, HALF)

            @pl.when(mine)
            def _():
                keep_ref[pl.ds(at, HALF), :] = block

            @pl.when(jnp.logical_not(mine))
            def _():
                give_ref[pl.ds(at, HALF), :] = block

            return carry

        low = jnp.maximum(slot0, start)
        high = jnp.minimum(slot0 + pages, start + size)
        lax.fori_loop(low, high, one_page, 0)
        return page + pages

    lax.fori_loop(0, len_ref.shape[1], sequence, 0)


def gather_rows(event_ids, seq_lengths, seq_owner, negative_ids, table, rows, tables, start, size):
    chips = tables // 2
    negatives = rows is None
    neg_half = negative_ids.shape[0] // 4
    columns, vocab = table.shape
    lanes = 2 * columns
    block = jax.ShapeDtypeStruct((chips * size * HALF + (neg_half if negatives else 0), lanes), BF)
    operands = [event_ids, seq_lengths, seq_owner]
    in_specs = [hbm()] * 3
    out_shape = [block, block]
    scratch = [
        pltpu.SMEM(event_ids.shape, jnp.int32),
        pltpu.SMEM(seq_lengths.shape, jnp.int32),
        pltpu.SMEM(seq_owner.shape, jnp.int32),
        pltpu.SMEM(negative_ids.shape, jnp.int32),
        pltpu.VMEM((max(HALF, neg_half), lanes), F32),
        pltpu.SMEM((tables,), jnp.int32),
        pltpu.SemaphoreType.DMA((4,)),
    ]
    if negatives:
        operands += [negative_ids, table]
        in_specs += [hbm(), hbm()]
        out_shape = [jax.ShapeDtypeStruct((vocab, lanes), F32)] + out_shape
        scratch = [
            pltpu.VMEM((columns, vocab), BF),
            pltpu.SemaphoreType.DMA((2, COPY_PARTS)),
        ] + scratch
    else:
        operands.append(rows)
        in_specs.append(vmem())
    kernel = functools.partial(gather_kernel, tables, start, size, negatives)
    return run(kernel, operands, in_specs, out_shape, scratch, 28, "gather_rows")


def merge_kernel(chips, pages, neg_half, keep_ref, got_ref, *out_refs):
    core = lax.axis_index("table") % 2
    width = keep_ref.shape[1] // 2
    own_lanes = (lane_ids((1, 2 * width)) < width) == (core == 0)

    def merged(at, half):
        own = keep_ref[at : at + half, :].astype(F32)
        other = got_ref[at : at + half, :].astype(F32)
        top = jnp.where(own_lanes, own, other)
        low = swap_halves(jnp.where(own_lanes, other, own))
        return top.astype(BF), low.astype(BF)

    if neg_half:
        top, low = merged(chips * pages * HALF, neg_half)
        at = pages * PAGE
        for s in range(chips):
            out_refs[s][at : at + neg_half, :] = top
            out_refs[s][at + neg_half : at + 2 * neg_half, :] = low
    for s in range(chips):
        for k in range(pages):
            top, low = merged((s * pages + k) * HALF, HALF)
            out_refs[s][k * PAGE : k * PAGE + HALF, :] = top
            out_refs[s][k * PAGE + HALF : (k + 1) * PAGE, :] = low


def merge_columns(keep, got, chips, pages, neg_half, after):
    shape = jax.ShapeDtypeStruct((pages * PAGE + 2 * neg_half, keep.shape[1]), BF)
    kernel = functools.partial(merge_kernel, chips, pages, neg_half)
    specs = [vmem(), vmem()]
    return run(kernel, [keep, got], specs, [shape] * chips, [], 12, "merge_columns", after)


def source_chip(s, chips):
    chip = lax.axis_index("table") // 2
    return lax.rem(chip - s + chips, chips)


def unit_negatives_kernel(chips, neg_rows, *refs):
    block_refs, out_ref, spare_ref = refs[:chips], refs[chips], refs[chips + 1]
    blocks = [ref[ref.shape[0] - neg_rows :, :].astype(F32) for ref in block_refs]
    squares = sum(jnp.sum(b * b, axis=1, keepdims=True) for b in blocks)
    scale = lax.rsqrt(squares + NORM_EPSILON)
    place_columns(out_ref, spare_ref, [(b * scale).astype(BF) for b in blocks], chips)


def unit_negatives(blocks, neg_rows, after):
    chips = len(blocks)
    lanes = blocks[0].shape[1]
    return run(
        functools.partial(unit_negatives_kernel, chips, neg_rows),
        blocks,
        [vmem()] * chips,
        [jax.ShapeDtypeStruct((neg_rows, chips * lanes), BF)],
        [spare_blocks(chips, neg_rows, lanes)],
        8,
        "unit_negatives",
        after,
    )[0]


def own_plan(len_ref, own_ref):
    me = lax.axis_index("table")
    segment = [jnp.int32(-1)] * CAP_PAGES
    length = [jnp.int32(1)] * CAP_PAGES
    start = jnp.int32(0)
    for i in range(len_ref.shape[1]):
        size = len_ref[0, i]
        mine = own_ref[0, i] == me
        end = jnp.where(mine, start + size // PAGE, start)
        for p in range(CAP_PAGES):
            inside = (start <= p) & (p < end)
            segment[p] = jnp.where(inside, i, segment[p])
            length[p] = jnp.where(inside, size, length[p])
        start = end
    return segment, length


def layer_kernel(chips, first, pages, last, *refs):
    len_ref, own_ref = refs[:2]
    block_refs = refs[2 : 2 + chips]
    refs = refs[2 + chips :]
    w_in, w_mid, w_uvqk, w_proj = refs[:4]
    refs = refs[4:]
    if first:
        prior_ref, refs = refs[0], refs[1:]
    unit_ref, item_ref = refs[:2]
    refs = refs[2:]
    if not last:
        kv_out, refs = refs[0], refs[1:]
    x_ref, proj_ref, att_ref, spare_ref = refs
    width = w_in.shape[0]
    segment, length = own_plan(len_ref, own_ref)
    place_columns(x_ref, spare_ref, [ref[0 : pages * PAGE, :] for ref in block_refs], chips)
    for p in range(pages):
        part = slice(p * PAGE, (p + 1) * PAGE)
        page_x = x_ref[part, :]
        page_x = jnp.where(segment[first + p] >= 0, page_x, jnp.zeros_like(page_x))
        x_ref[part, :] = page_x
        x32 = page_x.astype(F32)
        item_ref[part, :] = (
            x32 * lax.rsqrt(jnp.sum(x32 * x32, axis=1, keepdims=True) + NORM_EPSILON)
        ).astype(BF)

    x = x_ref[...]
    hidden_width = w_in.shape[1]
    step = 1024
    mixed = None
    for f in range(0, hidden_width, step):
        hidden = silu(
            jnp.dot(x, w_in[:, f : f + step], preferred_element_type=F32)
        ).astype(BF)
        part = jnp.dot(hidden, w_mid[f : f + step, :], preferred_element_type=F32)
        mixed = part if mixed is None else mixed + part
    mixed = mixed.astype(BF)
    for f in range(0, 4 * width, step):
        proj_ref[:, f : f + step] = silu(
            jnp.dot(mixed, w_uvqk[:, f : f + step], preferred_element_type=F32)
        ).astype(BF)
    if not last:
        kv_out[:, :width] = proj_ref[:, width : 2 * width]
        kv_out[:, width:] = proj_ref[:, 3 * width :]

    head_width = width // HEADS
    scale = 1.0 / math.sqrt(head_width)
    row_at = lax.broadcasted_iota(jnp.int32, (PAGE, PAGE), 0)
    causal = lane_ids((PAGE, PAGE)) <= row_at
    inverses = [
        jnp.where(
            segment[p] >= 0, 1.0 / jnp.full((1, PAGE), length[p], jnp.int32).astype(F32), 0.0
        )
        for p in range(first + pages)
    ]
    for group in range(0, pages, QUERY_PAGES):
        inside = range(group, min(group + QUERY_PAGES, pages))
        part = slice(group * PAGE, (inside[-1] + 1) * PAGE)
        upto = (inside[-1] + 1) * PAGE
        for h in range(HEADS):
            low = h * head_width
            query = proj_ref[part, 2 * width + low : 2 * width + low + head_width]
            keys = proj_ref[0:upto, 3 * width + low : 3 * width + low + head_width]
            values = proj_ref[0:upto, width + low : width + low + head_width]
            if first:
                keys = jnp.concatenate(
                    [prior_ref[:, width + low : width + low + head_width], keys], axis=0
                )
                values = jnp.concatenate([prior_ref[:, low : low + head_width], values], axis=0)
            scores = lax.dot_general(
                query, keys, (((1,), (1,)), ((), ())), preferred_element_type=F32
            )
            rows = []
            for i, p in enumerate(inside):
                whole = first + p
                row = []
                for c in range(first + inside[-1] + 1):
                    if c > whole:
                        row.append(jnp.zeros((PAGE, PAGE), BF))
                        continue
                    score = silu(
                        scores[i * PAGE : (i + 1) * PAGE, c * PAGE : (c + 1) * PAGE] * scale
                    )
                    if c < whole:
                        factor = jnp.where(segment[c] == segment[whole], inverses[whole], 0.0)
                        row.append((score * factor).astype(BF))
                    else:
                        row.append(jnp.where(causal, score * inverses[whole], 0.0).astype(BF))
                rows.append(row[0] if len(row) == 1 else jnp.concatenate(row, axis=1))
            weights = rows[0] if len(rows) == 1 else jnp.concatenate(rows, axis=0)
            att_ref[part, low : low + head_width] = jnp.dot(
                weights, values, preferred_element_type=F32
            )
    attended = att_ref[...]
    centered = attended - jnp.mean(attended, axis=1, keepdims=True)
    variance = jnp.mean(centered * centered, axis=1, keepdims=True)
    gated = (
        centered * lax.rsqrt(variance + LAYER_EPSILON) * proj_ref[:, :width].astype(F32)
    ).astype(BF)
    state = mixed.astype(F32) + jnp.dot(gated, w_proj[...], preferred_element_type=F32)
    unit_ref[...] = (
        state * lax.rsqrt(jnp.sum(state * state, axis=1, keepdims=True) + NORM_EPSILON)
    ).astype(BF)


def layer(seq_lengths, seq_owner, blocks, weights, prior, first, pages, last, after):
    chips = len(blocks)
    lanes = blocks[0].shape[1]
    width = chips * lanes
    rows = pages * PAGE
    wide = 4 * width
    operands = [seq_lengths, seq_owner, *blocks, *weights]
    in_specs = [smem(), smem()] + [vmem()] * (chips + 4)
    if first:
        operands.append(prior)
        in_specs.append(vmem())
    out_shape = [jax.ShapeDtypeStruct((rows, width), BF)] * 2
    if not last:
        out_shape.append(jax.ShapeDtypeStruct((first * PAGE + rows, 2 * width), BF))
    scratch = [
        pltpu.VMEM((rows, width), BF),
        pltpu.VMEM((rows, wide), BF),
        pltpu.VMEM((rows, width), F32),
        spare_blocks(chips, rows, lanes),
    ]
    kernel = functools.partial(layer_kernel, chips, first, pages, last)
    return run(kernel, operands, in_specs, out_shape, scratch, 28, "layer", after, LAYER_COST * rows * width * width)


def join_kernel(*refs):
    rows = refs[0].shape[0]
    for i, ref in enumerate(refs[:-1]):
        refs[-1][i * rows : (i + 1) * rows, :] = ref[...]


def join(parts, after):
    rows, width = parts[0].shape
    shape = [jax.ShapeDtypeStruct((len(parts) * rows, width), BF)]
    return run(join_kernel, parts, [vmem()] * len(parts), shape, [], 8, "join", after)[0]


def score_part(unit, negatives):
    scores = lax.dot_general(
        unit, negatives, (((1,), (1,)), ((), ())), preferred_element_type=F32
    )
    powers = jnp.exp(scores * (1.0 / SCORE_SHARPNESS))
    total = jnp.sum(powers, axis=1, keepdims=True)
    return total, jnp.dot(powers.astype(BF), negatives, preferred_element_type=F32)


def row_blocks(refs):
    at = 0
    for ref in refs:
        size = GRADIENT_PAGES * PAGE
        for low in range(0, ref.shape[0], size):
            block = min(size, ref.shape[0] - low)
            yield ref, low, at, block
            at += block


def next_limits(segment, first, pages):
    row_at = lax.broadcasted_iota(jnp.int32, (PAGE, 1), 0)
    limits = []
    for page in range(first, first + pages):
        last_row = jnp.where(segment[page + 1] == segment[page], PAGE, PAGE - 1)
        limit = jnp.where(segment[page] >= 0, last_row, 0)
        limits.append((row_at < limit).astype(F32))
    return (limits[0] if pages == 1 else jnp.concatenate(limits, axis=0)) > 0.5


def near_kernel(count, *refs):
    len_ref, own_ref, near_ref = refs[:3]
    unit_refs = refs[3 : 3 + count]
    item_refs = refs[3 + count : 3 + 2 * count]
    sum_ref, total_ref, positive_ref, all_unit_ref, target_ref, next_ref = refs[3 + 2 * count :]
    negatives = near_ref[...]
    at = 0
    for unit, item in zip(unit_refs, item_refs):
        size = item.shape[0]
        next_ref[at : at + size, :] = item[...].astype(F32)
        all_unit_ref[at : at + size, :] = unit[...]
        at += size
    next_ref[at:, :] = jnp.zeros_like(next_ref[at:, :])
    segment, _ = own_plan(len_ref, own_ref)
    segment = segment + [jnp.int32(-1)]
    sharp = 1.0 / SCORE_SHARPNESS
    for ref, low, at, block in row_blocks(unit_refs):
        unit = ref[low : low + block, :]
        has_next = next_limits(segment, at // PAGE, block // PAGE)
        targets = jnp.where(has_next, next_ref[at + 1 : at + 1 + block, :], 0.0)
        target_ref[at : at + block, :] = targets.astype(BF)
        positive = jnp.exp(jnp.sum(unit.astype(F32) * targets, axis=1, keepdims=True) * sharp)
        total, part = score_part(unit, negatives)
        sum_ref[at : at + block, :] = part
        total_ref[at : at + block, :] = total + positive
        positive_ref[at : at + block, :] = jnp.where(has_next, positive, -1.0)


def near_gradient(seq_lengths, seq_owner, near, units, items):
    rows = sum(u.shape[0] for u in units)
    width = near.shape[1]
    shapes = [
        jax.ShapeDtypeStruct((rows, width), F32),
        jax.ShapeDtypeStruct((rows, 1), F32),
        jax.ShapeDtypeStruct((rows, 1), F32),
        jax.ShapeDtypeStruct((rows, width), BF),
        jax.ShapeDtypeStruct((rows, width), BF),
    ]
    return run(
        functools.partial(near_kernel, len(units)),
        [seq_lengths, seq_owner, near, *units, *items],
        [smem(), smem()] + [vmem()] * (1 + 2 * len(units)),
        shapes,
        [pltpu.VMEM((rows + 8, width), F32)],
        20,
        "near_gradient",
        (),
        LAYER_COST * rows * width * width // 4,
    )


def far_kernel(far_ref, sum_ref, total_ref, positive_ref, unit_ref, target_ref, out_ref):
    sharp = 1.0 / SCORE_SHARPNESS
    total, part = score_part(unit_ref[...], far_ref[...])
    positive = positive_ref[...]
    inverse = 1.0 / (total + total_ref[...])
    grad = (part + sum_ref[...]) * inverse
    grad = (grad + (positive * inverse - 1.0) * target_ref[...].astype(F32)) * sharp
    out_ref[...] = jnp.where(positive >= 0.0, grad, 0.0)


def far_gradient(far, sums, totals, positives, unit, targets):
    rows, width = sums.shape
    block = FAR_PAGES * PAGE

    def spec(shape):
        return pl.BlockSpec((block, shape[1]), lambda i: (i, 0))

    operands = [sums, totals, positives, unit, targets]
    return pl.pallas_call(
        far_kernel,
        grid=(rows // block,),
        out_shape=jax.ShapeDtypeStruct((rows, width), F32),
        in_specs=[pl.BlockSpec(far.shape, lambda i: (0, 0))] + [spec(x.shape) for x in operands],
        out_specs=pl.BlockSpec((block, width), lambda i: (i, 0)),
        compiler_params=params(20),
        name="far_gradient",
    )(far, *operands)


def on_device(
    item_table, event_ids, seq_lengths, seq_owner, negative_ids, w_in, w_mid, w_uvqk, w_proj
):
    tables = lax.axis_size("table")
    users = lax.axis_size("user")
    chips = tables // 2
    neg_half = negative_ids.shape[0] // 4
    cores = [(t, t ^ 1) for t in range(tables)]
    table = stay(item_table.T)
    event_ids, negative_ids = stay(event_ids), stay(negative_ids)
    lengths, owners = stay(seq_lengths), stay(seq_owner)
    rows, first = None, 0
    packed = []
    for size in CHUNKS:
        outs = gather_rows(
            event_ids, lengths, owners, negative_ids, table, rows, tables, first, size
        )
        if rows is None:
            rows = outs[0]
        packed.append(outs[-2:])
        first += size
    packed.append(())
    arrived = []
    for c, size in enumerate(CHUNKS):
        keep, give = packed[c]
        got = lax.ppermute(give, "table", cores)
        own_neg = neg_half if c == 0 else 0
        after = list(packed[c + 1][-1:]) + (arrived[0][EARLIER] if c else [])
        blocks = list(merge_columns(keep, got, chips, size, own_neg, after))
        for s in range(1, chips):
            moves = [(t, (t // 2 + s) % chips * 2 + t % 2) for t in range(tables)]
            blocks[s] = lax.ppermute(blocks[s], "table", moves)
        arrived.append(blocks)
    arrived.append(())

    weights = (w_in, w_mid, w_uvqk, w_proj)
    units, items = [], []
    prior, first = None, 0
    for c, size in enumerate(CHUNKS):
        last = c == len(CHUNKS) - 1
        after = list(arrived[c + 1][:1])
        outs = layer(seq_lengths, seq_owner, arrived[c], weights, prior, first, size, last, after)
        units.append(outs[0])
        items.append(outs[1])
        if not last:
            prior = outs[2]
        if c == 0:
            own = unit_negatives(arrived[0], 2 * neg_half, units + list(arrived[1][1:2]))
            parts = [own]
            for s in range(1, users):
                parts.append(lax.ppermute(own, "user", [(u, u ^ s) for u in range(users)]))
        first += size
    near = join(parts, units[1:])
    far = lax.ppermute(near, "table", cores)
    return far_gradient(far, *near_gradient(seq_lengths, seq_owner, near, units, items))


def solution(mesh):
    return jax.shard_map(
        on_device,
        mesh=mesh,
        in_specs=(
            P(None, "table"),
            P("user"),
            P("user", None),
            P("user", None),
            P("user"),
            P(),
            P(),
            P(),
            P(),
        ),
        out_specs=P(("table", "user"), None),
        check_vma=False,
    )
```

```python
import functools
import math

import jax
import jax.numpy as jnp
from jax import lax
from jax.experimental import pallas as pl
from jax.experimental.pallas import tpu as pltpu
from jax.sharding import PartitionSpec as P

HEADS = 4
PAGE = 128
HALF = PAGE // 2
CAP_PAGES = 6
CHUNKS = (3, 3)
LANES = 128

SCORE_SHARPNESS = 0.02
NORM_EPSILON = 1e-06
LAYER_EPSILON = 1e-05

BF = jnp.bfloat16
F32 = jnp.float32
COPY_PARTS = 8
GRADIENT_PAGES = 3
LAYER_COST = 24
FAR_PAGES = 3
EARLIER = slice(2, 3)
QUERY_PAGES = 3


def params(mebibytes):
    return pltpu.CompilerParams(vmem_limit_bytes=mebibytes * 1024 * 1024)


def run(kernel, operands, in_specs, out_shape, scratch, mebibytes, name, after=(), flops=0):
    count = len(operands)

    def body(*refs):
        kernel(*refs[:count], *refs[count + len(after) :])

    return pl.pallas_call(
        body,
        out_shape=out_shape,
        in_specs=in_specs + [anywhere()] * len(after),
        out_specs=[vmem()] * len(out_shape),
        scratch_shapes=scratch,
        compiler_params=params(mebibytes),
        name=name,
        cost_estimate=pl.CostEstimate(flops=flops, transcendentals=0, bytes_accessed=flops // 300),
    )(*operands, *after)


def stay(array):
    return pltpu.with_memory_space_constraint(array, pltpu.HBM)


def smem():
    return pl.BlockSpec(memory_space=pltpu.SMEM)


def vmem():
    return pl.BlockSpec(memory_space=pltpu.VMEM)


def hbm():
    return pl.BlockSpec(memory_space=pltpu.HBM)


def anywhere():
    return pl.BlockSpec(memory_space=pl.ANY)


def silu(v):
    return v * (0.5 + 0.5 * jnp.tanh(0.5 * v))


def swap_halves(v):
    width = v.shape[1] // 2
    if v.shape[1] == LANES:
        return pltpu.roll(v, width, 1)
    return jnp.concatenate([v[:, width:], v[:, :width]], axis=1)


def place_columns(ref, spare_ref, blocks, chips):
    width = blocks[0].shape[1]
    for s, block in enumerate(blocks):
        chip = source_chip(s, chips)
        if width == LANES:
            ref[:, pl.ds(pl.multiple_of(chip * width, width), width)] = block
        else:
            spare_ref[chip] = block
    if width != LANES:
        ref[...] = jnp.concatenate([spare_ref[chip] for chip in range(chips)], axis=1)


def spare_blocks(chips, rows, width):
    return pltpu.VMEM((chips, rows, width) if width != LANES else (1, 16, LANES), BF)


def lane_ids(shape):
    return lax.broadcasted_iota(jnp.int32, shape, len(shape) - 1)


def turn_table(table_ref, part_ref, rows_ref, sem):
    middle = table_ref.shape[1] // 2
    piece = middle // COPY_PARTS

    def copy(side, i):
        at = pl.ds(side * middle + i * piece, piece)
        return pltpu.make_async_copy(table_ref.at[:, at], part_ref.at[:, at], sem.at[side, i])

    for i in range(COPY_PARTS):
        copy(0, i).start()
        copy(1, i).start()
    for i in range(COPY_PARTS):
        copy(0, i).wait()
        copy(1, i).wait()

        def turn(j, carry):
            at = pl.multiple_of(i * piece + j * LANES, LANES)
            low = part_ref[:, pl.ds(at, LANES)]
            high = part_ref[:, pl.ds(middle + at, LANES)]
            rows_ref[pl.ds(at, LANES), :] = jnp.concatenate([low, high], axis=0).T.astype(F32)
            rows_ref[pl.ds(middle + at, LANES), :] = jnp.concatenate([high, low], axis=0).T.astype(
                F32
            )
            return carry

        lax.fori_loop(0, piece // LANES, turn, 0, unroll=16)


def gather_kernel(tables, start, size, negatives, *refs):
    ids_in, len_in, own_in = refs[:3]
    if negatives:
        neg_in, table_ref, rows_ref, keep_ref, give_ref = refs[3:8]
    else:
        rows_ref, keep_ref, give_ref, second_ref = refs[3:7]
    ids_ref, len_ref, own_ref, neg_ref, stage_ref, next_ref, small_sem = refs[-7:]
    smalls = [(ids_in, ids_ref), (len_in, len_ref), (own_in, own_ref)]
    if negatives:
        smalls.append((neg_in, neg_ref))
    copies = [pltpu.make_async_copy(a, b, small_sem.at[i]) for i, (a, b) in enumerate(smalls)]
    for c in copies:
        c.start()
    if negatives:
        turn_table(table_ref, refs[-9], rows_ref, refs[-8])
    for c in copies:
        c.wait()
    me = lax.axis_index("table")
    core = me % 2
    chip = me // 2
    chips = tables // 2
    vocab, lanes = rows_ref.shape
    middle = vocab // 2
    first_xor = core * middle
    second_xor = middle - first_xor
    own_lanes = (lane_ids((1, lanes)) < lanes // 2) == (core == 0)

    def fetch(source, base, half):
        def step(j, carry):
            at = pl.multiple_of(j * 8, 8)
            for k in range(8):
                first = source[base + at + k] ^ first_xor
                second = source[base + half + at + k] ^ second_xor
                picked = jnp.where(
                    own_lanes, rows_ref[pl.ds(first, 1), :], rows_ref[pl.ds(second, 1), :]
                )
                stage_ref[pl.ds(at + k, 1), :] = picked
            return carry

        lax.fori_loop(0, half // 8, step, 0, unroll=8)
        return stage_ref[0:half, :].astype(BF)

    if negatives:
        neg_rows = neg_ref.shape[0] // 2
        neg_half = neg_rows // 2
        neg_at = chips * size * HALF
        keep_ref[neg_at : neg_at + neg_half, :] = fetch(neg_ref, core * neg_rows, neg_half)
        give_ref[neg_at : neg_at + neg_half, :] = fetch(neg_ref, (1 - core) * neg_rows, neg_half)

    for t in range(tables):
        next_ref[t] = 0

    def sequence(i, page):
        owner = own_ref[0, i]
        pages = len_ref[0, i] // PAGE
        slot0 = next_ref[owner]
        next_ref[owner] = slot0 + pages
        shift = lax.rem(owner // 2 - chip + chips, chips)
        mine = owner % 2 == core

        def one_page(slot, carry):
            block = fetch(ids_ref, (page + slot - slot0) * PAGE, HALF)
            at = pl.multiple_of((shift * size + slot - start) * HALF, HALF)

            @pl.when(mine)
            def _():
                keep_ref[pl.ds(at, HALF), :] = block

            if negatives:

                @pl.when(jnp.logical_not(mine))
                def _():
                    give_ref[pl.ds(at, HALF), :] = block

            else:
                late = shift >= chips // 2
                border = chips // 2 * size * HALF

                @pl.when(jnp.logical_not(mine) & jnp.logical_not(late))
                def _():
                    give_ref[pl.ds(at, HALF), :] = block

                @pl.when(jnp.logical_not(mine) & late)
                def _():
                    second_ref[pl.ds(pl.multiple_of(at - border, HALF), HALF), :] = block

            return carry

        low = jnp.maximum(slot0, start)
        high = jnp.minimum(slot0 + pages, start + size)
        lax.fori_loop(low, high, one_page, 0)
        return page + pages

    lax.fori_loop(0, len_ref.shape[1], sequence, 0)


def gather_rows(
    event_ids, seq_lengths, seq_owner, negative_ids, table, rows, tables, start, size, after
):
    chips = tables // 2
    negatives = rows is None
    neg_half = negative_ids.shape[0] // 4
    columns, vocab = table.shape
    lanes = 2 * columns
    block = jax.ShapeDtypeStruct((chips * size * HALF + (neg_half if negatives else 0), lanes), BF)
    operands = [event_ids, seq_lengths, seq_owner]
    in_specs = [hbm()] * 3
    out_shape = [block, block]
    scratch = [
        pltpu.SMEM(event_ids.shape, jnp.int32),
        pltpu.SMEM(seq_lengths.shape, jnp.int32),
        pltpu.SMEM(seq_owner.shape, jnp.int32),
        pltpu.SMEM(negative_ids.shape, jnp.int32),
        pltpu.VMEM((max(HALF, neg_half), lanes), F32),
        pltpu.SMEM((tables,), jnp.int32),
        pltpu.SemaphoreType.DMA((4,)),
    ]
    if negatives:
        operands += [negative_ids, table]
        in_specs += [hbm(), hbm()]
        out_shape = [jax.ShapeDtypeStruct((vocab, lanes), F32)] + out_shape
        scratch = [
            pltpu.VMEM((columns, vocab), BF),
            pltpu.SemaphoreType.DMA((2, COPY_PARTS)),
        ] + scratch
    else:
        part = jax.ShapeDtypeStruct((chips // 2 * size * HALF, lanes), BF)
        out_shape = [block, part, part]
        operands.append(rows)
        in_specs.append(vmem())
    kernel = functools.partial(gather_kernel, tables, start, size, negatives)
    return run(kernel, operands, in_specs, out_shape, scratch, 28, "gather_rows", after)


def merge_kernel(chips, pages, neg_half, keep_ref, *refs):
    got_refs, out_refs = refs[:-chips], refs[-chips:]
    core = lax.axis_index("table") % 2
    width = keep_ref.shape[1] // 2
    own_lanes = (lane_ids((1, 2 * width)) < width) == (core == 0)

    def merged(at, half):
        own = keep_ref[at : at + half, :].astype(F32)
        got_ref, low_at = got_refs[0], at
        if len(got_refs) > 1 and at >= got_ref.shape[0]:
            got_ref, low_at = got_refs[1], at - got_ref.shape[0]
        other = got_ref[low_at : low_at + half, :].astype(F32)
        top = jnp.where(own_lanes, own, other)
        low = swap_halves(jnp.where(own_lanes, other, own))
        return top.astype(BF), low.astype(BF)

    if neg_half:
        top, low = merged(chips * pages * HALF, neg_half)
        at = pages * PAGE
        for s in range(chips):
            out_refs[s][at : at + neg_half, :] = top
            out_refs[s][at + neg_half : at + 2 * neg_half, :] = low
    for s in range(chips):
        for k in range(pages):
            top, low = merged((s * pages + k) * HALF, HALF)
            out_refs[s][k * PAGE : k * PAGE + HALF, :] = top
            out_refs[s][k * PAGE + HALF : (k + 1) * PAGE, :] = low


def merge_columns(keep, got, chips, pages, neg_half, after):
    shape = jax.ShapeDtypeStruct((pages * PAGE + 2 * neg_half, keep.shape[1]), BF)
    kernel = functools.partial(merge_kernel, chips, pages, neg_half)
    specs = [vmem()] * (1 + len(got))
    return run(kernel, [keep, *got], specs, [shape] * chips, [], 12, "merge_columns", after)


def source_chip(s, chips):
    chip = lax.axis_index("table") // 2
    return lax.rem(chip - s + chips, chips)


def unit_negatives_kernel(chips, neg_rows, *refs):
    block_refs, out_ref, spare_ref = refs[:chips], refs[chips], refs[chips + 1]
    blocks = [ref[ref.shape[0] - neg_rows :, :].astype(F32) for ref in block_refs]
    squares = sum(jnp.sum(b * b, axis=1, keepdims=True) for b in blocks)
    scale = lax.rsqrt(squares + NORM_EPSILON)
    place_columns(out_ref, spare_ref, [(b * scale).astype(BF) for b in blocks], chips)


def unit_negatives(blocks, neg_rows, after):
    chips = len(blocks)
    lanes = blocks[0].shape[1]
    return run(
        functools.partial(unit_negatives_kernel, chips, neg_rows),
        blocks,
        [vmem()] * chips,
        [jax.ShapeDtypeStruct((neg_rows, chips * lanes), BF)],
        [spare_blocks(chips, neg_rows, lanes)],
        8,
        "unit_negatives",
        after,
    )[0]


def own_plan(len_ref, own_ref):
    me = lax.axis_index("table")
    segment = [jnp.int32(-1)] * CAP_PAGES
    length = [jnp.int32(1)] * CAP_PAGES
    start = jnp.int32(0)
    for i in range(len_ref.shape[1]):
        size = len_ref[0, i]
        mine = own_ref[0, i] == me
        end = jnp.where(mine, start + size // PAGE, start)
        for p in range(CAP_PAGES):
            inside = (start <= p) & (p < end)
            segment[p] = jnp.where(inside, i, segment[p])
            length[p] = jnp.where(inside, size, length[p])
        start = end
    return segment, length


def layer_kernel(chips, first, pages, last, *refs):
    len_ref, own_ref = refs[:2]
    block_refs = refs[2 : 2 + chips]
    refs = refs[2 + chips :]
    w_in, w_mid, w_uvqk, w_proj = refs[:4]
    refs = refs[4:]
    if first:
        prior_ref, refs = refs[0], refs[1:]
    unit_ref, item_ref = refs[:2]
    refs = refs[2:]
    if not last:
        kv_out, refs = refs[0], refs[1:]
    x_ref, proj_ref, att_ref, spare_ref = refs
    width = w_in.shape[0]
    segment, length = own_plan(len_ref, own_ref)
    place_columns(x_ref, spare_ref, [ref[0 : pages * PAGE, :] for ref in block_refs], chips)
    for p in range(pages):
        part = slice(p * PAGE, (p + 1) * PAGE)
        page_x = x_ref[part, :]
        page_x = jnp.where(segment[first + p] >= 0, page_x, jnp.zeros_like(page_x))
        x_ref[part, :] = page_x
        x32 = page_x.astype(F32)
        item_ref[part, :] = (
            x32 * lax.rsqrt(jnp.sum(x32 * x32, axis=1, keepdims=True) + NORM_EPSILON)
        ).astype(BF)

    x = x_ref[...]
    hidden_width = w_in.shape[1]
    step = 1024
    mixed = None
    for f in range(0, hidden_width, step):
        hidden = silu(
            jnp.dot(x, w_in[:, f : f + step], preferred_element_type=F32)
        ).astype(BF)
        part = jnp.dot(hidden, w_mid[f : f + step, :], preferred_element_type=F32)
        mixed = part if mixed is None else mixed + part
    mixed = mixed.astype(BF)
    for f in range(0, 4 * width, step):
        proj_ref[:, f : f + step] = silu(
            jnp.dot(mixed, w_uvqk[:, f : f + step], preferred_element_type=F32)
        ).astype(BF)
    if not last:
        kv_out[:, :width] = proj_ref[:, width : 2 * width]
        kv_out[:, width:] = proj_ref[:, 3 * width :]

    head_width = width // HEADS
    scale = 1.0 / math.sqrt(head_width)
    row_at = lax.broadcasted_iota(jnp.int32, (PAGE, PAGE), 0)
    causal = lane_ids((PAGE, PAGE)) <= row_at
    inverses = [
        jnp.where(
            segment[p] >= 0, 1.0 / jnp.full((1, PAGE), length[p], jnp.int32).astype(F32), 0.0
        )
        for p in range(first + pages)
    ]
    for group in range(0, pages, QUERY_PAGES):
        inside = range(group, min(group + QUERY_PAGES, pages))
        part = slice(group * PAGE, (inside[-1] + 1) * PAGE)
        upto = (inside[-1] + 1) * PAGE
        for h in range(HEADS):
            low = h * head_width
            query = proj_ref[part, 2 * width + low : 2 * width + low + head_width]
            keys = proj_ref[0:upto, 3 * width + low : 3 * width + low + head_width]
            values = proj_ref[0:upto, width + low : width + low + head_width]
            if first:
                keys = jnp.concatenate(
                    [prior_ref[:, width + low : width + low + head_width], keys], axis=0
                )
                values = jnp.concatenate([prior_ref[:, low : low + head_width], values], axis=0)
            scores = lax.dot_general(
                query, keys, (((1,), (1,)), ((), ())), preferred_element_type=F32
            )
            rows = []
            for i, p in enumerate(inside):
                whole = first + p
                row = []
                for c in range(first + inside[-1] + 1):
                    if c > whole:
                        row.append(jnp.zeros((PAGE, PAGE), BF))
                        continue
                    score = silu(
                        scores[i * PAGE : (i + 1) * PAGE, c * PAGE : (c + 1) * PAGE] * scale
                    )
                    if c < whole:
                        factor = jnp.where(segment[c] == segment[whole], inverses[whole], 0.0)
                        row.append((score * factor).astype(BF))
                    else:
                        row.append(jnp.where(causal, score * inverses[whole], 0.0).astype(BF))
                rows.append(row[0] if len(row) == 1 else jnp.concatenate(row, axis=1))
            weights = rows[0] if len(rows) == 1 else jnp.concatenate(rows, axis=0)
            att_ref[part, low : low + head_width] = jnp.dot(
                weights, values, preferred_element_type=F32
            )
    attended = att_ref[...]
    centered = attended - jnp.mean(attended, axis=1, keepdims=True)
    variance = jnp.mean(centered * centered, axis=1, keepdims=True)
    gated = (
        centered * lax.rsqrt(variance + LAYER_EPSILON) * proj_ref[:, :width].astype(F32)
    ).astype(BF)
    state = mixed.astype(F32) + jnp.dot(gated, w_proj[...], preferred_element_type=F32)
    unit_ref[...] = (
        state * lax.rsqrt(jnp.sum(state * state, axis=1, keepdims=True) + NORM_EPSILON)
    ).astype(BF)


def layer(seq_lengths, seq_owner, blocks, weights, prior, first, pages, last, after):
    chips = len(blocks)
    lanes = blocks[0].shape[1]
    width = chips * lanes
    rows = pages * PAGE
    wide = 4 * width
    operands = [seq_lengths, seq_owner, *blocks, *weights]
    in_specs = [smem(), smem()] + [vmem()] * (chips + 4)
    if first:
        operands.append(prior)
        in_specs.append(vmem())
    out_shape = [jax.ShapeDtypeStruct((rows, width), BF)] * 2
    if not last:
        out_shape.append(jax.ShapeDtypeStruct((first * PAGE + rows, 2 * width), BF))
    scratch = [
        pltpu.VMEM((rows, width), BF),
        pltpu.VMEM((rows, wide), BF),
        pltpu.VMEM((rows, width), F32),
        spare_blocks(chips, rows, lanes),
    ]
    kernel = functools.partial(layer_kernel, chips, first, pages, last)
    return run(kernel, operands, in_specs, out_shape, scratch, 28, "layer", after, LAYER_COST * rows * width * width)


def join_kernel(*refs):
    rows = refs[0].shape[0]
    for i, ref in enumerate(refs[:-1]):
        refs[-1][i * rows : (i + 1) * rows, :] = ref[...]


def join(parts, after):
    rows, width = parts[0].shape
    shape = [jax.ShapeDtypeStruct((len(parts) * rows, width), BF)]
    return run(join_kernel, parts, [vmem()] * len(parts), shape, [], 8, "join", after)[0]


def score_part(unit, negatives):
    scores = lax.dot_general(
        unit, negatives, (((1,), (1,)), ((), ())), preferred_element_type=F32
    )
    powers = jnp.exp(scores * (1.0 / SCORE_SHARPNESS))
    total = jnp.sum(powers, axis=1, keepdims=True)
    return total, jnp.dot(powers.astype(BF), negatives, preferred_element_type=F32)


def row_blocks(refs):
    at = 0
    for ref in refs:
        size = GRADIENT_PAGES * PAGE
        for low in range(0, ref.shape[0], size):
            block = min(size, ref.shape[0] - low)
            yield ref, low, at, block
            at += block


def next_limits(segment, first, pages):
    row_at = lax.broadcasted_iota(jnp.int32, (PAGE, 1), 0)
    limits = []
    for page in range(first, first + pages):
        last_row = jnp.where(segment[page + 1] == segment[page], PAGE, PAGE - 1)
        limit = jnp.where(segment[page] >= 0, last_row, 0)
        limits.append((row_at < limit).astype(F32))
    return (limits[0] if pages == 1 else jnp.concatenate(limits, axis=0)) > 0.5


def near_kernel(count, *refs):
    len_ref, own_ref, near_ref = refs[:3]
    unit_refs = refs[3 : 3 + count]
    item_refs = refs[3 + count : 3 + 2 * count]
    sum_ref, total_ref, positive_ref, all_unit_ref, target_ref, next_ref = refs[3 + 2 * count :]
    negatives = near_ref[...]
    at = 0
    for unit, item in zip(unit_refs, item_refs):
        size = item.shape[0]
        next_ref[at : at + size, :] = item[...].astype(F32)
        all_unit_ref[at : at + size, :] = unit[...]
        at += size
    next_ref[at:, :] = jnp.zeros_like(next_ref[at:, :])
    segment, _ = own_plan(len_ref, own_ref)
    segment = segment + [jnp.int32(-1)]
    sharp = 1.0 / SCORE_SHARPNESS
    for ref, low, at, block in row_blocks(unit_refs):
        unit = ref[low : low + block, :]
        has_next = next_limits(segment, at // PAGE, block // PAGE)
        targets = jnp.where(has_next, next_ref[at + 1 : at + 1 + block, :], 0.0)
        target_ref[at : at + block, :] = targets.astype(BF)
        positive = jnp.exp(jnp.sum(unit.astype(F32) * targets, axis=1, keepdims=True) * sharp)
        total, part = score_part(unit, negatives)
        sum_ref[at : at + block, :] = part
        total_ref[at : at + block, :] = total + positive
        positive_ref[at : at + block, :] = jnp.where(has_next, positive, -1.0)


def near_gradient(seq_lengths, seq_owner, near, units, items):
    rows = sum(u.shape[0] for u in units)
    width = near.shape[1]
    shapes = [
        jax.ShapeDtypeStruct((rows, width), F32),
        jax.ShapeDtypeStruct((rows, 1), F32),
        jax.ShapeDtypeStruct((rows, 1), F32),
        jax.ShapeDtypeStruct((rows, width), BF),
        jax.ShapeDtypeStruct((rows, width), BF),
    ]
    return run(
        functools.partial(near_kernel, len(units)),
        [seq_lengths, seq_owner, near, *units, *items],
        [smem(), smem()] + [vmem()] * (1 + 2 * len(units)),
        shapes,
        [pltpu.VMEM((rows + 8, width), F32)],
        20,
        "near_gradient",
        (),
        LAYER_COST * rows * width * width // 4,
    )


def far_kernel(far_ref, sum_ref, total_ref, positive_ref, unit_ref, target_ref, out_ref):
    sharp = 1.0 / SCORE_SHARPNESS
    total, part = score_part(unit_ref[...], far_ref[...])
    positive = positive_ref[...]
    inverse = 1.0 / (total + total_ref[...])
    grad = (part + sum_ref[...]) * inverse
    grad = (grad + (positive * inverse - 1.0) * target_ref[...].astype(F32)) * sharp
    out_ref[...] = jnp.where(positive >= 0.0, grad, 0.0)


def far_gradient(far, sums, totals, positives, unit, targets):
    rows, width = sums.shape
    block = FAR_PAGES * PAGE

    def spec(shape):
        return pl.BlockSpec((block, shape[1]), lambda i: (i, 0))

    operands = [sums, totals, positives, unit, targets]
    return pl.pallas_call(
        far_kernel,
        grid=(rows // block,),
        out_shape=jax.ShapeDtypeStruct((rows, width), F32),
        in_specs=[pl.BlockSpec(far.shape, lambda i: (0, 0))] + [spec(x.shape) for x in operands],
        out_specs=pl.BlockSpec((block, width), lambda i: (i, 0)),
        compiler_params=params(20),
        name="far_gradient",
    )(far, *operands)


def on_device(
    item_table, event_ids, seq_lengths, seq_owner, negative_ids, w_in, w_mid, w_uvqk, w_proj
):
    tables = lax.axis_size("table")
    users = lax.axis_size("user")
    chips = tables // 2
    neg_half = negative_ids.shape[0] // 4
    cores = [(t, t ^ 1) for t in range(tables)]
    table = stay(item_table.T)
    event_ids, negative_ids = stay(event_ids), stay(negative_ids)
    lengths, owners = stay(seq_lengths), stay(seq_owner)
    rows, first = None, 0
    arrived, after, gate = [], [], []
    for c, size in enumerate(CHUNKS):
        outs = gather_rows(
            event_ids, lengths, owners, negative_ids, table, rows, tables, first, size, after
        )
        if rows is None:
            rows = outs[0]
        keep, *gives = outs[1:] if c == 0 else outs
        got = [lax.ppermute(give, "table", cores) for give in gives]
        blocks = list(merge_columns(keep, got, chips, size, neg_half if c == 0 else 0, gate))
        after = blocks[:1]
        for s in range(1, chips):
            moves = [(t, (t // 2 + s) % chips * 2 + t % 2) for t in range(tables)]
            blocks[s] = lax.ppermute(blocks[s], "table", moves)
        gate = blocks[EARLIER]
        arrived.append(blocks)
        first += size
    arrived.append(())

    weights = (w_in, w_mid, w_uvqk, w_proj)
    units, items = [], []
    prior, first = None, 0
    for c, size in enumerate(CHUNKS):
        last = c == len(CHUNKS) - 1
        after = list(arrived[c + 1][:1])
        outs = layer(seq_lengths, seq_owner, arrived[c], weights, prior, first, size, last, after)
        units.append(outs[0])
        items.append(outs[1])
        if not last:
            prior = outs[2]
        if c == 0:
            own = unit_negatives(arrived[0], 2 * neg_half, units + list(arrived[1][1:2]))
            parts = [own]
            for s in range(1, users):
                parts.append(lax.ppermute(own, "user", [(u, u ^ s) for u in range(users)]))
        first += size
    near = join(parts, units[1:])
    far = lax.ppermute(near, "table", cores)
    return far_gradient(far, *near_gradient(seq_lengths, seq_owner, near, units, items))


def solution(mesh):
    return jax.shard_map(
        on_device,
        mesh=mesh,
        in_specs=(
            P(None, "table"),
            P("user"),
            P("user", None),
            P("user", None),
            P("user"),
            P(),
            P(),
            P(),
            P(),
        ),
        out_specs=P(("table", "user"), None),
        check_vma=False,
    )
```

```python
import functools
import math

import jax
import jax.numpy as jnp
from jax import lax
from jax.experimental import pallas as pl
from jax.experimental.pallas import tpu as pltpu
from jax.sharding import PartitionSpec as P

HEADS = 4
PAGE = 128
HALF = PAGE // 2
CAP_PAGES = 6
CHUNKS = (3, 3)
LANES = 128

SCORE_SHARPNESS = 0.02
NORM_EPSILON = 1e-06
LAYER_EPSILON = 1e-05

BF = jnp.bfloat16
F32 = jnp.float32
COPY_PARTS = 8
GRADIENT_PAGES = 3
LAYER_COST = 24
FAR_PAGES = 3
EARLIER = slice(2, 3)
QUERY_PAGES = 3


def params(mebibytes):
    return pltpu.CompilerParams(vmem_limit_bytes=mebibytes * 1024 * 1024)


def run(kernel, operands, in_specs, out_shape, scratch, mebibytes, name, after=(), flops=0):
    count = len(operands)

    def body(*refs):
        kernel(*refs[:count], *refs[count + len(after) :])

    return pl.pallas_call(
        body,
        out_shape=out_shape,
        in_specs=in_specs + [anywhere()] * len(after),
        out_specs=[vmem()] * len(out_shape),
        scratch_shapes=scratch,
        compiler_params=params(mebibytes),
        name=name,
        cost_estimate=pl.CostEstimate(flops=flops, transcendentals=0, bytes_accessed=flops // 300),
    )(*operands, *after)


def stay(array):
    return pltpu.with_memory_space_constraint(array, pltpu.HBM)


def smem():
    return pl.BlockSpec(memory_space=pltpu.SMEM)


def vmem():
    return pl.BlockSpec(memory_space=pltpu.VMEM)


def hbm():
    return pl.BlockSpec(memory_space=pltpu.HBM)


def anywhere():
    return pl.BlockSpec(memory_space=pl.ANY)


def silu(v):
    return v * (0.5 + 0.5 * jnp.tanh(0.5 * v))


def swap_halves(v):
    width = v.shape[1] // 2
    if v.shape[1] == LANES:
        return pltpu.roll(v, width, 1)
    return jnp.concatenate([v[:, width:], v[:, :width]], axis=1)


def place_columns(ref, spare_ref, blocks, chips):
    width = blocks[0].shape[1]
    for s, block in enumerate(blocks):
        chip = source_chip(s, chips)
        if width == LANES:
            ref[:, pl.ds(pl.multiple_of(chip * width, width), width)] = block
        else:
            spare_ref[chip] = block
    if width != LANES:
        ref[...] = jnp.concatenate([spare_ref[chip] for chip in range(chips)], axis=1)


def spare_blocks(chips, rows, width):
    return pltpu.VMEM((chips, rows, width) if width != LANES else (1, 16, LANES), BF)


def lane_ids(shape):
    return lax.broadcasted_iota(jnp.int32, shape, len(shape) - 1)


def turn_table(table_ref, part_ref, rows_ref, sem):
    middle = table_ref.shape[1] // 2
    piece = middle // COPY_PARTS

    def copy(side, i):
        at = pl.ds(side * middle + i * piece, piece)
        return pltpu.make_async_copy(table_ref.at[:, at], part_ref.at[:, at], sem.at[side, i])

    for i in range(COPY_PARTS):
        copy(0, i).start()
        copy(1, i).start()
    for i in range(COPY_PARTS):
        copy(0, i).wait()
        copy(1, i).wait()

        def turn(j, carry):
            at = pl.multiple_of(i * piece + j * LANES, LANES)
            low = part_ref[:, pl.ds(at, LANES)]
            high = part_ref[:, pl.ds(middle + at, LANES)]
            rows_ref[pl.ds(at, LANES), :] = jnp.concatenate([low, high], axis=0).T.astype(F32)
            rows_ref[pl.ds(middle + at, LANES), :] = jnp.concatenate([high, low], axis=0).T.astype(
                F32
            )
            return carry

        lax.fori_loop(0, piece // LANES, turn, 0, unroll=16)


def gather_kernel(tables, start, size, negatives, *refs):
    ids_in, len_in, own_in = refs[:3]
    if negatives:
        neg_in, table_ref, rows_ref, keep_ref, give_ref = refs[3:8]
    else:
        rows_ref, keep_ref, give_ref, second_ref = refs[3:7]
    ids_ref, len_ref, own_ref, neg_ref, stage_ref, next_ref, small_sem = refs[-7:]
    smalls = [(ids_in, ids_ref), (len_in, len_ref), (own_in, own_ref)]
    if negatives:
        smalls.append((neg_in, neg_ref))
    copies = [pltpu.make_async_copy(a, b, small_sem.at[i]) for i, (a, b) in enumerate(smalls)]
    for c in copies:
        c.start()
    if negatives:
        turn_table(table_ref, refs[-9], rows_ref, refs[-8])
    for c in copies:
        c.wait()
    me = lax.axis_index("table")
    core = me % 2
    chip = me // 2
    chips = tables // 2
    vocab, lanes = rows_ref.shape
    middle = vocab // 2
    first_xor = core * middle
    second_xor = middle - first_xor
    own_lanes = (lane_ids((1, lanes)) < lanes // 2) == (core == 0)

    def fetch(source, base, half):
        def step(j, carry):
            at = pl.multiple_of(j * 8, 8)
            for k in range(8):
                first = source[base + at + k] ^ first_xor
                second = source[base + half + at + k] ^ second_xor
                picked = jnp.where(
                    own_lanes, rows_ref[pl.ds(first, 1), :], rows_ref[pl.ds(second, 1), :]
                )
                stage_ref[pl.ds(at + k, 1), :] = picked
            return carry

        lax.fori_loop(0, half // 8, step, 0, unroll=8)
        return stage_ref[0:half, :].astype(BF)

    if negatives:
        neg_rows = neg_ref.shape[0] // 2
        neg_half = neg_rows // 2
        neg_at = chips * size * HALF
        keep_ref[neg_at : neg_at + neg_half, :] = fetch(neg_ref, core * neg_rows, neg_half)
        give_ref[neg_at : neg_at + neg_half, :] = fetch(neg_ref, (1 - core) * neg_rows, neg_half)

    for t in range(tables):
        next_ref[t] = 0

    def sequence(i, page):
        owner = own_ref[0, i]
        pages = len_ref[0, i] // PAGE
        slot0 = next_ref[owner]
        next_ref[owner] = slot0 + pages
        shift = lax.rem(owner // 2 - chip + chips, chips)
        mine = owner % 2 == core

        def one_page(slot, carry):
            block = fetch(ids_ref, (page + slot - slot0) * PAGE, HALF)
            at = pl.multiple_of((shift * size + slot - start) * HALF, HALF)

            @pl.when(mine)
            def _():
                keep_ref[pl.ds(at, HALF), :] = block

            if negatives:

                @pl.when(jnp.logical_not(mine))
                def _():
                    give_ref[pl.ds(at, HALF), :] = block

            else:
                late = shift >= chips // 2
                border = chips // 2 * size * HALF

                @pl.when(jnp.logical_not(mine) & jnp.logical_not(late))
                def _():
                    give_ref[pl.ds(at, HALF), :] = block

                @pl.when(jnp.logical_not(mine) & late)
                def _():
                    second_ref[pl.ds(pl.multiple_of(at - border, HALF), HALF), :] = block

            return carry

        low = jnp.maximum(slot0, start)
        high = jnp.minimum(slot0 + pages, start + size)
        lax.fori_loop(low, high, one_page, 0)
        return page + pages

    lax.fori_loop(0, len_ref.shape[1], sequence, 0)


def gather_rows(
    event_ids, seq_lengths, seq_owner, negative_ids, table, rows, tables, start, size, after
):
    chips = tables // 2
    negatives = rows is None
    neg_half = negative_ids.shape[0] // 4
    columns, vocab = table.shape
    lanes = 2 * columns
    block = jax.ShapeDtypeStruct((chips * size * HALF + (neg_half if negatives else 0), lanes), BF)
    operands = [event_ids, seq_lengths, seq_owner]
    in_specs = [hbm()] * 3
    out_shape = [block, block]
    scratch = [
        pltpu.SMEM(event_ids.shape, jnp.int32),
        pltpu.SMEM(seq_lengths.shape, jnp.int32),
        pltpu.SMEM(seq_owner.shape, jnp.int32),
        pltpu.SMEM(negative_ids.shape, jnp.int32),
        pltpu.VMEM((max(HALF, neg_half), lanes), F32),
        pltpu.SMEM((tables,), jnp.int32),
        pltpu.SemaphoreType.DMA((4,)),
    ]
    if negatives:
        operands += [negative_ids, table]
        in_specs += [hbm(), hbm()]
        out_shape = [jax.ShapeDtypeStruct((vocab, lanes), F32)] + out_shape
        scratch = [
            pltpu.VMEM((columns, vocab), BF),
            pltpu.SemaphoreType.DMA((2, COPY_PARTS)),
        ] + scratch
    else:
        part = jax.ShapeDtypeStruct((chips // 2 * size * HALF, lanes), BF)
        out_shape = [block, part, part]
        operands.append(rows)
        in_specs.append(vmem())
    kernel = functools.partial(gather_kernel, tables, start, size, negatives)
    return run(kernel, operands, in_specs, out_shape, scratch, 28, "gather_rows", after)


def merge_kernel(chips, pages, neg_half, keep_ref, *refs):
    got_refs, out_refs = refs[:-chips], refs[-chips:]
    core = lax.axis_index("table") % 2
    width = keep_ref.shape[1] // 2
    own_lanes = (lane_ids((1, 2 * width)) < width) == (core == 0)

    def merged(at, half):
        own = keep_ref[at : at + half, :].astype(F32)
        got_ref, low_at = got_refs[0], at
        if len(got_refs) > 1 and at >= got_ref.shape[0]:
            got_ref, low_at = got_refs[1], at - got_ref.shape[0]
        other = got_ref[low_at : low_at + half, :].astype(F32)
        top = jnp.where(own_lanes, own, other)
        low = swap_halves(jnp.where(own_lanes, other, own))
        return top.astype(BF), low.astype(BF)

    if neg_half:
        top, low = merged(chips * pages * HALF, neg_half)
        at = pages * PAGE
        for s in range(chips):
            out_refs[s][at : at + neg_half, :] = top
            out_refs[s][at + neg_half : at + 2 * neg_half, :] = low
    for s in range(chips):
        for k in range(pages):
            top, low = merged((s * pages + k) * HALF, HALF)
            out_refs[s][k * PAGE : k * PAGE + HALF, :] = top
            out_refs[s][k * PAGE + HALF : (k + 1) * PAGE, :] = low


def merge_columns(keep, got, chips, pages, neg_half, after):
    shape = jax.ShapeDtypeStruct((pages * PAGE + 2 * neg_half, keep.shape[1]), BF)
    kernel = functools.partial(merge_kernel, chips, pages, neg_half)
    specs = [vmem()] * (1 + len(got))
    return run(kernel, [keep, *got], specs, [shape] * chips, [], 12, "merge_columns", after)


def source_chip(s, chips):
    chip = lax.axis_index("table") // 2
    return lax.rem(chip - s + chips, chips)


def unit_negatives_kernel(chips, neg_rows, *refs):
    block_refs, out_ref, spare_ref = refs[:chips], refs[chips], refs[chips + 1]
    blocks = [ref[ref.shape[0] - neg_rows :, :].astype(F32) for ref in block_refs]
    squares = sum(jnp.sum(b * b, axis=1, keepdims=True) for b in blocks)
    scale = lax.rsqrt(squares + NORM_EPSILON)
    place_columns(out_ref, spare_ref, [(b * scale).astype(BF) for b in blocks], chips)


def unit_negatives(blocks, neg_rows, after):
    chips = len(blocks)
    lanes = blocks[0].shape[1]
    return run(
        functools.partial(unit_negatives_kernel, chips, neg_rows),
        blocks,
        [vmem()] * chips,
        [jax.ShapeDtypeStruct((neg_rows, chips * lanes), BF)],
        [spare_blocks(chips, neg_rows, lanes)],
        8,
        "unit_negatives",
        after,
    )[0]


def own_plan(len_ref, own_ref):
    me = lax.axis_index("table")
    segment = [jnp.int32(-1)] * CAP_PAGES
    length = [jnp.int32(1)] * CAP_PAGES
    start = jnp.int32(0)
    for i in range(len_ref.shape[1]):
        size = len_ref[0, i]
        mine = own_ref[0, i] == me
        end = jnp.where(mine, start + size // PAGE, start)
        for p in range(CAP_PAGES):
            inside = (start <= p) & (p < end)
            segment[p] = jnp.where(inside, i, segment[p])
            length[p] = jnp.where(inside, size, length[p])
        start = end
    return segment, length


def layer_kernel(chips, first, pages, last, *refs):
    len_ref, own_ref = refs[:2]
    block_refs = refs[2 : 2 + chips]
    refs = refs[2 + chips :]
    w_in, w_mid, w_uvqk, w_proj = refs[:4]
    refs = refs[4:]
    if first:
        prior_ref, refs = refs[0], refs[1:]
    unit_ref, item_ref = refs[:2]
    refs = refs[2:]
    if not last:
        kv_out, refs = refs[0], refs[1:]
    x_ref, proj_ref, att_ref, spare_ref = refs
    width = w_in.shape[0]
    segment, length = own_plan(len_ref, own_ref)
    place_columns(x_ref, spare_ref, [ref[0 : pages * PAGE, :] for ref in block_refs], chips)
    for p in range(pages):
        part = slice(p * PAGE, (p + 1) * PAGE)
        page_x = x_ref[part, :]
        page_x = jnp.where(segment[first + p] >= 0, page_x, jnp.zeros_like(page_x))
        x_ref[part, :] = page_x
        x32 = page_x.astype(F32)
        item_ref[part, :] = (
            x32 * lax.rsqrt(jnp.sum(x32 * x32, axis=1, keepdims=True) + NORM_EPSILON)
        ).astype(BF)

    x = x_ref[...]
    hidden_width = w_in.shape[1]
    step = 1024
    mixed = None
    for f in range(0, hidden_width, step):
        hidden = silu(
            jnp.dot(x, w_in[:, f : f + step], preferred_element_type=F32)
        ).astype(BF)
        part = jnp.dot(hidden, w_mid[f : f + step, :], preferred_element_type=F32)
        mixed = part if mixed is None else mixed + part
    mixed = mixed.astype(BF)
    for f in range(0, 4 * width, step):
        proj_ref[:, f : f + step] = silu(
            jnp.dot(mixed, w_uvqk[:, f : f + step], preferred_element_type=F32)
        ).astype(BF)
    if not last:
        kv_out[:, :width] = proj_ref[:, width : 2 * width]
        kv_out[:, width:] = proj_ref[:, 3 * width :]

    head_width = width // HEADS
    scale = 1.0 / math.sqrt(head_width)
    row_at = lax.broadcasted_iota(jnp.int32, (PAGE, PAGE), 0)
    causal = lane_ids((PAGE, PAGE)) <= row_at
    inverses = [
        jnp.where(
            segment[p] >= 0, 1.0 / jnp.full((1, PAGE), length[p], jnp.int32).astype(F32), 0.0
        )
        for p in range(first + pages)
    ]
    for group in range(0, pages, QUERY_PAGES):
        inside = range(group, min(group + QUERY_PAGES, pages))
        part = slice(group * PAGE, (inside[-1] + 1) * PAGE)
        upto = (inside[-1] + 1) * PAGE
        for h in range(HEADS):
            low = h * head_width
            query = proj_ref[part, 2 * width + low : 2 * width + low + head_width]
            keys = proj_ref[0:upto, 3 * width + low : 3 * width + low + head_width]
            values = proj_ref[0:upto, width + low : width + low + head_width]
            if first:
                keys = jnp.concatenate(
                    [prior_ref[:, width + low : width + low + head_width], keys], axis=0
                )
                values = jnp.concatenate([prior_ref[:, low : low + head_width], values], axis=0)
            scores = lax.dot_general(
                query, keys, (((1,), (1,)), ((), ())), preferred_element_type=F32
            )
            rows = []
            for i, p in enumerate(inside):
                whole = first + p
                row = []
                for c in range(first + inside[-1] + 1):
                    if c > whole:
                        row.append(jnp.zeros((PAGE, PAGE), BF))
                        continue
                    score = silu(
                        scores[i * PAGE : (i + 1) * PAGE, c * PAGE : (c + 1) * PAGE] * scale
                    )
                    if c < whole:
                        factor = jnp.where(segment[c] == segment[whole], inverses[whole], 0.0)
                        row.append((score * factor).astype(BF))
                    else:
                        row.append(jnp.where(causal, score * inverses[whole], 0.0).astype(BF))
                rows.append(row[0] if len(row) == 1 else jnp.concatenate(row, axis=1))
            weights = rows[0] if len(rows) == 1 else jnp.concatenate(rows, axis=0)
            att_ref[part, low : low + head_width] = jnp.dot(
                weights, values, preferred_element_type=F32
            )
    attended = att_ref[...]
    centered = attended - jnp.mean(attended, axis=1, keepdims=True)
    variance = jnp.mean(centered * centered, axis=1, keepdims=True)
    gated = (
        centered * lax.rsqrt(variance + LAYER_EPSILON) * proj_ref[:, :width].astype(F32)
    ).astype(BF)
    state = mixed.astype(F32) + jnp.dot(gated, w_proj[...], preferred_element_type=F32)
    unit_ref[...] = (
        state * lax.rsqrt(jnp.sum(state * state, axis=1, keepdims=True) + NORM_EPSILON)
    ).astype(BF)


def layer(seq_lengths, seq_owner, blocks, weights, prior, first, pages, last, after):
    chips = len(blocks)
    lanes = blocks[0].shape[1]
    width = chips * lanes
    rows = pages * PAGE
    wide = 4 * width
    operands = [seq_lengths, seq_owner, *blocks, *weights]
    in_specs = [smem(), smem()] + [vmem()] * (chips + 4)
    if first:
        operands.append(prior)
        in_specs.append(vmem())
    out_shape = [jax.ShapeDtypeStruct((rows, width), BF)] * 2
    if not last:
        out_shape.append(jax.ShapeDtypeStruct((first * PAGE + rows, 2 * width), BF))
    scratch = [
        pltpu.VMEM((rows, width), BF),
        pltpu.VMEM((rows, wide), BF),
        pltpu.VMEM((rows, width), F32),
        spare_blocks(chips, rows, lanes),
    ]
    kernel = functools.partial(layer_kernel, chips, first, pages, last)
    return run(kernel, operands, in_specs, out_shape, scratch, 28, "layer", after, LAYER_COST * rows * width * width)


def join_kernel(*refs):
    rows = refs[0].shape[0]
    for i, ref in enumerate(refs[:-1]):
        refs[-1][i * rows : (i + 1) * rows, :] = ref[...]


def join(parts, after):
    rows, width = parts[0].shape
    shape = [jax.ShapeDtypeStruct((len(parts) * rows, width), BF)]
    return run(join_kernel, parts, [vmem()] * len(parts), shape, [], 8, "join", after)[0]


def score_part(unit, negatives):
    scores = lax.dot_general(
        unit, negatives, (((1,), (1,)), ((), ())), preferred_element_type=F32
    )
    powers = jnp.exp(scores * (1.0 / SCORE_SHARPNESS))
    total = jnp.sum(powers, axis=1, keepdims=True)
    return total, jnp.dot(powers.astype(BF), negatives, preferred_element_type=F32)


def row_blocks(refs, pages):
    at = 0
    for ref in refs:
        size = pages * PAGE
        for low in range(0, ref.shape[0], size):
            block = min(size, ref.shape[0] - low)
            yield ref, low, at, block
            at += block


def next_limits(segment, first, pages):
    row_at = lax.broadcasted_iota(jnp.int32, (PAGE, 1), 0)
    limits = []
    for page in range(first, first + pages):
        last_row = jnp.where(segment[page + 1] == segment[page], PAGE, PAGE - 1)
        limit = jnp.where(segment[page] >= 0, last_row, 0)
        limits.append((row_at < limit).astype(F32))
    return (limits[0] if pages == 1 else jnp.concatenate(limits, axis=0)) > 0.5


def near_kernel(count, *refs):
    len_ref, own_ref, near_ref = refs[:3]
    unit_refs = refs[3 : 3 + count]
    item_refs = refs[3 + count : 3 + 2 * count]
    sum_ref, total_ref, positive_ref, target_ref, next_ref = refs[3 + 2 * count :]
    negatives = near_ref[...]
    at = 0
    for item in item_refs:
        size = item.shape[0]
        next_ref[at : at + size, :] = item[...].astype(F32)
        at += size
    next_ref[at:, :] = jnp.zeros_like(next_ref[at:, :])
    segment, _ = own_plan(len_ref, own_ref)
    segment = segment + [jnp.int32(-1)]
    sharp = 1.0 / SCORE_SHARPNESS
    for ref, low, at, block in row_blocks(unit_refs, GRADIENT_PAGES):
        unit = ref[low : low + block, :]
        has_next = next_limits(segment, at // PAGE, block // PAGE)
        targets = jnp.where(has_next, next_ref[at + 1 : at + 1 + block, :], 0.0)
        target_ref[at : at + block, :] = targets.astype(BF)
        positive = jnp.exp(jnp.sum(unit.astype(F32) * targets, axis=1, keepdims=True) * sharp)
        total, part = score_part(unit, negatives)
        sum_ref[at : at + block, :] = part
        total_ref[at : at + block, :] = total + positive
        positive_ref[at : at + block, :] = jnp.where(has_next, positive, -1.0)


def near_gradient(seq_lengths, seq_owner, near, units, items):
    rows = sum(u.shape[0] for u in units)
    width = near.shape[1]
    shapes = [
        jax.ShapeDtypeStruct((rows, width), F32),
        jax.ShapeDtypeStruct((rows, 1), F32),
        jax.ShapeDtypeStruct((rows, 1), F32),
        jax.ShapeDtypeStruct((rows, width), BF),
    ]
    return run(
        functools.partial(near_kernel, len(units)),
        [seq_lengths, seq_owner, near, *units, *items],
        [smem(), smem()] + [vmem()] * (1 + 2 * len(units)),
        shapes,
        [pltpu.VMEM((rows + 8, width), F32)],
        20,
        "near_gradient",
        (),
        LAYER_COST * rows * width * width // 4,
    )


def far_kernel(count, *refs):
    far_ref, sum_ref, total_ref, positive_ref, target_ref = refs[:5]
    unit_refs = refs[5 : 5 + count]
    out_ref, stage_ref, sem = refs[5 + count :]
    negatives = far_ref[...]
    sharp = 1.0 / SCORE_SHARPNESS
    copies = []
    for ref, low, at, block in row_blocks(unit_refs, FAR_PAGES):
        part_rows = slice(at, at + block)
        total, part = score_part(ref[low : low + block, :], negatives)
        positive = positive_ref[part_rows, :]
        inverse = 1.0 / (total + total_ref[part_rows, :])
        grad = (part + sum_ref[part_rows, :]) * inverse
        targets = target_ref[part_rows, :].astype(F32)
        grad = (grad + (positive * inverse - 1.0) * targets) * sharp
        stage_ref[part_rows, :] = jnp.where(positive >= 0.0, grad, 0.0)
        rows = pl.ds(at, block)
        copies.append(
            pltpu.make_async_copy(stage_ref.at[rows, :], out_ref.at[rows, :], sem.at[len(copies)])
        )
        copies[-1].start()
    for copy in copies:
        copy.wait()


def far_gradient(far, sums, totals, positives, targets, units):
    rows, width = sums.shape
    return pl.pallas_call(
        functools.partial(far_kernel, len(units)),
        out_shape=jax.ShapeDtypeStruct((rows, width), F32),
        in_specs=[vmem()] * (5 + len(units)),
        out_specs=hbm(),
        scratch_shapes=[
            pltpu.VMEM((rows, width), F32),
            pltpu.SemaphoreType.DMA((rows // PAGE,)),
        ],
        compiler_params=params(20),
        name="far_gradient",
    )(far, sums, totals, positives, targets, *units)


def on_device(
    item_table, event_ids, seq_lengths, seq_owner, negative_ids, w_in, w_mid, w_uvqk, w_proj
):
    tables = lax.axis_size("table")
    users = lax.axis_size("user")
    chips = tables // 2
    neg_half = negative_ids.shape[0] // 4
    cores = [(t, t ^ 1) for t in range(tables)]
    table = stay(item_table.T)
    event_ids, negative_ids = stay(event_ids), stay(negative_ids)
    lengths, owners = stay(seq_lengths), stay(seq_owner)
    rows, first = None, 0
    arrived, after, gate = [], [], []
    for c, size in enumerate(CHUNKS):
        outs = gather_rows(
            event_ids, lengths, owners, negative_ids, table, rows, tables, first, size, after
        )
        if rows is None:
            rows = outs[0]
        keep, *gives = outs[1:] if c == 0 else outs
        got = [lax.ppermute(give, "table", cores) for give in gives]
        blocks = list(merge_columns(keep, got, chips, size, neg_half if c == 0 else 0, gate))
        after = blocks[:1]
        for s in range(1, chips):
            moves = [(t, (t // 2 + s) % chips * 2 + t % 2) for t in range(tables)]
            blocks[s] = lax.ppermute(blocks[s], "table", moves)
        gate = blocks[EARLIER]
        arrived.append(blocks)
        first += size
    arrived.append(())

    weights = (w_in, w_mid, w_uvqk, w_proj)
    units, items = [], []
    prior, first = None, 0
    for c, size in enumerate(CHUNKS):
        last = c == len(CHUNKS) - 1
        after = list(arrived[c + 1][:1])
        outs = layer(seq_lengths, seq_owner, arrived[c], weights, prior, first, size, last, after)
        units.append(outs[0])
        items.append(outs[1])
        if not last:
            prior = outs[2]
        if c == 0:
            own = unit_negatives(arrived[0], 2 * neg_half, units)
            parts = [own]
            for s in range(1, users):
                parts.append(lax.ppermute(own, "user", [(u, u ^ s) for u in range(users)]))
        first += size
    near = join(parts, units[1:])
    far = lax.ppermute(near, "table", cores)
    parts = near_gradient(seq_lengths, seq_owner, near, units, items)
    return far_gradient(far, *parts, units)


def solution(mesh):
    return jax.shard_map(
        on_device,
        mesh=mesh,
        in_specs=(
            P(None, "table"),
            P("user"),
            P("user", None),
            P("user", None),
            P("user"),
            P(),
            P(),
            P(),
            P(),
        ),
        out_specs=P(("table", "user"), None),
        check_vma=False,
    )
```

```python
import functools
import math

import jax
import jax.numpy as jnp
from jax import lax
from jax.experimental import pallas as pl
from jax.experimental.pallas import tpu as pltpu
from jax.sharding import PartitionSpec as P

HEADS = 4
PAGE = 128
HALF = PAGE // 2
CAP_PAGES = 6
CHUNKS = (3, 3)
LANES = 128

SCORE_SHARPNESS = 0.02
NORM_EPSILON = 1e-06
LAYER_EPSILON = 1e-05

BF = jnp.bfloat16
F32 = jnp.float32
COPY_PARTS = 4
GRADIENT_PAGES = 3
LAYER_COST = 24
FAR_PAGES = 3
EARLIER = slice(2, 3)
QUERY_PAGES = 3


def params(mebibytes):
    return pltpu.CompilerParams(vmem_limit_bytes=mebibytes * 1024 * 1024)


def run(kernel, operands, in_specs, out_shape, scratch, mebibytes, name, after=(), flops=0):
    count = len(operands)

    def body(*refs):
        kernel(*refs[:count], *refs[count + len(after) :])

    return pl.pallas_call(
        body,
        out_shape=out_shape,
        in_specs=in_specs + [anywhere()] * len(after),
        out_specs=[vmem()] * len(out_shape),
        scratch_shapes=scratch,
        compiler_params=params(mebibytes),
        name=name,
        cost_estimate=pl.CostEstimate(flops=flops, transcendentals=0, bytes_accessed=flops // 300),
    )(*operands, *after)


def stay(array):
    return pltpu.with_memory_space_constraint(array, pltpu.HBM)


def smem():
    return pl.BlockSpec(memory_space=pltpu.SMEM)


def vmem():
    return pl.BlockSpec(memory_space=pltpu.VMEM)


def hbm():
    return pl.BlockSpec(memory_space=pltpu.HBM)


def anywhere():
    return pl.BlockSpec(memory_space=pl.ANY)


def silu(v):
    return v * (0.5 + 0.5 * jnp.tanh(0.5 * v))


def swap_halves(v):
    width = v.shape[1] // 2
    if v.shape[1] == LANES:
        return pltpu.roll(v, width, 1)
    return jnp.concatenate([v[:, width:], v[:, :width]], axis=1)


def place_columns(ref, spare_ref, blocks, chips):
    width = blocks[0].shape[1]
    for s, block in enumerate(blocks):
        chip = source_chip(s, chips)
        if width == LANES:
            ref[:, pl.ds(pl.multiple_of(chip * width, width), width)] = block
        else:
            spare_ref[chip] = block
    if width != LANES:
        ref[...] = jnp.concatenate([spare_ref[chip] for chip in range(chips)], axis=1)


def spare_blocks(chips, rows, width):
    return pltpu.VMEM((chips, rows, width) if width != LANES else (1, 16, LANES), BF)


def lane_ids(shape):
    return lax.broadcasted_iota(jnp.int32, shape, len(shape) - 1)


def turn_table(table_ref, part_ref, rows_ref, sem):
    middle = table_ref.shape[1] // 2
    piece = middle // COPY_PARTS

    def copy(side, i):
        at = pl.ds(side * middle + i * piece, piece)
        return pltpu.make_async_copy(table_ref.at[:, at], part_ref.at[:, at], sem.at[side, i])

    for i in range(COPY_PARTS):
        copy(0, i).start()
        copy(1, i).start()
    for i in range(COPY_PARTS):
        copy(0, i).wait()
        copy(1, i).wait()

        def turn(j, carry):
            at = pl.multiple_of(i * piece + j * LANES, LANES)
            low = part_ref[:, pl.ds(at, LANES)]
            high = part_ref[:, pl.ds(middle + at, LANES)]
            rows_ref[pl.ds(at, LANES), :] = jnp.concatenate([low, high], axis=0).T.astype(F32)
            rows_ref[pl.ds(middle + at, LANES), :] = jnp.concatenate([high, low], axis=0).T.astype(
                F32
            )
            return carry

        lax.fori_loop(0, piece // LANES, turn, 0, unroll=32)


def gather_kernel(tables, start, size, negatives, *refs):
    ids_in, len_in, own_in = refs[:3]
    if negatives:
        neg_in, table_ref, rows_ref, keep_ref, give_ref = refs[3:8]
    else:
        rows_ref, keep_ref, give_ref, second_ref = refs[3:7]
    ids_ref, len_ref, own_ref, neg_ref, stage_ref, next_ref, small_sem = refs[-7:]
    smalls = [(ids_in, ids_ref), (len_in, len_ref), (own_in, own_ref)]
    if negatives:
        smalls.append((neg_in, neg_ref))
    copies = [pltpu.make_async_copy(a, b, small_sem.at[i]) for i, (a, b) in enumerate(smalls)]
    for c in copies:
        c.start()
    if negatives:
        turn_table(table_ref, refs[-9], rows_ref, refs[-8])
    for c in copies:
        c.wait()
    me = lax.axis_index("table")
    core = me % 2
    chip = me // 2
    chips = tables // 2
    vocab, lanes = rows_ref.shape
    middle = vocab // 2
    first_xor = core * middle
    second_xor = middle - first_xor
    own_lanes = (lane_ids((1, lanes)) < lanes // 2) == (core == 0)

    def fetch(source, base, half):
        def step(j, carry):
            at = pl.multiple_of(j * 8, 8)
            for k in range(8):
                first = source[base + at + k] ^ first_xor
                second = source[base + half + at + k] ^ second_xor
                picked = jnp.where(
                    own_lanes, rows_ref[pl.ds(first, 1), :], rows_ref[pl.ds(second, 1), :]
                )
                stage_ref[pl.ds(at + k, 1), :] = picked
            return carry

        lax.fori_loop(0, half // 8, step, 0, unroll=8)
        return stage_ref[0:half, :].astype(BF)

    if negatives:
        neg_rows = neg_ref.shape[0] // 2
        neg_half = neg_rows // 2
        neg_at = chips * size * HALF
        keep_ref[neg_at : neg_at + neg_half, :] = fetch(neg_ref, core * neg_rows, neg_half)
        give_ref[neg_at : neg_at + neg_half, :] = fetch(neg_ref, (1 - core) * neg_rows, neg_half)

    for t in range(tables):
        next_ref[t] = 0

    def sequence(i, page):
        owner = own_ref[0, i]
        pages = len_ref[0, i] // PAGE
        slot0 = next_ref[owner]
        next_ref[owner] = slot0 + pages
        shift = lax.rem(owner // 2 - chip + chips, chips)
        mine = owner % 2 == core

        def one_page(slot, carry):
            block = fetch(ids_ref, (page + slot - slot0) * PAGE, HALF)
            at = pl.multiple_of((shift * size + slot - start) * HALF, HALF)

            @pl.when(mine)
            def _():
                keep_ref[pl.ds(at, HALF), :] = block

            if negatives:

                @pl.when(jnp.logical_not(mine))
                def _():
                    give_ref[pl.ds(at, HALF), :] = block

            else:
                late = shift >= chips // 2
                border = chips // 2 * size * HALF

                @pl.when(jnp.logical_not(mine) & jnp.logical_not(late))
                def _():
                    give_ref[pl.ds(at, HALF), :] = block

                @pl.when(jnp.logical_not(mine) & late)
                def _():
                    second_ref[pl.ds(pl.multiple_of(at - border, HALF), HALF), :] = block

            return carry

        low = jnp.maximum(slot0, start)
        high = jnp.minimum(slot0 + pages, start + size)
        lax.fori_loop(low, high, one_page, 0)
        return page + pages

    lax.fori_loop(0, len_ref.shape[1], sequence, 0)


def gather_rows(
    event_ids, seq_lengths, seq_owner, negative_ids, table, rows, tables, start, size, after
):
    chips = tables // 2
    negatives = rows is None
    neg_half = negative_ids.shape[0] // 4
    columns, vocab = table.shape
    lanes = 2 * columns
    block = jax.ShapeDtypeStruct((chips * size * HALF + (neg_half if negatives else 0), lanes), BF)
    operands = [event_ids, seq_lengths, seq_owner]
    in_specs = [hbm()] * 3
    out_shape = [block, block]
    scratch = [
        pltpu.SMEM(event_ids.shape, jnp.int32),
        pltpu.SMEM(seq_lengths.shape, jnp.int32),
        pltpu.SMEM(seq_owner.shape, jnp.int32),
        pltpu.SMEM(negative_ids.shape, jnp.int32),
        pltpu.VMEM((max(HALF, neg_half), lanes), F32),
        pltpu.SMEM((tables,), jnp.int32),
        pltpu.SemaphoreType.DMA((4,)),
    ]
    if negatives:
        operands += [negative_ids, table]
        in_specs += [hbm(), hbm()]
        out_shape = [jax.ShapeDtypeStruct((vocab, lanes), F32)] + out_shape
        scratch = [
            pltpu.VMEM((columns, vocab), BF),
            pltpu.SemaphoreType.DMA((2, COPY_PARTS)),
        ] + scratch
    else:
        part = jax.ShapeDtypeStruct((chips // 2 * size * HALF, lanes), BF)
        out_shape = [block, part, part]
        operands.append(rows)
        in_specs.append(vmem())
    kernel = functools.partial(gather_kernel, tables, start, size, negatives)
    return run(kernel, operands, in_specs, out_shape, scratch, 28, "gather_rows", after)


def merge_kernel(chips, pages, neg_half, keep_ref, *refs):
    got_refs, out_refs = refs[:-chips], refs[-chips:]
    core = lax.axis_index("table") % 2
    width = keep_ref.shape[1] // 2
    own_lanes = (lane_ids((1, 2 * width)) < width) == (core == 0)

    def merged(at, half):
        own = keep_ref[at : at + half, :].astype(F32)
        got_ref, low_at = got_refs[0], at
        if len(got_refs) > 1 and at >= got_ref.shape[0]:
            got_ref, low_at = got_refs[1], at - got_ref.shape[0]
        other = got_ref[low_at : low_at + half, :].astype(F32)
        top = jnp.where(own_lanes, own, other)
        low = swap_halves(jnp.where(own_lanes, other, own))
        return top.astype(BF), low.astype(BF)

    if neg_half:
        top, low = merged(chips * pages * HALF, neg_half)
        at = pages * PAGE
        for s in range(chips):
            out_refs[s][at : at + neg_half, :] = top
            out_refs[s][at + neg_half : at + 2 * neg_half, :] = low
    for s in range(chips):
        for k in range(pages):
            top, low = merged((s * pages + k) * HALF, HALF)
            out_refs[s][k * PAGE : k * PAGE + HALF, :] = top
            out_refs[s][k * PAGE + HALF : (k + 1) * PAGE, :] = low


def merge_columns(keep, got, chips, pages, neg_half, after):
    shape = jax.ShapeDtypeStruct((pages * PAGE + 2 * neg_half, keep.shape[1]), BF)
    kernel = functools.partial(merge_kernel, chips, pages, neg_half)
    specs = [vmem()] * (1 + len(got))
    return run(kernel, [keep, *got], specs, [shape] * chips, [], 12, "merge_columns", after)


def source_chip(s, chips):
    chip = lax.axis_index("table") // 2
    return lax.rem(chip - s + chips, chips)


def unit_negatives_kernel(chips, neg_rows, *refs):
    block_refs, out_ref, spare_ref = refs[:chips], refs[chips], refs[chips + 1]
    blocks = [ref[ref.shape[0] - neg_rows :, :].astype(F32) for ref in block_refs]
    squares = sum(jnp.sum(b * b, axis=1, keepdims=True) for b in blocks)
    scale = lax.rsqrt(squares + NORM_EPSILON)
    place_columns(out_ref, spare_ref, [(b * scale).astype(BF) for b in blocks], chips)


def unit_negatives(blocks, neg_rows, after):
    chips = len(blocks)
    lanes = blocks[0].shape[1]
    return run(
        functools.partial(unit_negatives_kernel, chips, neg_rows),
        blocks,
        [vmem()] * chips,
        [jax.ShapeDtypeStruct((neg_rows, chips * lanes), BF)],
        [spare_blocks(chips, neg_rows, lanes)],
        8,
        "unit_negatives",
        after,
    )[0]


def own_plan(len_ref, own_ref):
    me = lax.axis_index("table")
    segment = [jnp.int32(-1)] * CAP_PAGES
    length = [jnp.int32(1)] * CAP_PAGES
    start = jnp.int32(0)
    for i in range(len_ref.shape[1]):
        size = len_ref[0, i]
        mine = own_ref[0, i] == me
        end = jnp.where(mine, start + size // PAGE, start)
        for p in range(CAP_PAGES):
            inside = (start <= p) & (p < end)
            segment[p] = jnp.where(inside, i, segment[p])
            length[p] = jnp.where(inside, size, length[p])
        start = end
    return segment, length


def layer_kernel(chips, first, pages, last, *refs):
    len_ref, own_ref = refs[:2]
    block_refs = refs[2 : 2 + chips]
    refs = refs[2 + chips :]
    w_in, w_mid, w_uvqk, w_proj = refs[:4]
    refs = refs[4:]
    if first:
        prior_ref, refs = refs[0], refs[1:]
    unit_ref, item_ref = refs[:2]
    refs = refs[2:]
    if not last:
        kv_out, refs = refs[0], refs[1:]
    x_ref, proj_ref, att_ref, spare_ref = refs
    width = w_in.shape[0]
    segment, length = own_plan(len_ref, own_ref)
    place_columns(x_ref, spare_ref, [ref[0 : pages * PAGE, :] for ref in block_refs], chips)
    for p in range(pages):
        part = slice(p * PAGE, (p + 1) * PAGE)
        page_x = x_ref[part, :]
        page_x = jnp.where(segment[first + p] >= 0, page_x, jnp.zeros_like(page_x))
        x_ref[part, :] = page_x
        x32 = page_x.astype(F32)
        item_ref[part, :] = (
            x32 * lax.rsqrt(jnp.sum(x32 * x32, axis=1, keepdims=True) + NORM_EPSILON)
        ).astype(BF)

    x = x_ref[...]
    hidden_width = w_in.shape[1]
    step = 1024
    mixed = None
    for f in range(0, hidden_width, step):
        hidden = silu(
            jnp.dot(x, w_in[:, f : f + step], preferred_element_type=F32)
        ).astype(BF)
        part = jnp.dot(hidden, w_mid[f : f + step, :], preferred_element_type=F32)
        mixed = part if mixed is None else mixed + part
    mixed = mixed.astype(BF)
    for f in range(0, 4 * width, step):
        proj_ref[:, f : f + step] = silu(
            jnp.dot(mixed, w_uvqk[:, f : f + step], preferred_element_type=F32)
        ).astype(BF)
    if not last:
        kv_out[:, :width] = proj_ref[:, width : 2 * width]
        kv_out[:, width:] = proj_ref[:, 3 * width :]

    head_width = width // HEADS
    scale = 1.0 / math.sqrt(head_width)
    row_at = lax.broadcasted_iota(jnp.int32, (PAGE, PAGE), 0)
    causal = lane_ids((PAGE, PAGE)) <= row_at
    inverses = [
        jnp.where(
            segment[p] >= 0, 1.0 / jnp.full((1, PAGE), length[p], jnp.int32).astype(F32), 0.0
        )
        for p in range(first + pages)
    ]
    for group in range(0, pages, QUERY_PAGES):
        inside = range(group, min(group + QUERY_PAGES, pages))
        part = slice(group * PAGE, (inside[-1] + 1) * PAGE)
        upto = (inside[-1] + 1) * PAGE
        for h in range(HEADS):
            low = h * head_width
            query = proj_ref[part, 2 * width + low : 2 * width + low + head_width]
            keys = proj_ref[0:upto, 3 * width + low : 3 * width + low + head_width]
            values = proj_ref[0:upto, width + low : width + low + head_width]
            if first:
                keys = jnp.concatenate(
                    [prior_ref[:, width + low : width + low + head_width], keys], axis=0
                )
                values = jnp.concatenate([prior_ref[:, low : low + head_width], values], axis=0)
            scores = lax.dot_general(
                query, keys, (((1,), (1,)), ((), ())), preferred_element_type=F32
            )
            rows = []
            for i, p in enumerate(inside):
                whole = first + p
                row = []
                for c in range(first + inside[-1] + 1):
                    if c > whole:
                        row.append(jnp.zeros((PAGE, PAGE), BF))
                        continue
                    score = silu(
                        scores[i * PAGE : (i + 1) * PAGE, c * PAGE : (c + 1) * PAGE] * scale
                    )
                    if c < whole:
                        factor = jnp.where(segment[c] == segment[whole], inverses[whole], 0.0)
                        row.append((score * factor).astype(BF))
                    else:
                        row.append(jnp.where(causal, score * inverses[whole], 0.0).astype(BF))
                rows.append(row[0] if len(row) == 1 else jnp.concatenate(row, axis=1))
            weights = rows[0] if len(rows) == 1 else jnp.concatenate(rows, axis=0)
            att_ref[part, low : low + head_width] = jnp.dot(
                weights, values, preferred_element_type=F32
            )
    attended = att_ref[...]
    centered = attended - jnp.mean(attended, axis=1, keepdims=True)
    variance = jnp.mean(centered * centered, axis=1, keepdims=True)
    gated = (
        centered * lax.rsqrt(variance + LAYER_EPSILON) * proj_ref[:, :width].astype(F32)
    ).astype(BF)
    state = mixed.astype(F32) + jnp.dot(gated, w_proj[...], preferred_element_type=F32)
    unit_ref[...] = (
        state * lax.rsqrt(jnp.sum(state * state, axis=1, keepdims=True) + NORM_EPSILON)
    ).astype(BF)


def layer(seq_lengths, seq_owner, blocks, weights, prior, first, pages, last, after):
    chips = len(blocks)
    lanes = blocks[0].shape[1]
    width = chips * lanes
    rows = pages * PAGE
    wide = 4 * width
    operands = [seq_lengths, seq_owner, *blocks, *weights]
    in_specs = [smem(), smem()] + [vmem()] * (chips + 4)
    if first:
        operands.append(prior)
        in_specs.append(vmem())
    out_shape = [jax.ShapeDtypeStruct((rows, width), BF)] * 2
    if not last:
        out_shape.append(jax.ShapeDtypeStruct((first * PAGE + rows, 2 * width), BF))
    scratch = [
        pltpu.VMEM((rows, width), BF),
        pltpu.VMEM((rows, wide), BF),
        pltpu.VMEM((rows, width), F32),
        spare_blocks(chips, rows, lanes),
    ]
    kernel = functools.partial(layer_kernel, chips, first, pages, last)
    return run(kernel, operands, in_specs, out_shape, scratch, 28, "layer", after, LAYER_COST * rows * width * width)


def join_kernel(*refs):
    rows = refs[0].shape[0]
    for i, ref in enumerate(refs[:-1]):
        refs[-1][i * rows : (i + 1) * rows, :] = ref[...]


def join(parts, after):
    rows, width = parts[0].shape
    shape = [jax.ShapeDtypeStruct((len(parts) * rows, width), BF)]
    return run(join_kernel, parts, [vmem()] * len(parts), shape, [], 8, "join", after)[0]


def score_part(unit, negatives):
    scores = lax.dot_general(
        unit, negatives, (((1,), (1,)), ((), ())), preferred_element_type=F32
    )
    powers = jnp.exp(scores * (1.0 / SCORE_SHARPNESS))
    total = jnp.sum(powers, axis=1, keepdims=True)
    return total, jnp.dot(powers.astype(BF), negatives, preferred_element_type=F32)


def row_blocks(refs, pages):
    at = 0
    for ref in refs:
        size = pages * PAGE
        for low in range(0, ref.shape[0], size):
            block = min(size, ref.shape[0] - low)
            yield ref, low, at, block
            at += block


def next_limits(segment, first, pages):
    row_at = lax.broadcasted_iota(jnp.int32, (PAGE, 1), 0)
    limits = []
    for page in range(first, first + pages):
        last_row = jnp.where(segment[page + 1] == segment[page], PAGE, PAGE - 1)
        limit = jnp.where(segment[page] >= 0, last_row, 0)
        limits.append((row_at < limit).astype(F32))
    return (limits[0] if pages == 1 else jnp.concatenate(limits, axis=0)) > 0.5


def near_kernel(count, *refs):
    len_ref, own_ref, near_ref = refs[:3]
    unit_refs = refs[3 : 3 + count]
    item_refs = refs[3 + count : 3 + 2 * count]
    sum_ref, total_ref, positive_ref, target_ref, next_ref = refs[3 + 2 * count :]
    negatives = near_ref[...]
    at = 0
    for item in item_refs:
        size = item.shape[0]
        next_ref[at : at + size, :] = item[...].astype(F32)
        at += size
    next_ref[at:, :] = jnp.zeros_like(next_ref[at:, :])
    segment, _ = own_plan(len_ref, own_ref)
    segment = segment + [jnp.int32(-1)]
    sharp = 1.0 / SCORE_SHARPNESS
    for ref, low, at, block in row_blocks(unit_refs, GRADIENT_PAGES):
        unit = ref[low : low + block, :]
        has_next = next_limits(segment, at // PAGE, block // PAGE)
        targets = jnp.where(has_next, next_ref[at + 1 : at + 1 + block, :], 0.0)
        target_ref[at : at + block, :] = targets.astype(BF)
        positive = jnp.exp(jnp.sum(unit.astype(F32) * targets, axis=1, keepdims=True) * sharp)
        total, part = score_part(unit, negatives)
        sum_ref[at : at + block, :] = part
        total_ref[at : at + block, :] = total + positive
        positive_ref[at : at + block, :] = jnp.where(has_next, positive, -1.0)


def near_gradient(seq_lengths, seq_owner, near, units, items):
    rows = sum(u.shape[0] for u in units)
    width = near.shape[1]
    shapes = [
        jax.ShapeDtypeStruct((rows, width), F32),
        jax.ShapeDtypeStruct((rows, 1), F32),
        jax.ShapeDtypeStruct((rows, 1), F32),
        jax.ShapeDtypeStruct((rows, width), BF),
    ]
    return run(
        functools.partial(near_kernel, len(units)),
        [seq_lengths, seq_owner, near, *units, *items],
        [smem(), smem()] + [vmem()] * (1 + 2 * len(units)),
        shapes,
        [pltpu.VMEM((rows + 8, width), F32)],
        20,
        "near_gradient",
        (),
        LAYER_COST * rows * width * width // 4,
    )


def far_kernel(count, *refs):
    far_ref, sum_ref, total_ref, positive_ref, target_ref = refs[:5]
    unit_refs = refs[5 : 5 + count]
    out_ref, stage_ref, sem = refs[5 + count :]
    negatives = far_ref[...]
    sharp = 1.0 / SCORE_SHARPNESS
    copies = []
    for ref, low, at, block in row_blocks(unit_refs, FAR_PAGES):
        part_rows = slice(at, at + block)
        total, part = score_part(ref[low : low + block, :], negatives)
        positive = positive_ref[part_rows, :]
        inverse = 1.0 / (total + total_ref[part_rows, :])
        grad = (part + sum_ref[part_rows, :]) * inverse
        targets = target_ref[part_rows, :].astype(F32)
        grad = (grad + (positive * inverse - 1.0) * targets) * sharp
        stage_ref[part_rows, :] = jnp.where(positive >= 0.0, grad, 0.0)
        rows = pl.ds(at, block)
        copies.append(
            pltpu.make_async_copy(stage_ref.at[rows, :], out_ref.at[rows, :], sem.at[len(copies)])
        )
        copies[-1].start()
    for copy in copies:
        copy.wait()


def far_gradient(far, sums, totals, positives, targets, units):
    rows, width = sums.shape
    return pl.pallas_call(
        functools.partial(far_kernel, len(units)),
        out_shape=jax.ShapeDtypeStruct((rows, width), F32),
        in_specs=[vmem()] * (5 + len(units)),
        out_specs=hbm(),
        scratch_shapes=[
            pltpu.VMEM((rows, width), F32),
            pltpu.SemaphoreType.DMA((rows // PAGE,)),
        ],
        compiler_params=params(20),
        name="far_gradient",
    )(far, sums, totals, positives, targets, *units)


def on_device(
    item_table, event_ids, seq_lengths, seq_owner, negative_ids, w_in, w_mid, w_uvqk, w_proj
):
    tables = lax.axis_size("table")
    users = lax.axis_size("user")
    chips = tables // 2
    neg_half = negative_ids.shape[0] // 4
    cores = [(t, t ^ 1) for t in range(tables)]
    table = stay(item_table.T)
    event_ids, negative_ids = stay(event_ids), stay(negative_ids)
    lengths, owners = stay(seq_lengths), stay(seq_owner)
    rows, first = None, 0
    arrived, after, gate = [], [], []
    for c, size in enumerate(CHUNKS):
        outs = gather_rows(
            event_ids, lengths, owners, negative_ids, table, rows, tables, first, size, after
        )
        if rows is None:
            rows = outs[0]
        keep, *gives = outs[1:] if c == 0 else outs
        got = [lax.ppermute(give, "table", cores) for give in gives]
        blocks = list(merge_columns(keep, got, chips, size, neg_half if c == 0 else 0, gate))
        after = blocks[:1]
        for s in range(1, chips):
            moves = [(t, (t // 2 + s) % chips * 2 + t % 2) for t in range(tables)]
            blocks[s] = lax.ppermute(blocks[s], "table", moves)
        gate = blocks[EARLIER]
        arrived.append(blocks)
        first += size
    arrived.append(())

    weights = (w_in, w_mid, w_uvqk, w_proj)
    units, items = [], []
    prior, first = None, 0
    for c, size in enumerate(CHUNKS):
        last = c == len(CHUNKS) - 1
        after = list(arrived[c + 1][:1])
        outs = layer(seq_lengths, seq_owner, arrived[c], weights, prior, first, size, last, after)
        units.append(outs[0])
        items.append(outs[1])
        if not last:
            prior = outs[2]
        if c == 0:
            own = unit_negatives(arrived[0], 2 * neg_half, units)
            parts = [own]
            for s in range(1, users):
                parts.append(lax.ppermute(own, "user", [(u, u ^ s) for u in range(users)]))
        first += size
    near = join(parts, units[1:])
    far = lax.ppermute(near, "table", cores)
    parts = near_gradient(seq_lengths, seq_owner, near, units, items)
    return far_gradient(far, *parts, units)


def solution(mesh):
    return jax.shard_map(
        on_device,
        mesh=mesh,
        in_specs=(
            P(None, "table"),
            P("user"),
            P("user", None),
            P("user", None),
            P("user"),
            P(),
            P(),
            P(),
            P(),
        ),
        out_specs=P(("table", "user"), None),
        check_vma=False,
    )
```
